32 devices in a mesh: dp: 8 (over z, y), mp: 4 (over x, core).
Axes of the slice: x: 2, y: 2, z: 4, core: 2. Of those that a mesh axis runs over, the one named last changes fastest.
Arguments:
- tokens: bfloat16 [4096, 1024], P('dp'), may hold values from -6 to 6
- cotangent: bfloat16 [4096, 1024], P('dp'), may hold values from -6 to 6
- patch_counts: int32 [4], replicated, may hold values from 320 to 512, as said below
- patch_ids: int32 [4, 512], replicated, may hold values from 0 to 2047, as said below
- text_lengths: int32 [4], replicated, may hold values from 128 to 512, as said below
- margin: int32 [4, 512], replicated, may hold values from 0 to 511, as said below
- box_offsets: int32 [4, 512, 2], replicated, may hold values from 0 to 3
- owners: int32 [8], replicated, may hold values from 0 to 7, each once
- attention_weights: float32 [4, 1024, 1024], P(None, 'dp', 'mp'), may hold values from -0.375 to 0.375
- attention_first: float32 [4, 1024, 1024], P(None, 'dp', 'mp'), may hold values from -80 to 80
- attention_second: float32 [4, 1024, 1024], P(None, 'dp', 'mp'), may hold values from 184.32 to 737.28
- hidden_weights: float32 [3, 1024, 2816], P(None, 'dp', 'mp'), may hold values from -0.1875 to 0.1875
- hidden_first: float32 [3, 1024, 2816], P(None, 'dp', 'mp'), may hold values from -128 to 128
- hidden_second: float32 [3, 1024, 2816], P(None, 'dp', 'mp'), may hold values from 512 to 2048
- norm_gains: float32 [2, 1024], P(None, 'dp'), may hold values from 0.5 to 1.5
- gain_first: float32 [2, 1024], P(None, 'dp'), may hold values from -256 to 256
- gain_second: float32 [2, 1024], P(None, 'dp'), may hold values from 2048 to 8192
- bias_tables: float32 [3, 32, 16], P(None, 'dp', 'mp'), may hold values from -3 to 3
- table_first: float32 [3, 32, 16], P(None, 'dp', 'mp'), may hold values from -80 to 80
- table_second: float32 [3, 32, 16], P(None, 'dp', 'mp'), may hold values from 184.32 to 737.28
Outputs:
- layer_output: bfloat16 [4096, 1024], P('dp')
- token_gradient: float32 [4096, 1024], P('dp')
- attention_gradient: float32 [4, 1024, 1024], P(None, 'dp', 'mp')
- attention_moment: float32 [4, 1024, 1024], P(None, 'dp', 'mp')
- attention_square: float32 [4, 1024, 1024], P(None, 'dp', 'mp')
- attention_update: float32 [4, 1024, 1024], P(None, 'dp', 'mp')
- hidden_gradient: float32 [3, 1024, 2816], P(None, 'dp', 'mp')
- hidden_moment: float32 [3, 1024, 2816], P(None, 'dp', 'mp')
- hidden_square: float32 [3, 1024, 2816], P(None, 'dp', 'mp')
- hidden_update: float32 [3, 1024, 2816], P(None, 'dp', 'mp')
- gain_gradient: float32 [2, 1024], P(None, 'dp')
- gain_moment: float32 [2, 1024], P(None, 'dp')
- gain_square: float32 [2, 1024], P(None, 'dp')
- gain_update: float32 [2, 1024], P(None, 'dp')
- table_gradient: float32 [3, 32, 16], P(None, 'dp', 'mp')
- table_moment: float32 [3, 32, 16], P(None, 'dp', 'mp')
- table_square: float32 [3, 32, 16], P(None, 'dp', 'mp')
- table_update: float32 [3, 32, 16], P(None, 'dp', 'mp')
The draws below stay inside these ranges and needn't reach their ends.
Inputs may be any that keep to these rules, and one draw needn't show every extreme that they name: `patch_counts`: one page has 512 visible patches. `patch_ids`: the first patch_counts[p] entries of row p are distinct patch numbers of page p (row by row over a grid 32 patches wide) in rising order; the other entries are 0. `text_lengths`: one page has the full 512 text tokens. margin[p, t] is below patch_counts[p]. `owners`: each dp index appears once.
All inputs are finite; a program needn't handle non-finite values.
Results may differ from the reference program's by a relative error of at most 0.019.
The reference program's roundings to bfloat16 on the way count: a program that leaves them out, or rounds other values in their place, can miss the bound.
Values may be sent and summed in bfloat16 or wider, within the bound.
No kernel may reach another device: no remote copies, remote signals or barrier semaphores. Data moves between devices by JAX's collectives and lax.ppermute only.
A program may use at most 192 MiB of HBM per device.

```python
import math
import jax
import jax.numpy as jnp
from jax import lax

D = 1024
H = 16
HD = 64
FF = 2816
NB = 32
GX = 32
STEP = 5
ROWS = 512
PATCHES = 2048
PAGES = 4
TOKENS = 4096
N_DP = 8


def page_counts(key):
    own_key = jax.random.fold_in(key, 101)
    count_key, chosen_key = jax.random.split(own_key)
    counts = jax.random.randint(count_key, (PAGES,), ROWS * 5 // 8, ROWS + 1)
    chosen = jax.random.randint(chosen_key, (), 0, PAGES)
    return (jnp.where(jnp.arange(PAGES) == chosen, ROWS, counts).astype(jnp.int32), chosen)


def draw_patch_counts(key, part):
    counts, chosen = page_counts(key)
    return counts


def draw_patch_ids(key, part):
    counts, chosen = page_counts(key)
    key = jax.random.fold_in(key, 13)
    page_keys = jax.random.split(key, PAGES)

    def one_page(page_key, count, is_chosen):
        anywhere = jax.random.permutation(page_key, PATCHES)[:ROWS].astype(jnp.int32)
        inner = (jax.random.permutation(page_key, PATCHES - 2)[:ROWS - 2] + 1).astype(jnp.int32)
        forced = jnp.concatenate([jnp.array([0, PATCHES - 1], jnp.int32), inner])
        picked = jnp.where(is_chosen, forced, anywhere)
        slots = jnp.arange(ROWS, dtype=jnp.int32)
        scores = jnp.where(slots < count, picked, PATCHES + slots)
        ordered = jnp.sort(scores)
        return jnp.where(slots < count, ordered, 0).astype(jnp.int32)
    return jax.vmap(one_page)(page_keys, counts, jnp.arange(PAGES) == chosen)


def draw_margin(key, part):
    counts, chosen = page_counts(key)
    key = jax.random.fold_in(key, 17)
    first_key, second_key = jax.random.split(key)
    first = jax.random.randint(first_key, (PAGES, ROWS), 0, ROWS)
    second = jax.random.randint(second_key, (PAGES, ROWS), 0, ROWS)
    lowest = jnp.minimum(first, second)
    slots = lowest * counts[:, None] // ROWS
    text_slot = jnp.arange(ROWS, dtype=jnp.int32)[None, :]
    on_chosen = jnp.arange(PAGES, dtype=jnp.int32)[:, None] == chosen
    slots = jnp.where(on_chosen & (text_slot == ROWS - 1), ROWS - 1, slots)
    slots = jnp.where(on_chosen & (text_slot == 0), 0, slots)
    return slots.astype(jnp.int32)


def draw_text_lengths(key, part):
    key = jax.random.fold_in(key, 7)
    length_key, chosen_key = jax.random.split(key)
    lengths = jax.random.randint(length_key, (PAGES,), ROWS // 4, ROWS + 1)
    chosen = jax.random.randint(chosen_key, (), 0, PAGES)
    return jnp.where(jnp.arange(PAGES) == chosen, ROWS, lengths).astype(jnp.int32)


def with_ends(values, key, low, largest):
    place = [jax.random.randint(jax.random.fold_in(key, axis), (), 0, length) for axis, length in enumerate(values.shape)]
    longest = values.shape.index(max(values.shape))
    neighbour = place[:longest] + [(place[longest] + 1) % values.shape[longest]] + place[longest + 1:]
    return values.at[tuple(place)].set(low).at[tuple(neighbour)].set(largest)


def shard_levels(stream_key, shape, shards, least, high):
    factor_of = 1.0
    for position, shards_of in shards:
        draws = jax.random.uniform(jax.random.fold_in(jax.random.fold_in(stream_key, 6), position), (shards_of,), jnp.float32, least / len(shards), high / len(shards))
        factor_of = factor_of * jnp.repeat(jnp.exp(draws), shape[position] // shards_of).reshape((-1,) + (1,) * (len(shape) - 1 - position))
    return factor_of


def noise(key, dims, width, most, cuts=(), kind=jnp.bfloat16):
    entries = width * jax.random.normal(key, dims, jnp.float32)
    if cuts:
        entries = entries * shard_levels(key, dims, cuts, -0.22, 0.18)
    return jnp.clip(entries, -most, most).astype(kind)


def setup_inputs(seed: int = 0) -> dict:
    streams_of = jax.random.split(jax.random.key(seed), 21)
    tokens = noise(streams_of[0], (TOKENS, D), 1.0, 6.0, ((0, 8),))
    cotangent = noise(streams_of[1], (TOKENS, D), 1.0, 6.0, ((0, 8),))
    patch_counts = draw_patch_counts(jax.random.fold_in(streams_of[20], 71), 0)
    patch_ids = draw_patch_ids(jax.random.fold_in(streams_of[20], 71), 0)
    text_lengths = draw_text_lengths(jax.random.fold_in(streams_of[20], 71), 0)
    margin = draw_margin(jax.random.fold_in(streams_of[20], 71), 0)
    box_offsets = with_ends(jax.random.randint(streams_of[6], (PAGES, ROWS, 2), 0, 4), jax.random.fold_in(streams_of[6], 1), 0, 3).astype(jnp.int32)
    owners = jax.random.permutation(streams_of[7], N_DP).astype(jnp.int32)
    attention_weights = noise(streams_of[8], (4, D, H * HD), (D // 4) ** -0.5, 0.375, ((1, 8), (2, 4)), jnp.float32)
    attention_first = noise(streams_of[9], (4, D, H * HD), (0.3 * (PAGES * ROWS) ** 0.5), 80.0, ((1, 8), (2, 4)), jnp.float32)
    attention_second = jnp.clip(jnp.exp(math.log(737.28) - 1.3862944 * jax.random.uniform(streams_of[10], (4, D, H * HD), jnp.float32) ** shard_levels(streams_of[10], (4, D, H * HD), ((1, 8), (2, 4)), -0.2, 0.2)), 184.32, 737.28)
    hidden_weights = noise(streams_of[11], (3, D, FF), D ** -0.5, 0.1875, ((1, 8), (2, 4)), jnp.float32)
    hidden_first = noise(streams_of[12], (3, D, FF), (0.5 * (PAGES * ROWS) ** 0.5), 128.0, ((1, 8), (2, 4)), jnp.float32)
    hidden_second = jnp.clip(jnp.exp(math.log(2048.0) - 1.3862944 * jax.random.uniform(streams_of[13], (3, D, FF), jnp.float32) ** shard_levels(streams_of[13], (3, D, FF), ((1, 8), (2, 4)), -0.2, 0.2)), 512.0, 2048.0)
    norm_gains = jnp.clip(1.0 + 0.1 * jax.random.normal(streams_of[14], (2, D), jnp.float32), 0.5, 1.5)
    gain_first = noise(streams_of[15], (2, D), ((PAGES * ROWS) ** 0.5), 256.0, ((1, 8),), jnp.float32)
    gain_second = jnp.clip(jnp.exp(math.log(8192.0) - 1.3862944 * jax.random.uniform(streams_of[16], (2, D), jnp.float32) ** shard_levels(streams_of[16], (2, D), ((1, 8),), -0.2, 0.2)), 2048.0, 8192.0)
    bias_tables = noise(streams_of[17], (3, NB, H), 0.5, 3.0, ((1, 8), (2, 4)), jnp.float32)
    table_first = noise(streams_of[18], (3, NB, H), (0.3 * (PAGES * ROWS) ** 0.5), 80.0, ((1, 8), (2, 4)), jnp.float32)
    table_second = jnp.clip(jnp.exp(math.log(737.28) - 1.3862944 * jax.random.uniform(streams_of[19], (3, NB, H), jnp.float32) ** shard_levels(streams_of[19], (3, NB, H), ((1, 8), (2, 4)), -0.2, 0.2)), 184.32, 737.28)
    return {"tokens": tokens, "cotangent": cotangent, "patch_counts": patch_counts, "patch_ids": patch_ids, "text_lengths": text_lengths, "margin": margin, "box_offsets": box_offsets, "owners": owners, "attention_weights": attention_weights, "attention_first": attention_first, "attention_second": attention_second, "hidden_weights": hidden_weights, "hidden_first": hidden_first, "hidden_second": hidden_second, "norm_gains": norm_gains, "gain_first": gain_first, "gain_second": gain_second, "bias_tables": bias_tables, "table_first": table_first, "table_second": table_second}


NORM_EPSILON = 1e-06
SCORE_SCALE = 0.0625
BETA_ONE = 0.5
BETA_TWO = 0.5
ADAM_EPSILON = 1e-08
MATRIX_RATE = 0.03
VECTOR_RATE = 0.2
WEIGHT_DECAY = 0.01

@jax.custom_vjp
def low(v):
    return lax.optimization_barrier(v.astype(jnp.bfloat16)).astype(jnp.float32)

@jax.custom_vjp
def low_back(v):
    return v

def low_keep(v):
    return (low(v), None)

def low_pass(kept, grad):
    return (grad,)

def back_keep(v):
    return (v, None)

def back_low(kept, grad):
    return (low(grad),)
low.defvjp(low_keep, low_pass)
low_back.defvjp(back_keep, back_low)

def by_owner(stacked, order_list):
    blocks = order_list.shape[0]
    full_shape = stacked.shape
    blocked = stacked.reshape((full_shape[0], blocks, full_shape[1] // blocks) + full_shape[2:])
    return jnp.take(blocked, order_list, axis=1).reshape(full_shape)

def rms_norm(values, gain_row):
    inverse = lax.rsqrt(lax.optimization_barrier(jnp.mean(values * values, axis=-1, keepdims=True)) + NORM_EPSILON)
    return values * inverse * gain_row

def page_coords(ids_row, margin_row, offset_rows):
    patch_xy = jnp.stack([4 * (ids_row % GX) + 2, 4 * (ids_row // GX) + 2], axis=1)
    under = jnp.take(ids_row, margin_row, axis=0)
    text_xy = jnp.stack([4 * (under % GX) + offset_rows[:, 0], 4 * (under // GX) + offset_rows[:, 1]], axis=1)
    return jnp.concatenate([patch_xy, text_xy], axis=0).astype(jnp.int32)

def page_buckets(query_pos, key_pos, query_xy, key_xy, row_count):
    middle = NB // 2
    relative = query_pos[:, None] - key_pos[None, :]
    along_seq = jnp.clip(relative * (NB // 4) // row_count + middle, 0, NB - 1)
    delta_x = query_xy[:, None, 0] - key_xy[None, :, 0]
    along_x = jnp.clip(delta_x // 2 + middle, 0, NB - 1)
    delta_y = query_xy[:, None, 1] - key_xy[None, :, 1]
    along_y = jnp.clip(delta_y // 2 + middle, 0, NB - 1)
    return jnp.stack([along_seq, along_x, along_y]).astype(jnp.int32)

def matmul(left, right):
    return jnp.dot(left, right, precision=lax.Precision.HIGHEST)

def gelu_tanh(values):
    return jax.nn.gelu(values, approximate=True)

def page_layer(params, page_data):
    attn_mats, hidden_mats, gain_rows, table_rows = params
    patch, text, patch_count, ids_row, text_length, margin_row, offset_rows = page_data
    positions = jnp.arange(ROWS, dtype=jnp.int32)
    patch_valid = (positions < patch_count).astype(jnp.float32)
    text_valid = (positions < text_length).astype(jnp.float32)
    patch_input = patch_valid[:, None] * patch
    sent_rows = low(patch_input)
    joined_text = text_valid[:, None] * (text + jnp.take(sent_rows, margin_row, axis=0))
    page_rows = jnp.concatenate([patch_input, joined_text], axis=0)
    valid = jnp.concatenate([patch_valid, text_valid])
    attn_in = low(rms_norm(page_rows, gain_rows[0]))

    def project(matrix):
        return low(low_back(matmul(attn_in, matrix))).reshape(2 * ROWS, H, HD)
    queries = project(attn_mats[0])
    keys_all = project(attn_mats[1])
    values_all = project(attn_mats[2])
    raw_scores = low_back(jnp.einsum('ihd,jhd->hij', queries, keys_all, precision=lax.Precision.HIGHEST))
    page_pos = jnp.arange(2 * ROWS, dtype=jnp.int32)
    page_xy = page_coords(ids_row, margin_row, offset_rows)
    buckets = page_buckets(page_pos, page_pos, page_xy, page_xy, ROWS)
    bias_rows = table_rows[0][buckets[0]] + table_rows[1][buckets[1]] + table_rows[2][buckets[2]]
    logits = raw_scores * SCORE_SCALE + jnp.transpose(bias_rows, (2, 0, 1))
    logits = jnp.where(valid[None, None, :] > 0.5, logits, -jnp.inf)
    row_max = lax.optimization_barrier(jnp.max(logits, axis=-1, keepdims=True))
    expon = jnp.exp(logits - row_max)
    attend = expon / lax.optimization_barrier(jnp.sum(expon, axis=-1, keepdims=True))
    mixed_rows = jnp.einsum('hij,jhd->ihd', low(attend), values_all, precision=lax.Precision.HIGHEST)
    mixed_rows = low(low_back(mixed_rows)).reshape(2 * ROWS, H * HD)
    attn_out = low_back(matmul(mixed_rows, attn_mats[3].T))
    after_attn = page_rows + attn_out
    hidden_in = low(rms_norm(after_attn, gain_rows[1]))
    gate_rows = low_back(matmul(hidden_in, hidden_mats[0]))
    up_rows = low_back(matmul(hidden_in, hidden_mats[1]))
    activated = low(low_back(gelu_tanh(gate_rows) * up_rows))
    hidden_out = low_back(matmul(activated, hidden_mats[2].T))
    result = valid[:, None] * (after_attn + hidden_out)
    return (result[:ROWS], result[ROWS:])

def adam_step(weight, moment, square, gradient, step_rate, decay_rate):
    new_moment = BETA_ONE * moment + (1.0 - BETA_ONE) * gradient
    new_square = BETA_TWO * square + (1.0 - BETA_TWO) * gradient * gradient
    moment_hat = new_moment / (1.0 - BETA_ONE ** STEP)
    square_hat = new_square / (1.0 - BETA_TWO ** STEP)
    new_weight = weight - step_rate * (moment_hat / (jnp.sqrt(square_hat) + ADAM_EPSILON) + decay_rate * weight)
    return (new_moment, new_square, new_weight)

def reference(tokens, cotangent, patch_counts, patch_ids, text_lengths, margin, box_offsets, owners, attention_weights, attention_first, attention_second, hidden_weights, hidden_first, hidden_second, norm_gains, gain_first, gain_second, bias_tables, table_first, table_second):
    half_rows = PAGES * ROWS

    def forward_pass(token_rows, attention_master, hidden_master, gain_master, table_master):
        params = (low(by_owner(attention_master, owners)), low(by_owner(hidden_master, owners)), low(by_owner(gain_master, owners)), low(by_owner(table_master, owners)))
        patch_part = token_rows[:half_rows].reshape(PAGES, ROWS, D)
        text_part = token_rows[half_rows:].reshape(PAGES, ROWS, D)

        def one_page(carry, page_data):
            return (carry, page_layer(params, page_data))
        unused, outputs = lax.scan(jax.checkpoint(one_page), jnp.zeros((), jnp.float32), (patch_part, text_part, patch_counts, patch_ids, text_lengths, margin, box_offsets))
        return jnp.concatenate([outputs[0].reshape(half_rows, D), outputs[1].reshape(half_rows, D)], axis=0)
    result, backward = jax.vjp(forward_pass, tokens.astype(jnp.float32), attention_weights, hidden_weights, norm_gains, bias_tables)
    token_gradient, attention_gradient, hidden_gradient, gain_gradient, table_gradient = backward(cotangent.astype(jnp.float32))
    attention_moment, attention_square, attention_update = adam_step(attention_weights, attention_first, attention_second, attention_gradient, MATRIX_RATE, WEIGHT_DECAY)
    hidden_moment, hidden_square, hidden_update = adam_step(hidden_weights, hidden_first, hidden_second, hidden_gradient, MATRIX_RATE, WEIGHT_DECAY)
    gain_moment, gain_square, gain_update = adam_step(norm_gains, gain_first, gain_second, gain_gradient, VECTOR_RATE, 0.0)
    table_moment, table_square, table_update = adam_step(bias_tables, table_first, table_second, table_gradient, VECTOR_RATE, 0.0)
    return (result.astype(jnp.bfloat16), token_gradient, attention_gradient, attention_moment, attention_square, attention_update, hidden_gradient, hidden_moment, hidden_square, hidden_update, gain_gradient, gain_moment, gain_square, gain_update, table_gradient, table_moment, table_square, table_update)
```

```python
import jax
import jax.numpy as jnp
from jax import lax
from jax.experimental import pallas as pl
from jax.experimental.pallas import tpu as pltpu
from jax.sharding import PartitionSpec as P

HD = 64
NB = 32
GX = 32
STEP = 5

NORM_EPSILON = 1e-06
SCORE_SCALE = 0.0625
BETA_ONE = 0.5
BETA_TWO = 0.5
ADAM_EPSILON = 1e-08
MATRIX_RATE = 0.03
VECTOR_RATE = 0.2
WEIGHT_DECAY = 0.01

BF = jnp.bfloat16
F32 = jnp.float32
NX = 128
NY = 256
MASKED = -1e30
HIGH = lax.Precision.HIGHEST


def dot(a, b, precision=None):
    return lax.dot_general(
        a, b, (((1,), (0,)), ((), ())), preferred_element_type=F32, precision=precision
    )


def dot_nt(a, b, precision=None):
    return lax.dot_general(
        a, b, (((1,), (1,)), ((), ())), preferred_element_type=F32, precision=precision
    )


def dot_tn(a, b):
    return lax.dot_general(a, b, (((0,), (0,)), ((), ())), preferred_element_type=F32)


def iota(shape, axis):
    return lax.broadcasted_iota(jnp.int32, shape, axis)


def call(body, ins, outs, scratch=(), flops=0, spaces=None):
    specs = [pl.BlockSpec(memory_space=pltpu.SMEM)]
    for place in range(1, len(ins)):
        space = pltpu.VMEM
        if spaces is not None and place in spaces:
            space = spaces[place]
        specs.append(pl.BlockSpec(memory_space=space))
    moved = sum(x.size * x.dtype.itemsize for x in ins) + sum(
        x.size * x.dtype.itemsize for x in outs
    )
    return pl.pallas_call(
        body,
        in_specs=specs,
        out_specs=[pl.BlockSpec(memory_space=pltpu.VMEM) for _ in outs],
        out_shape=list(outs),
        scratch_shapes=list(scratch),
        compiler_params=pltpu.CompilerParams(vmem_limit_bytes=56 * 1024 * 1024),
        cost_estimate=pl.CostEstimate(flops=flops, bytes_accessed=moved, transcendentals=0),
    )(*ins)


def shape(dims, dtype):
    return jax.ShapeDtypeStruct(tuple(dims), dtype)


def swap(array, axis, mask):
    count = lax.axis_size(axis)
    return lax.ppermute(array, axis, [(i, i ^ mask) for i in range(count)])


def gather_xor(block):
    count = lax.axis_size("dp")
    if count == 8:
        held = {0: block, 1: swap(block, "dp", 1)}
        for k in (2, 4, 6):
            held[k] = swap(block, "dp", k)
        for k in (2, 4, 6):
            held[k + 1] = swap(held[k], "dp", 1)
        return [held[k] for k in range(8)]
    held = [block]
    while len(held) < count:
        held = held + [swap(x, "dp", len(held)) for x in held]
    return held


def scatter_xor(parts):
    count = len(parts)
    if count == 8:
        sums = {}
        for k in (4, 6, 2, 0):
            sums[k] = (parts[k].astype(F32) + swap(parts[k + 1], "dp", 1).astype(F32)).astype(BF)
        total = sums[0].astype(F32)
        for k in (4, 6, 2):
            total = total + swap(sums[k], "dp", k).astype(F32)
        return total
    held = list(parts)
    while len(held) > 1:
        half = len(held) // 2
        came = [swap(x, "dp", half) for x in held[half:]]
        held = [
            (x.astype(F32) + y.astype(F32)).astype(BF if half > 1 else F32)
            for x, y in zip(held[:half], came)
        ]
    return held[0].astype(F32)


def adam_step(weight, moment, square, gradient, step_rate, decay_rate):
    new_moment = BETA_ONE * moment + (1.0 - BETA_ONE) * gradient
    new_square = BETA_TWO * square + (1.0 - BETA_TWO) * gradient * gradient
    moment_hat = new_moment / (1.0 - BETA_ONE**STEP)
    square_hat = new_square / (1.0 - BETA_TWO**STEP)
    new_weight = weight - step_rate * (
        moment_hat / (jnp.sqrt(square_hat) + ADAM_EPSILON) + decay_rate * weight
    )
    return (new_moment, new_square, new_weight)


SIDE, CORE, CHIP, COUNT, LENGTH, FIRST = 0, 1, 2, 3, 4, 5


def take_columns(src, sc, dst_store, blocks, width):
    if width % 128 == 0:
        for k in range(blocks):
            at = pl.multiple_of(sc[FIRST + k] * width, 128)
            dst_store(slice(k * width, (k + 1) * width), src[:, pl.ds(at, width)])
        return
    full = blocks * width
    rows = iota((full, full), 0)
    columns = iota((1, full), 1)
    wanted = jnp.zeros((1, full), jnp.int32)
    for k in range(blocks):
        here = (columns >= k * width) & (columns < (k + 1) * width)
        wanted = jnp.where(here, sc[FIRST + k] * width + columns - k * width, wanted)
    picks = (rows == wanted).astype(BF)
    dst_store(slice(0, full), dot(src[...], picks).astype(BF))


def prep_body(blocks, sc, own, q0, q1, q2, q3, cot, ids, margin, offs,
              x, inv, x_half, x_q, inv_q, gy, marks, raw, rawp):
    rows, width = own.shape[0], own.shape[1] // blocks
    half, quarter = rows // 2, rows // 4
    side, core, chip = sc[SIDE], sc[CORE], sc[CHIP]
    raw[pl.ds(pl.multiple_of(side * rows, rows), rows), :] = own[...]
    for ref, t, u in ((q0, 0, 0), (q1, 0, 1), (q2, 1, 0), (q3, 1, 1)):
        at = (1 - side) * rows + (core ^ t) * half + (chip ^ u) * quarter
        raw[pl.ds(pl.multiple_of(at, quarter), quarter), :] = ref[...]

    def keep(columns, value):
        rawp[:, columns] = value

    take_columns(raw, sc, keep, blocks, width)
    slot = iota((rows, 1), 0)
    patch_ok = (slot < sc[COUNT]).astype(F32)
    text_ok = (slot < sc[LENGTH]).astype(F32)
    patch = rawp[0:rows, :].astype(F32) * patch_ok
    hits = (margin[...] == iota((rows, rows), 1)).astype(BF)
    x[0:rows, :] = patch
    x[rows:, :] = text_ok * (rawp[rows:, :].astype(F32) + dot(hits, patch.astype(BF)))
    for part in range(4):
        at = slice(part * half, (part + 1) * half)
        value = x[at, :]
        inv[at, :] = lax.rsqrt(jnp.mean(value * value, axis=-1, keepdims=True) + NORM_EPSILON)
    start = pl.multiple_of(side * rows + core * half, half)
    x_half[...] = x[pl.ds(start, half), :]
    for s in range(2):
        at = pl.multiple_of((side ^ s) * rows + core * half + chip * quarter, quarter)
        x_q[s] = x[pl.ds(at, quarter), :]
        inv_q[s] = inv[pl.ds(at, quarter), :]

    def keep_low(columns, value):
        rawp[0:rows, columns] = value

    take_columns(cot, sc, keep_low, blocks, width)
    own_limit = jnp.where(side == 1, sc[LENGTH], sc[COUNT])
    for t in range(2):
        at = pl.multiple_of((core ^ t) * half, half)
        ok = (at + iota((half, 1), 0) < own_limit).astype(F32)
        gy[t * half:(t + 1) * half, :] = (rawp[pl.ds(at, half), :].astype(F32) * ok).astype(BF)
    n = ids[...]
    px, py = 4 * (n & (GX - 1)), 4 * (n >> 5)
    lane = iota((rows, 128), 1)
    both = jnp.where(lane == 0, px.astype(F32), jnp.where(lane == 1, py.astype(F32), 0.0))
    under = dot(hits, both.astype(BF))
    off = offs[...]
    cx = under[:, 0:1].astype(jnp.int32) + off[:, 0:1]
    cy = under[:, 1:2].astype(jnp.int32) + off[:, 1:2]
    marks[0:rows, 0:NX] = (iota((rows, NX), 1) == px + 2).astype(BF)
    marks[0:rows, NX:] = (iota((rows, NY), 1) == py + 2).astype(BF)
    marks[rows:, 0:NX] = (iota((rows, NX), 1) == cx).astype(BF)
    marks[rows:, NX:] = (iota((rows, NY), 1) == cy).astype(BF)


def table_places(width, along):
    lane = iota((NB, width), 1)
    ahead = jnp.where(lane < width // 2, lane, lane - width)
    if along:
        bucket = NB // 2 - 1 - (ahead >> 6)
    else:
        bucket = ((0 - ahead) >> 1) + NB // 2
    bucket = jnp.clip(bucket, 0, NB - 1)
    return (iota((NB, width), 0) == bucket).astype(F32)


def attend_body(blocks, sc, *refs):
    x, inv, gains, tables, marks = refs[:5]
    parts = refs[5:5 + blocks]
    (a, q, k, v, w, o, kept, sent, w3, wo, keys, bias, scores, feats) = refs[5 + blocks:]
    rows2 = x.shape[0]
    rows = rows2 // 2
    half = rows // 2
    width = x.shape[1] // blocks
    cols = wo.shape[1]
    heads = cols // HD
    side, core = sc[SIDE], sc[CORE]
    for b in range(blocks):
        at = slice(b * width, (b + 1) * width)
        for n in range(3):
            w3[at, n * cols:(n + 1) * cols] = parts[b][n * width:(n + 1) * width, :]
        wo[at, :] = parts[b][3 * width:4 * width, :]
    g1 = gains[0:1, :]
    for part in range(4):
        at = slice(part * half, (part + 1) * half)
        a[at, :] = (x[at, :] * inv[at, :] * g1).astype(BF)
        kv = dot(a[at, :], w3[:, cols:]).astype(BF)
        k[at, :] = kv[:, :cols]
        v[at, :] = kv[:, cols:]
    starts = []
    for t in range(2):
        start = pl.multiple_of(side * rows + (core ^ t) * half, half)
        starts.append(start)
        q[t * half:(t + 1) * half, :] = dot(a[pl.ds(start, half), :], w3[:, :cols]).astype(BF)
    base0 = dot(tables[0:heads, :], table_places(2 * rows2, True), HIGH)
    base1 = dot(tables[heads:2 * heads, :], table_places(2 * NX, False), HIGH)
    base2 = dot(tables[2 * heads:3 * heads, :], table_places(2 * NY, False), HIGH)
    key = iota((1, rows2), 1)
    limit = jnp.where(key < rows, sc[COUNT], rows + sc[LENGTH])
    mask = jnp.where(key < limit, 0.0, MASKED)
    band = rows // (NB // 4)
    keys[:, 128:] = marks[...]
    low_lanes = iota((1, 128), 1) < HD
    triangle = iota((band, rows2), 0) >= (iota((band, rows2), 1) & (band - 1))
    for h in range(heads):
        pair = slice((h // 2) * 128, (h // 2) * 128 + 128)
        mine = low_lanes if h % 2 == 0 else ~low_lanes
        if h % 2 == 0:
            keys[:, 0:128] = k[:, pair]
        for r in range(2 * rows2 // rows * 4 + 1):
            shifted = pltpu.roll(base0[h:h + 1, :], r * band, 1) if r else base0[h:h + 1, :]
            bias[r:r + 1, :] = shifted[:, :rows2] + mask
        t1 = pltpu.roll(
            jnp.broadcast_to(base1[h:h + 1, :], (NX, 2 * NX)), 0, 1, stride=1, stride_axis=0
        )[:, :NX].astype(BF)
        t2 = pltpu.roll(
            jnp.broadcast_to(base2[h:h + 1, :], (NY, 2 * NY)), 0, 1, stride=1, stride_axis=0
        )[:, :NY].astype(BF)
        for t in range(2):
            at = slice(t * half, (t + 1) * half)
            mq = marks[pl.ds(starts[t], half), :]
            feats[:, 0:128] = jnp.where(mine, q[at, pair].astype(F32) * SCORE_SCALE, 0.0).astype(BF)
            feats[:, 128:128 + NX] = dot(mq[:, :NX], t1).astype(BF)
            feats[:, 128 + NX:] = dot(mq[:, NX:], t2).astype(BF)
            scores[...] = dot_nt(feats[...], keys[...])
            first = (side * rows + (core ^ t) * half) // band
            for sb in range(half // band):
                z = scores[sb * band:(sb + 1) * band, :]
                z = z + jnp.where(
                    triangle, bias[pl.ds(first + sb + 1, 1), :], bias[pl.ds(first + sb, 1), :]
                )
                e = jnp.exp(z - jnp.max(z, axis=-1, keepdims=True))
                e = e * (1.0 / jnp.sum(e, axis=-1, keepdims=True))
                w[h, t * half + sb * band:t * half + (sb + 1) * band, :] = e.astype(BF)
            mixed = dot(w[h, at, :], v[:, pair])
            if h % 2 == 0:
                o[at, pair] = mixed.astype(BF)
            else:
                o[at, pair] = jnp.where(mine, mixed.astype(BF), o[at, pair])
    kept[...] = dot_nt(o[0:half, :], wo[...]).astype(BF)
    sent[...] = dot_nt(o[half:, :], wo[...]).astype(BF)


def enter_body(sc, x_half, s_own, s_far, gains, h1, inv2, c):
    value = x_half[...] + (s_own[...].astype(F32) + s_far[...].astype(F32))
    h1[...] = value
    inverse = lax.rsqrt(jnp.mean(value * value, axis=-1, keepdims=True) + NORM_EPSILON)
    inv2[...] = inverse
    c[...] = (value * inverse * gains[1:2, :]).astype(BF)


GELU_A = 0.7978845608028654
GELU_B = 0.044715


def feed_body(blocks, sc, c_own, c_far, gy, hid, f, dgate, dup, kept, sent, wg, wu, wd, sems):
    half = c_own.shape[0]
    width = c_own.shape[1] // blocks
    copies = []
    for b in range(blocks):
        row = sc[FIRST + blocks + b]
        for n, dst in enumerate((wg, wu, wd)):
            copies.append(pltpu.make_async_copy(
                hid.at[row, pl.ds(n * width, width), :],
                dst.at[pl.ds(b * width, width), :],
                sems.at[n, b],
            ))
    for item in copies:
        item.start()
    for item in copies:
        item.wait()
    for t, c_ref, out in ((0, c_own, kept), (1, c_far, sent)):
        at = slice(t * half, (t + 1) * half)
        gate = dot(c_ref[...], wg[...])
        up = dot(c_ref[...], wu[...])
        df = dot(gy[at, :], wd[...]).astype(BF).astype(F32)
        inner = jnp.tanh(GELU_A * (gate + GELU_B * gate * gate * gate))
        gelu = 0.5 * gate * (1.0 + inner)
        slope = 0.5 * (1.0 + inner) + 0.5 * gate * (1.0 - inner * inner) * (
            GELU_A * (1.0 + 3.0 * GELU_B * gate * gate)
        )
        f[at, :] = (gelu * up).astype(BF)
        dgate[at, :] = (df * up * slope).astype(BF)
        dup[at, :] = (df * gelu).astype(BF)
        out[...] = (dot_nt(dgate[at, :], wg[...]) + dot_nt(dup[at, :], wu[...])).astype(BF)


def down_body(blocks, sc, c_own, c_far, gy, hid, f, dgate, dup, kept, sent, grads, c, wd, sems):
    half = c_own.shape[0]
    width = c_own.shape[1] // blocks
    copies = []
    for b in range(blocks):
        row = sc[FIRST + blocks + b]
        copies.append(pltpu.make_async_copy(
            hid.at[row, pl.ds(2 * width, width), :],
            wd.at[pl.ds(b * width, width), :],
            sems.at[b],
        ))
    for item in copies:
        item.start()
    c[0:half, :] = c_own[...]
    c[half:, :] = c_far[...]
    for b in range(blocks):
        row = sc[FIRST + blocks + b]
        at = slice(b * width, (b + 1) * width)
        grads[row, 0:width, :] = dot_tn(c[:, at], dgate[...]).astype(BF)
        grads[row, width:2 * width, :] = dot_tn(c[:, at], dup[...]).astype(BF)
        grads[row, 2 * width:, :] = dot_tn(gy[:, at], f[...]).astype(BF)
    for item in copies:
        item.wait()
    kept[...] = dot_nt(f[0:half, :], wd[...]).astype(BF)
    sent[...] = dot_nt(f[half:, :], wd[...]).astype(BF)


def norm_back(value, inverse, gain, grad):
    weighted = grad * gain
    inner = jnp.mean(weighted * value, axis=-1, keepdims=True)
    return inverse * weighted - value * (inverse * inverse * inverse * inner)


def turn_body(sc, s_own, s_far, h1, inv2, gains, gy, dh1_q, dh1_low, gal, dg2):
    half = h1.shape[0]
    quarter = half // 2
    dc = s_own[...].astype(F32) + s_far[...].astype(F32)
    value, inverse = h1[...], inv2[...]
    dh1 = gy[0:half, :].astype(F32) + norm_back(value, inverse, gains[1:2, :], dc)
    gal[...] = dh1.astype(BF)
    pick = sc[CHIP] == 0
    dh1_q[...] = jnp.where(pick, dh1[:quarter], dh1[quarter:])
    dh1_low[...] = jnp.where(pick, dh1[:quarter], dh1[quarter:]).astype(BF)
    terms = dc * (value * inverse)
    mine = jnp.where(pick, terms[:quarter], terms[quarter:])
    dg2[...] = jnp.sum(mine, axis=0, keepdims=True)


def attend_back_body(sc, gal0, gal1, w3, wo, q, k, v, w, marks, x, inv,
                     dq, dk, dv, keep, send, dg1, m1, m2, low_sums, all_sums,
                     dol, dkt, dvt, keys, dsl, picked):
    half = gal0.shape[0]
    rows = 2 * half
    rows2 = x.shape[0]
    cols = wo.shape[1]
    heads = cols // HD
    side, core, chip = sc[SIDE], sc[CORE], sc[CHIP]
    dol[0:half, :] = dot(gal0[...], wo[...]).astype(BF)
    dol[half:, :] = dot(gal1[...], wo[...]).astype(BF)
    band = rows // (NB // 4)
    keys[:, 128:] = marks[...]
    low_lanes = iota((1, 128), 1) < HD
    triangle = iota((band, rows2), 0) >= (iota((band, rows2), 1) & (band - 1))
    for h in range(heads):
        pair = slice((h // 2) * 128, (h // 2) * 128 + 128)
        mine = low_lanes if h % 2 == 0 else ~low_lanes
        if h % 2 == 0:
            keys[:, 0:128] = k[:, pair]
        for t in range(2):
            at = slice(t * half, (t + 1) * half)
            dol_h = jnp.where(mine, dol[at, pair], jnp.zeros((), BF))
            q_h = jnp.where(mine, q[at, pair], jnp.zeros((), BF))
            dw = dot_nt(dol_h, v[:, pair])
            for sb in range(half // band):
                rs = slice(sb * band, (sb + 1) * band)
                here = w[h, t * half + sb * band:t * half + (sb + 1) * band, :].astype(F32)
                part = here * dw[rs, :]
                ds = part - here * jnp.sum(part, axis=-1, keepdims=True)
                place = t * (half // band) + sb
                all_sums[h, place:place + 1, :] = jnp.sum(ds, axis=0, keepdims=True)
                low_sums[h, place:place + 1, :] = jnp.sum(
                    jnp.where(triangle, ds, 0.0), axis=0, keepdims=True
                )
                dsl[rs, :] = (ds * SCORE_SCALE).astype(BF)
            dvt_part = dot_tn(dol_h, w[h, at, :])
            dkt_part = dot_tn(q_h, dsl[...])
            if h % 2 == 0 and t == 0:
                dvt[...] = dvt_part
                dkt[...] = dkt_part
            else:
                dvt[...] += dvt_part
                dkt[...] += dkt_part
            out = dot(dsl[...], keys[...])
            if h % 2 == 0:
                dq[at, pair] = out[:, 0:128].astype(BF)
            else:
                dq[at, pair] = jnp.where(mine, out[:, 0:128].astype(BF), dq[at, pair])
            picked[at, :] = out[:, 128:]
        if h % 2 == 1:
            dv[:, pair] = dvt[...].T.astype(BF)
            dk[:, pair] = dkt[...].T.astype(BF)
        first = picked[...]
        upper = first.astype(BF)
        lower = (first - upper.astype(F32)).astype(BF)
        total1 = jnp.zeros((NX, NX), F32)
        total2 = jnp.zeros((NY, NY), F32)
        for t in range(2):
            at = slice(t * half, (t + 1) * half)
            mq = marks[pl.ds(pl.multiple_of(side * rows + (core ^ t) * half, half), half), :]
            for value in (upper, lower):
                total1 = total1 + dot_tn(mq[:, :NX], value[at, :NX])
                total2 = total2 + dot_tn(mq[:, NX:], value[at, NX:])
        m1[h] = total1
        m2[h] = total2
    quarter = half // 2
    gain_sum = jnp.zeros((1, x.shape[1]), F32)
    for s in range(2):
        for t in range(2):
            for u in range(2):
                start = (side ^ s) * rows + (core ^ t) * half + (chip ^ u) * quarter
                at = pl.ds(pl.multiple_of(start, quarter), quarter)
                da = dot_nt(dk[at, :], w3[:, cols:2 * cols]) + dot_nt(dv[at, :], w3[:, 2 * cols:])
                if s == 0:
                    mine_q = pl.ds(pl.multiple_of(t * half + (chip ^ u) * quarter, quarter), quarter)
                    da = da + dot_nt(dq[mine_q, :], w3[:, :cols])
                low = da.astype(BF)
                if t == 0:
                    keep[u, s] = low
                else:
                    send[u, s] = low
                gain_sum = gain_sum + jnp.sum(da * (x[at, :] * inv[at, :]), axis=0, keepdims=True)
    dg1[...] = gain_sum


def tables_body(heads, rows2, sc, m1, m2, low_sums, all_sums, out):
    rows = rows2 // 2
    half = rows // 2
    band = rows // (NB // 4)
    side, core = sc[SIDE], sc[CORE]
    scale = 1.0 / SCORE_SCALE
    sums0, sums1, sums2 = [], [], []
    for h in range(heads):
        line = jnp.zeros((1, 2 * rows2), F32)
        blank = jnp.zeros((1, rows2), F32)
        for t in range(2):
            for sb in range(half // band):
                place = t * (half // band) + sb
                row = (side * rows + (core ^ t) * half) // band + sb
                low = low_sums[h, place:place + 1, :]
                high = all_sums[h, place:place + 1, :] - low
                back = 2 * rows2 - row * band
                line = line + pltpu.roll(jnp.concatenate([high, blank], axis=1), back, 1)
                line = line + pltpu.roll(jnp.concatenate([low, blank], axis=1), back - band, 1)
        sums0.append(line)
        sums1.append(diagonals(m1[h], NX) * scale)
        sums2.append(diagonals(m2[h], NY) * scale)
    for n, (sums, places) in enumerate((
        (sums0, table_places(2 * rows2, True)),
        (sums1, table_places(2 * NX, False)),
        (sums2, table_places(2 * NY, False)),
    )):
        out[n * heads:(n + 1) * heads, :] = dot_nt(jnp.concatenate(sums, axis=0), places, HIGH)


def diagonals(square, size):
    mirror = (iota((size, size), 0) + iota((size, size), 1) == size - 1).astype(F32)
    flipped = dot(mirror, square, HIGH)
    wide = jnp.concatenate([flipped, jnp.zeros((size, size), F32)], axis=1)
    turned = pltpu.roll(wide, 0, 1, stride=1, stride_axis=0)
    return pltpu.roll(jnp.sum(turned, axis=0, keepdims=True), size + 1, 1)


def weights_body(blocks, sc, a, q_grad, k_grad, v_grad, gal0, gal1, o, small, *refs):
    outs, (joined, gal, own) = refs[:blocks], refs[blocks:]
    rows2 = a.shape[0]
    rows = rows2 // 2
    half = rows // 2
    width = a.shape[1] // blocks
    cols = o.shape[1]
    joined[:, 0:cols] = k_grad[...]
    joined[:, cols:] = v_grad[...]
    gal[0:half, :] = gal0[...]
    gal[half:, :] = gal1[...]
    for t in range(2):
        start = pl.multiple_of(sc[SIDE] * rows + (sc[CORE] ^ t) * half, half)
        own[t * half:(t + 1) * half, :] = a[pl.ds(start, half), :]
    for b in range(blocks):
        at = slice(b * width, (b + 1) * width)
        kv = dot_tn(a[:, at], joined[...]).astype(BF)
        outs[b][0:width, :] = dot_tn(own[:, at], q_grad[...]).astype(BF)
        outs[b][width:2 * width, :] = kv[:, :cols]
        outs[b][2 * width:3 * width, :] = kv[:, cols:]
        outs[b][3 * width:4 * width, :] = dot_tn(gal[:, at], o[...]).astype(BF)
        outs[b][4 * width:, :] = small[b]


def halves_swapped(ref):
    middle = ref.shape[1] // 2
    return jnp.concatenate([ref[:, middle:], ref[:, :middle]], axis=1).astype(F32)


def leave_body(sc, keep, came, came_x, from_own, from_text, dh1, dh1_text, x_q, inv_q, gains, out):
    quarter = dh1.shape[0]
    side, core, chip = sc[SIDE], sc[CORE], sc[CHIP]
    slot = core * 2 * quarter + chip * quarter + iota((quarter, 1), 0)
    own_limit = jnp.where(side == 1, sc[LENGTH], sc[COUNT])
    g1 = gains[0:1, :]
    own, far = [
        keep[s].astype(F32) + came[s].astype(F32) + came_x[s].astype(F32) for s in range(2)
    ]
    own = own + halves_swapped(from_own)
    dx = dh1[...] + norm_back(x_q[0], inv_q[0], g1, own)
    out[0] = (dx * (slot < own_limit).astype(F32)).astype(BF)
    far = far + halves_swapped(from_text)
    dx = halves_swapped(dh1_text) + norm_back(x_q[1], inv_q[1], g1, far)
    out[1] = (dx * (slot < sc[LENGTH]).astype(F32)).astype(BF)


def put_columns(src, sc, dst, blocks, width):
    if width % 128 == 0:
        for k in range(blocks):
            at = pl.multiple_of(sc[FIRST + k] * width, 128)
            dst[:, pl.ds(at, width)] = src[:, k * width:(k + 1) * width].astype(dst.dtype)
        return
    full = blocks * width
    columns = iota((full, full), 1)
    rows = iota((full, 1), 0)
    wanted = jnp.zeros((full, 1), jnp.int32)
    for k in range(blocks):
        here = (rows >= k * width) & (rows < (k + 1) * width)
        wanted = jnp.where(here, sc[FIRST + k] * width + rows - k * width, wanted)
    picks = (columns == wanted).astype(F32)
    dst[...] = dot(src[...].astype(F32), picks, HIGH).astype(dst.dtype)


def token_body(blocks, sc, p0, p1, p2, p3, margin, out, own, text, total):
    rows = own.shape[0]
    half, quarter = rows // 2, rows // 4
    width = own.shape[1] // blocks
    side, core, chip = sc[SIDE], sc[CORE], sc[CHIP]
    for ref, t, u in ((p0, 0, 0), (p1, 0, 1), (p2, 1, 0), (p3, 1, 1)):
        at = pl.ds(pl.multiple_of((core ^ t) * half + (chip ^ u) * quarter, quarter), quarter)
        own[at, :] = ref[0]
        text[at, :] = ref[1]

    @pl.when(side == 1)
    def _():
        total[...] = own[...].astype(F32)

    @pl.when(side == 0)
    def _():
        hits = (margin[...] == iota((rows, rows), 1)).astype(BF)
        ok = (iota((rows, 1), 0) < sc[COUNT]).astype(F32)
        total[...] = own[...].astype(F32) + ok * dot_tn(hits, text[...])

    put_columns(total, sc, out, blocks, width)


def output_body(blocks, sc, y_own, y_far, out, whole):
    half = y_own.shape[0]
    core = sc[CORE]
    whole[pl.ds(pl.multiple_of(core * half, half), half), :] = y_own[...]
    whole[pl.ds(pl.multiple_of((1 - core) * half, half), half), :] = y_far[...]
    put_columns(whole, sc, out, blocks, y_own.shape[1] // blocks)


def bind(body, *first):
    def bound(*refs):
        return body(*first, *refs)

    return bound


def local(
    tokens,
    cotangent,
    patch_counts,
    patch_ids,
    text_lengths,
    margin,
    box_offsets,
    owners,
    attention_weights,
    attention_first,
    attention_second,
    hidden_weights,
    hidden_first,
    hidden_second,
    norm_gains,
    gain_first,
    gain_second,
    bias_tables,
    table_first,
    table_second,
):
    blocks = lax.axis_size("dp")
    half_way = blocks // 2
    me = lax.axis_index("dp")
    mp = lax.axis_index("mp")
    page = me % half_way
    side = me // half_way
    core, chip = mp % 2, mp // 2
    rows, features = tokens.shape
    half, quarter = rows // 2, rows // 4
    width = features // blocks
    cols = attention_weights.shape[2]
    heads = cols // HD
    hidden = hidden_weights.shape[2]
    share = NB // blocks

    small = jnp.zeros((16, cols), BF)
    small = small.at[0, :2 * width].set(norm_gains.astype(BF).reshape(-1))
    small = small.at[1, :3 * share * heads].set(bias_tables.astype(BF).reshape(-1))
    packed = jnp.concatenate([attention_weights.astype(BF).reshape(4 * width, cols), small], axis=0)
    gathered = gather_xor(packed)
    hid = lax.all_gather(hidden_weights.astype(BF).reshape(3 * width, hidden), "dp", axis=0)

    mine = lax.dynamic_slice_in_dim(tokens, core * half + chip * quarter, quarter, 0)
    q0 = swap(mine, "dp", half_way)
    q1 = swap(q0, "mp", 2)
    q2 = swap(q0, "mp", 1)
    q3 = swap(q1, "mp", 1)

    order = jnp.arange(blocks, dtype=jnp.int32)
    place_of = jnp.sum(
        jnp.where(owners[None, :] == order[:, None], order[None, :], 0), axis=1
    )
    owner_k = me ^ order
    place_k = jnp.sum(
        jnp.where(owner_k[:, None] == order[None, :], place_of[None, :], 0), axis=1
    )
    counts = lax.dynamic_index_in_dim(patch_counts, page, 0, True)
    lengths = lax.dynamic_index_in_dim(text_lengths, page, 0, True)
    scalars = jnp.concatenate([
        jnp.stack([side, core, chip]).astype(jnp.int32), counts, lengths, place_k, owner_k
    ]).astype(jnp.int32)
    ids_column = lax.dynamic_index_in_dim(patch_ids, page, 0, False)[:, None]
    margin_column = lax.dynamic_index_in_dim(margin, page, 0, False)[:, None]
    offsets = lax.dynamic_index_in_dim(box_offsets, page, 0, False)

    x, inv, x_half, x_q, inv_q, gy, marks = call(
        bind(prep_body, blocks),
        [scalars, tokens, q0, q1, q2, q3, cotangent, ids_column, margin_column, offsets],
        [
            shape((2 * rows, features), F32),
            shape((2 * rows, 1), F32),
            shape((half, features), F32),
            shape((2, quarter, features), F32),
            shape((2, quarter, 1), F32),
            shape((rows, features), BF),
            shape((2 * rows, NX + NY), BF),
        ],
        [pltpu.VMEM((2 * rows, features), BF), pltpu.VMEM((2 * rows, features), BF)],
        flops=4 * rows * rows * features,
    )

    rest = jnp.stack([block[4 * width:] for block in gathered])
    gains = rest[:, 0, :2 * width].reshape(blocks, 2, width)
    gains = jnp.transpose(gains, (1, 0, 2)).reshape(2, features).astype(F32)
    table_blocks = rest[:, 1, :3 * share * heads].reshape(blocks, 3, share, heads).astype(F32)
    chosen = place_k[:, None] == order[None, :]
    tables = jnp.sum(
        jnp.where(chosen[:, :, None, None, None], table_blocks[:, None], 0.0), axis=0
    )
    tables = jnp.transpose(tables, (1, 3, 0, 2)).reshape(3 * heads, NB)

    a, q, k, v, w, o, kept, sent, w3, wo = call(
        bind(attend_body, blocks),
        [scalars, x, inv, gains, tables, marks] + gathered,
        [
            shape((2 * rows, features), BF),
            shape((rows, cols), BF),
            shape((2 * rows, cols), BF),
            shape((2 * rows, cols), BF),
            shape((heads, rows, 2 * rows), BF),
            shape((rows, cols), BF),
            shape((half, features), BF),
            shape((half, features), BF),
            shape((features, 3 * cols), BF),
            shape((features, cols), BF),
        ],
        [
            pltpu.VMEM((2 * rows, 128 + NX + NY), BF),
            pltpu.VMEM((24, 2 * rows), F32),
            pltpu.VMEM((half, 2 * rows), F32),
            pltpu.VMEM((half, 128 + NX + NY), BF),
        ],
        flops=8 * rows * rows * cols * 8,
    )

    def mp_sum(kept_rows, sent_rows):
        came = swap(sent_rows, "mp", 1)
        chip_sum = (kept_rows.astype(F32) + came.astype(F32)).astype(BF)
        return chip_sum, swap(chip_sum, "mp", 2)

    s_own, s_far = mp_sum(kept, sent)
    h1, inv2, c_own = call(
        enter_body,
        [scalars, x_half, s_own, s_far, gains],
        [shape((half, features), F32), shape((half, 1), F32), shape((half, features), BF)],
    )
    c_far = swap(c_own, "mp", 1)

    any_space = {4: pl.ANY}
    f, dgate, dup, kept, sent = call(
        bind(feed_body, blocks),
        [scalars, c_own, c_far, gy, hid],
        [shape((rows, hidden), BF)] * 3 + [shape((half, features), BF)] * 2,
        [pltpu.VMEM((features, hidden), BF)] * 3 + [pltpu.SemaphoreType.DMA((3, blocks))],
        flops=10 * rows * features * hidden,
        spaces=any_space,
    )
    s_own, s_far = mp_sum(kept, sent)
    y_kept, y_sent, hidden_grads = call(
        bind(down_body, blocks),
        [scalars, c_own, c_far, gy, hid, f, dgate, dup],
        [shape((half, features), BF)] * 2 + [shape((blocks, 3 * width, hidden), BF)],
        [
            pltpu.VMEM((rows, features), BF),
            pltpu.VMEM((features, hidden), BF),
            pltpu.SemaphoreType.DMA((blocks,)),
        ],
        flops=8 * rows * features * hidden,
        spaces=any_space,
    )
    hidden_sum = lax.psum_scatter(hidden_grads, "dp", scatter_dimension=0, tiled=False)

    dh1_q, dh1_low, gal_own, dg2 = call(
        turn_body,
        [scalars, s_own, s_far, h1, inv2, gains, gy],
        [
            shape((quarter, features), F32),
            shape((quarter, features), BF),
            shape((half, features), BF),
            shape((1, features), F32),
        ],
    )
    gal_far = swap(gal_own, "mp", 1)
    to_patch = [(i, i - half_way) for i in range(half_way, blocks)]
    dh1_text = lax.ppermute(dh1_low, "dp", to_patch)

    dq, dk, dv, keep, send, dg1, m1, m2, low_sums, all_sums = call(
        attend_back_body,
        [scalars, gal_own, gal_far, w3, wo, q, k, v, w, marks, x, inv],
        [
            shape((rows, cols), BF),
            shape((2 * rows, cols), BF),
            shape((2 * rows, cols), BF),
            shape((2, 2, quarter, features), BF),
            shape((2, 2, quarter, features), BF),
            shape((1, features), F32),
            shape((heads, NX, NX), F32),
            shape((heads, NY, NY), F32),
            shape((heads, NB // 4, 2 * rows), F32),
            shape((heads, NB // 4, 2 * rows), F32),
        ],
        [
            pltpu.VMEM((rows, cols), BF),
            pltpu.VMEM((128, 2 * rows), F32),
            pltpu.VMEM((128, 2 * rows), F32),
            pltpu.VMEM((2 * rows, 128 + NX + NY), BF),
            pltpu.VMEM((half, 2 * rows), BF),
            pltpu.VMEM((rows, NX + NY), F32),
        ],
        flops=8 * rows * rows * cols * 10,
    )
    came = swap(send, "mp", 1)
    to_chip = (keep[1].astype(F32) + came[1].astype(F32)).astype(BF)
    came_x = swap(to_chip, "mp", 2)

    y_own, y_far = mp_sum(y_kept, y_sent)
    own_limit = jnp.where(side == 1, lengths, counts)
    slots = core * half + jnp.arange(half, dtype=jnp.int32)
    y_low = (
        (slots < own_limit).astype(F32)[:, None]
        * (h1 + (y_own.astype(F32) + y_far.astype(F32)))
    ).astype(BF)
    y_other = swap(y_low, "mp", 1)
    layer_output = call(
        bind(output_body, blocks),
        [scalars, y_low, y_other],
        [shape((rows, features), BF)],
        [pltpu.VMEM((rows, features), BF)],
    )[0]

    table_part = call(
        bind(tables_body, heads, 2 * rows),
        [scalars, m1, m2, low_sums, all_sums],
        [shape((3 * heads, NB), F32)],
    )[0]
    gain_blocks = jnp.transpose(
        jnp.concatenate([dg1, dg2], axis=0).reshape(2, blocks, width), (1, 0, 2)
    ).reshape(blocks, 1, 2 * width)
    gain_rows = jnp.pad(gain_blocks, ((0, 0), (0, 0), (0, cols - 2 * width)))
    table_flat = table_part.reshape(-1)
    table_height = -(-table_flat.shape[0] // cols)
    table_rows = jnp.pad(table_flat, (0, table_height * cols - table_flat.shape[0]))
    table_rows = jnp.broadcast_to(
        table_rows.reshape(1, table_height, cols), (blocks, table_height, cols)
    )
    small_grads = jnp.concatenate([gain_rows, table_rows], axis=1)
    small_grads = jnp.pad(
        small_grads, ((0, 0), (0, 16 - small_grads.shape[1]), (0, 0))
    ).astype(BF)
    parts = call(
        bind(weights_body, blocks),
        [scalars, a, dq, dk, dv, gal_own, gal_far, o, small_grads],
        [shape((4 * width + 16, cols), BF)] * blocks,
        [
            pltpu.VMEM((2 * rows, 2 * cols), BF),
            pltpu.VMEM((rows, features), BF),
            pltpu.VMEM((rows, features), BF),
        ],
        flops=12 * rows * features * cols,
    )

    far_sum = (keep[0, 1].astype(F32) + came[0, 1].astype(F32) + came_x[1].astype(F32)).astype(BF)
    own_sum = (keep[0, 0].astype(F32) + came[0, 0].astype(F32) + came_x[0].astype(F32)).astype(BF)
    from_own = swap(far_sum, "dp", half_way)
    from_text = lax.ppermute(own_sum, "dp", to_patch)
    pieces = call(
        leave_body,
        [scalars, keep[0], came[0], came_x, from_own, from_text, dh1_q, dh1_text, x_q, inv_q, gains],
        [shape((2, quarter, features), BF)],
    )[0]
    p1 = swap(pieces, "mp", 2)
    p2 = swap(pieces, "mp", 1)
    p3 = swap(p1, "mp", 1)
    token_gradient = call(
        bind(token_body, blocks),
        [scalars, pieces, p1, p2, p3, margin_column],
        [shape((rows, features), F32)],
        [
            pltpu.VMEM((rows, features), BF),
            pltpu.VMEM((rows, features), BF),
            pltpu.VMEM((rows, features), F32),
        ],
        flops=2 * rows * rows * features,
    )[0]

    attention_sum = scatter_xor(list(parts))
    attention_gradient = attention_sum[:4 * width].reshape(4, width, cols)
    small_sum = attention_sum[4 * width:]
    gain_part = small_sum[0:1, :2 * width]
    gain_part = gain_part + swap(gain_part, "mp", 1)
    gain_gradient = (gain_part + swap(gain_part, "mp", 2)).reshape(2, width)
    table_all = small_sum[1:1 + table_height].reshape(-1)[:3 * heads * NB]
    table_all = table_all.reshape(3, heads, blocks, share)
    table_gradient = jnp.transpose(
        lax.dynamic_index_in_dim(table_all, place_k[0], 2, False), (0, 2, 1)
    )
    hidden_gradient = hidden_sum.astype(F32).reshape(3, width, hidden)

    attention_new = adam_step(
        attention_weights, attention_first, attention_second, attention_gradient,
        MATRIX_RATE, WEIGHT_DECAY,
    )
    hidden_new = adam_step(
        hidden_weights, hidden_first, hidden_second, hidden_gradient, MATRIX_RATE, WEIGHT_DECAY
    )
    gain_new = adam_step(norm_gains, gain_first, gain_second, gain_gradient, VECTOR_RATE, 0.0)
    table_new = adam_step(bias_tables, table_first, table_second, table_gradient, VECTOR_RATE, 0.0)
    return (
        (layer_output, token_gradient, attention_gradient)
        + attention_new
        + (hidden_gradient,)
        + hidden_new
        + (gain_gradient,)
        + gain_new
        + (table_gradient,)
        + table_new
    )


def solution(mesh):
    rows = P("dp", None)
    matrix = P(None, "dp", "mp")
    gain = P(None, "dp")
    return jax.shard_map(
        local,
        mesh=mesh,
        in_specs=(rows,) * 2 + (P(),) * 6 + (matrix,) * 6 + (gain,) * 3 + (matrix,) * 3,
        out_specs=(rows,) * 2 + (matrix,) * 8 + (gain,) * 4 + (matrix,) * 4,
        check_vma=False,
    )
```

```python
import jax
import jax.numpy as jnp
from jax import lax
from jax.experimental import pallas as pl
from jax.experimental.pallas import tpu as pltpu
from jax.sharding import PartitionSpec as P

HD = 64
NB = 32
GX = 32
STEP = 5

NORM_EPSILON = 1e-06
SCORE_SCALE = 0.0625
BETA_ONE = 0.5
BETA_TWO = 0.5
ADAM_EPSILON = 1e-08
MATRIX_RATE = 0.03
VECTOR_RATE = 0.2
WEIGHT_DECAY = 0.01

BF = jnp.bfloat16
F32 = jnp.float32
NX = 128
NY = 256
MASKED = -1e30
FLOPS = 1.15e9
HIGH = lax.Precision.HIGHEST


def dot(a, b, precision=None):
    return lax.dot_general(
        a, b, (((1,), (0,)), ((), ())), preferred_element_type=F32, precision=precision
    )


def dot_nt(a, b, precision=None):
    return lax.dot_general(
        a, b, (((1,), (1,)), ((), ())), preferred_element_type=F32, precision=precision
    )


def dot_tn(a, b):
    return lax.dot_general(a, b, (((0,), (0,)), ((), ())), preferred_element_type=F32)


def iota(shape, axis):
    return lax.broadcasted_iota(jnp.int32, shape, axis)


def call(body, ins, outs, scratch=(), spaces=None, behind=(), cost=3.0):
    specs = []
    count = len(ins)
    behind = list(behind)
    inner = body
    if behind:

        def body(*refs):
            inner(*refs[:count], *refs[count + len(behind):])

    for place in range(len(ins)):
        space = pltpu.VMEM if place else pltpu.SMEM
        if spaces is not None and place in spaces:
            space = spaces[place]
        specs.append(pl.BlockSpec(memory_space=space))
    specs += [pl.BlockSpec(memory_space=pl.ANY)] * len(behind)
    return pl.pallas_call(
        body,
        in_specs=specs,
        out_specs=[pl.BlockSpec(memory_space=pltpu.VMEM) for _ in outs],
        out_shape=list(outs),
        scratch_shapes=list(scratch),
        compiler_params=pltpu.CompilerParams(vmem_limit_bytes=56 * 1024 * 1024),
        cost_estimate=pl.CostEstimate(
            flops=int(cost * FLOPS), bytes_accessed=0, transcendentals=0
        ),
    )(*ins, *behind)


def shape(dims, dtype):
    return jax.ShapeDtypeStruct(tuple(dims), dtype)


def swap(array, axis, mask):
    count = lax.axis_size(axis)
    return lax.ppermute(array, axis, [(i, i ^ mask) for i in range(count)])


def after(array, *others):
    return lax.optimization_barrier((array,) + others)[0]


def gather_xor(block):
    held = [block]
    while len(held) < lax.axis_size("dp"):
        held = held + [swap(x, "dp", len(held)) for x in held]
    return held


def entry_place(entry):
    return entry // 8 * 4 + (0, 2, 1, 3)[entry // 2 % 4]


def plus(left, right):
    return (left.astype(F32) + right.astype(F32)).astype(BF)


def scatter_near(even, came):
    if even.shape[0] == 4:
        return plus(even[:2], came[:2]), plus(even[2:], came[2:])
    sums = plus(even, came)
    while sums.shape[0] > 4:
        middle = sums.shape[0] // 2
        sums = plus(sums[:middle], swap(sums[middle:], "dp", 2 * middle))
    return sums[:2], sums[2:]


def adam_step(weight, moment, square, gradient, step_rate, decay_rate):
    new_moment = BETA_ONE * moment + (1.0 - BETA_ONE) * gradient
    new_square = BETA_TWO * square + (1.0 - BETA_TWO) * gradient * gradient
    moment_hat = new_moment / (1.0 - BETA_ONE**STEP)
    square_hat = new_square / (1.0 - BETA_TWO**STEP)
    new_weight = weight - step_rate * (
        moment_hat / (jnp.sqrt(square_hat) + ADAM_EPSILON) + decay_rate * weight
    )
    return (new_moment, new_square, new_weight)


SIDE, CORE, CHIP, COUNT, LENGTH, FIRST = 0, 1, 2, 3, 4, 5


def take_columns(src, sc, dst_store, blocks, width):
    if width % 128 == 0:
        for k in range(blocks):
            at = pl.multiple_of(sc[FIRST + k] * width, 128)
            dst_store(slice(k * width, (k + 1) * width), src[:, pl.ds(at, width)])
        return
    full = blocks * width
    rows = iota((full, full), 0)
    columns = iota((1, full), 1)
    wanted = jnp.zeros((1, full), jnp.int32)
    for k in range(blocks):
        here = (columns >= k * width) & (columns < (k + 1) * width)
        wanted = jnp.where(here, sc[FIRST + k] * width + columns - k * width, wanted)
    picks = (rows == wanted).astype(BF)
    dst_store(slice(0, full), dot(src[...], picks).astype(BF))


def prep_body(blocks, sc, own, q0, q1, q2, q3, cot, ids, margin, offs,
              x, inv, x_half, x_q, inv_q, gy, marks, raw, rawp):
    rows, width = own.shape[0], own.shape[1] // blocks
    half, quarter = rows // 2, rows // 4
    side, core, chip = sc[SIDE], sc[CORE], sc[CHIP]
    raw[pl.ds(pl.multiple_of(side * rows, rows), rows), :] = own[...]
    for ref, t, u in ((q0, 0, 0), (q1, 0, 1), (q2, 1, 0), (q3, 1, 1)):
        at = (1 - side) * rows + (core ^ t) * half + (chip ^ u) * quarter
        raw[pl.ds(pl.multiple_of(at, quarter), quarter), :] = ref[...]

    def keep(columns, value):
        rawp[:, columns] = value

    take_columns(raw, sc, keep, blocks, width)
    slot = iota((rows, 1), 0)
    patch_ok = (slot < sc[COUNT]).astype(F32)
    text_ok = (slot < sc[LENGTH]).astype(F32)
    patch = rawp[0:rows, :].astype(F32) * patch_ok
    hits = (margin[...] == iota((rows, rows), 1)).astype(BF)
    x[0:rows, :] = patch
    x[rows:, :] = text_ok * (rawp[rows:, :].astype(F32) + dot(hits, patch.astype(BF)))
    for part in range(4):
        at = slice(part * half, (part + 1) * half)
        value = x[at, :]
        inv[at, :] = lax.rsqrt(jnp.mean(value * value, axis=-1, keepdims=True) + NORM_EPSILON)
    start = pl.multiple_of(side * rows + core * half, half)
    x_half[...] = x[pl.ds(start, half), :]
    for s in range(2):
        at = pl.multiple_of((side ^ s) * rows + core * half + chip * quarter, quarter)
        x_q[s] = x[pl.ds(at, quarter), :]
        inv_q[s] = inv[pl.ds(at, quarter), :]

    def keep_low(columns, value):
        rawp[0:rows, columns] = value

    take_columns(cot, sc, keep_low, blocks, width)
    own_limit = jnp.where(side == 1, sc[LENGTH], sc[COUNT])
    for t in range(2):
        at = pl.multiple_of((core ^ t) * half, half)
        ok = (at + iota((half, 1), 0) < own_limit).astype(F32)
        gy[t * half:(t + 1) * half, :] = (rawp[pl.ds(at, half), :].astype(F32) * ok).astype(BF)
    n = ids[...]
    px, py = 4 * (n & (GX - 1)), 4 * (n >> 5)
    lane = iota((rows, 128), 1)
    both = jnp.where(lane == 0, px.astype(F32), jnp.where(lane == 1, py.astype(F32), 0.0))
    under = dot(hits, both.astype(BF))
    off = offs[...]
    cx = under[:, 0:1].astype(jnp.int32) + off[:, 0:1]
    cy = under[:, 1:2].astype(jnp.int32) + off[:, 1:2]
    marks[0:rows, 0:NX] = (iota((rows, NX), 1) == px + 2).astype(BF)
    marks[0:rows, NX:] = (iota((rows, NY), 1) == py + 2).astype(BF)
    marks[rows:, 0:NX] = (iota((rows, NX), 1) == cx).astype(BF)
    marks[rows:, NX:] = (iota((rows, NY), 1) == cy).astype(BF)


def table_places(width, along, named=None):
    lane = iota((NB, width), 1)
    ahead = jnp.where(lane < width // 2, lane, lane - width)
    if along:
        bucket = NB // 2 - 1 - (ahead >> 6)
    else:
        bucket = ((0 - ahead) >> 1) + NB // 2
    bucket = jnp.clip(bucket, 0, NB - 1)
    if named is None:
        named = iota((NB, width), 0)
    return (named == bucket).astype(F32)


def pack_body(weights, gains, tables, out):
    width = weights.shape[1]
    share = tables.shape[1]
    for n in range(4):
        out[n * width:(n + 1) * width, :] = weights[n].astype(BF)
    rest = jnp.zeros((out.shape[0] - 4 * width, out.shape[1]), F32)
    row = iota(rest.shape, 0)
    if width % 128 == 0:
        joined = jnp.concatenate([gains[0:1, :], gains[1:2, :]], axis=1)
        if joined.shape[1] < rest.shape[1]:
            blank = jnp.zeros((1, rest.shape[1] - joined.shape[1]), F32)
            joined = jnp.concatenate([joined, blank], axis=1)
        rest = jnp.where(row == 0, joined, rest)
    lane = iota(rest.shape, 1)
    for n in range(3):
        for t in range(share):
            for h in range(tables.shape[2]):
                here = (row == 1 + n * share + t) & (lane == h)
                rest = jnp.where(here, tables[n, t, h], rest)
    out[4 * width:, :] = rest.astype(BF)


def table_lines(blocks, sc, parts, width):
    share = NB // blocks
    found = []
    for n in range(3):
        lines = [
            parts[b][4 * width:, 0:128].astype(F32)[1 + n * share:1 + (n + 1) * share]
            for b in range(blocks)
        ]
        found.append(jnp.concatenate(lines, axis=0))
    row = iota((NB, 1), 0)
    named = jnp.zeros((NB, 1), jnp.int32)
    for b in range(blocks):
        here = (row >= b * share) & (row < (b + 1) * share)
        named = jnp.where(here, sc[FIRST + b] * share + row - b * share, named)
    return found, named


def attend_body(blocks, sc, *refs):
    x, inv, gains_in, marks = refs[:4]
    parts = refs[4:4 + blocks]
    (a, q, k, v, w, o, kept, sent, w3, wo, gains, keys, bias, scores, feats) = refs[4 + blocks:]
    rows2 = x.shape[0]
    rows = rows2 // 2
    half = rows // 2
    width = x.shape[1] // blocks
    cols = wo.shape[1]
    heads = cols // HD
    side, core = sc[SIDE], sc[CORE]
    for b in range(blocks):
        at = slice(b * width, (b + 1) * width)
        for n in range(3):
            w3[at, n * cols:(n + 1) * cols] = parts[b][n * width:(n + 1) * width, :]
        wo[at, :] = parts[b][3 * width:4 * width, :]
    if width % 128 == 0:
        for b in range(blocks):
            line = parts[b][4 * width:, :].astype(F32)
            at = slice(b * width, (b + 1) * width)
            gains[0:1, at] = line[0:1, :width]
            gains[1:2, at] = line[0:1, width:2 * width]
    else:
        gains[...] = gains_in[...]
    g1 = gains[0:1, :]
    for part in range(4):
        at = slice(part * half, (part + 1) * half)
        a[at, :] = (x[at, :] * inv[at, :] * g1).astype(BF)
        kv = dot(a[at, :], w3[:, cols:]).astype(BF)
        k[at, :] = kv[:, :cols]
        v[at, :] = kv[:, cols:]
    starts = []
    for t in range(2):
        start = pl.multiple_of(side * rows + (core ^ t) * half, half)
        starts.append(start)
        q[t * half:(t + 1) * half, :] = dot(a[pl.ds(start, half), :], w3[:, :cols]).astype(BF)
    tables, named = table_lines(blocks, sc, parts, width)
    base0 = dot_tn(tables[0].astype(BF), table_places(2 * rows2, True, named).astype(BF))
    base1 = dot_tn(tables[1].astype(BF), table_places(2 * NX, False, named).astype(BF))
    base2 = dot_tn(tables[2].astype(BF), table_places(2 * NY, False, named).astype(BF))
    key = iota((1, rows2), 1)
    limit = jnp.where(key < rows, sc[COUNT], rows + sc[LENGTH])
    mask = jnp.where(key < limit, 0.0, MASKED)
    band = rows // (NB // 4)
    keys[:, 128:] = marks[...]
    low_lanes = iota((1, 128), 1) < HD
    triangle = iota((band, rows2), 0) >= (iota((band, rows2), 1) & (band - 1))
    for h in range(heads):
        pair = slice((h // 2) * 128, (h // 2) * 128 + 128)
        mine = low_lanes if h % 2 == 0 else ~low_lanes
        if h % 2 == 0:
            keys[:, 0:128] = k[:, pair]
        for r in range(2 * rows2 // rows * 4 + 1):
            shifted = pltpu.roll(base0[h:h + 1, :], r * band, 1) if r else base0[h:h + 1, :]
            bias[r:r + 1, :] = shifted[:, :rows2] + mask
        t1 = pltpu.roll(
            jnp.broadcast_to(base1[h:h + 1, :], (NX, 2 * NX)), 0, 1, stride=1, stride_axis=0
        )[:, :NX].astype(BF)
        t2 = pltpu.roll(
            jnp.broadcast_to(base2[h:h + 1, :], (NY, 2 * NY)), 0, 1, stride=1, stride_axis=0
        )[:, :NY].astype(BF)
        for t in range(2):
            at = slice(t * half, (t + 1) * half)
            mq = marks[pl.ds(starts[t], half), :]
            feats[:, 0:128] = jnp.where(mine, q[at, pair].astype(F32) * SCORE_SCALE, 0.0).astype(BF)
            feats[:, 128:128 + NX] = dot(mq[:, :NX], t1).astype(BF)
            feats[:, 128 + NX:] = dot(mq[:, NX:], t2).astype(BF)
            scores[...] = dot_nt(feats[...], keys[...])
            first = (side * rows + (core ^ t) * half) // band
            for sb in range(half // band):
                z = scores[sb * band:(sb + 1) * band, :]
                z = z + jnp.where(
                    triangle, bias[pl.ds(first + sb + 1, 1), :], bias[pl.ds(first + sb, 1), :]
                )
                e = jnp.exp(z - jnp.max(z, axis=-1, keepdims=True))
                e = e * (1.0 / jnp.sum(e, axis=-1, keepdims=True))
                w[h, t * half + sb * band:t * half + (sb + 1) * band, :] = e.astype(BF)
            mixed = dot(w[h, at, :], v[:, pair])
            if h % 2 == 0:
                o[at, pair] = mixed.astype(BF)
            else:
                o[at, pair] = jnp.where(mine, mixed.astype(BF), o[at, pair])
    kept[...] = dot_nt(o[0:half, :], wo[...]).astype(BF)
    sent[...] = dot_nt(o[half:, :], wo[...]).astype(BF)


def enter_body(sc, x_half, s_own, s_far, gains, h1, inv2, c):
    value = x_half[...] + (s_own[...].astype(F32) + s_far[...].astype(F32))
    h1[...] = value
    inverse = lax.rsqrt(jnp.mean(value * value, axis=-1, keepdims=True) + NORM_EPSILON)
    inv2[...] = inverse
    c[...] = (value * inverse * gains[1:2, :]).astype(BF)


GELU_A = 0.7978845608028654
GELU_B = 0.044715


def hidden_copies(sc, hid, targets, sems):
    blocks, width = hid.shape[0], hid.shape[3]
    copies = []
    for b in range(blocks):
        row = sc[FIRST + blocks + b] if blocks > 1 else 0
        for n, dst in enumerate(targets):
            copies.append(pltpu.make_async_copy(
                hid.at[row, n], dst.at[:, pl.ds(b * width, width)], sems.at[n, b]
            ))
    return copies


def feed_body(sc, c_own, c_far, gy, hid, f, dgate, dup, kept, sent, wd, wg, wu, sems):
    half = c_own.shape[0]
    copies = hidden_copies(sc, hid, (wg, wu, wd), sems)
    for item in copies:
        item.start()
    for item in copies:
        item.wait()
    for t, c_ref, out in ((0, c_own, kept), (1, c_far, sent)):
        at = slice(t * half, (t + 1) * half)
        gate = dot_nt(c_ref[...], wg[...])
        up = dot_nt(c_ref[...], wu[...])
        df = dot_nt(gy[at, :], wd[...]).astype(BF).astype(F32)
        inner = jnp.tanh(GELU_A * (gate + GELU_B * gate * gate * gate))
        gelu = 0.5 * gate * (1.0 + inner)
        slope = 0.5 * (1.0 + inner) + 0.5 * gate * (1.0 - inner * inner) * (
            GELU_A * (1.0 + 3.0 * GELU_B * gate * gate)
        )
        f[at, :] = (gelu * up).astype(BF)
        dgate[at, :] = (df * up * slope).astype(BF)
        dup[at, :] = (df * gelu).astype(BF)
        out[...] = (dot(dgate[at, :], wg[...]) + dot(dup[at, :], wu[...])).astype(BF)


def down_body(blocks, sc, c_own, c_far, gy, wd, f, dgate, dup, kept, sent,
              even0, odd0, even1, odd1, c):
    half = c_own.shape[0]
    features = c_own.shape[1]
    width = features // blocks
    c[0:half, :] = c_own[...]
    c[half:, :] = c_far[...]
    for n, (left, right) in enumerate(((dgate, c), (dup, c), (f, gy))):
        product = dot_tn(left[...], right[...]).astype(BF)
        even, odd, n = (even0, odd0, n) if n < 2 else (even1, odd1, 0)
        if len(odd.shape) == 3:
            even[n] = product
            continue
        for b in range(blocks):
            out = odd if b % 2 else even
            out[entry_place(b), n] = product[:, b * width:(b + 1) * width]
    kept[...] = dot(f[0:half, :], wd[...]).astype(BF)
    sent[...] = dot(f[half:, :], wd[...]).astype(BF)


def norm_back(value, inverse, gain, grad):
    weighted = grad * gain
    inner = jnp.mean(weighted * value, axis=-1, keepdims=True)
    return inverse * weighted - value * (inverse * inverse * inverse * inner)


def turn_body(sc, s_own, s_far, h1, inv2, gains, gy, dh1_q, gal, dg2):
    half = h1.shape[0]
    quarter = half // 2
    dc = s_own[...].astype(F32) + s_far[...].astype(F32)
    value, inverse = h1[...], inv2[...]
    dh1 = gy[0:half, :].astype(F32) + norm_back(value, inverse, gains[1:2, :], dc)
    gal[...] = dh1.astype(BF)
    pick = sc[CHIP] == 0
    dh1_q[...] = jnp.where(pick, dh1[:quarter], dh1[quarter:])
    terms = dc * (value * inverse)
    mine = jnp.where(pick, terms[:quarter], terms[quarter:])
    dg2[...] = jnp.sum(mine, axis=0, keepdims=True)


def attend_back_body(sc, gal0, gal1, w3, wo, q, k, v, w, marks, x, inv,
                     dq, dk, dv, keep, send, dg1, m1, m2, low_sums, all_sums,
                     dol, dkt, dvt, keys, dsl, picked):
    half = gal0.shape[0]
    rows = 2 * half
    rows2 = x.shape[0]
    cols = wo.shape[1]
    heads = cols // HD
    side, core, chip = sc[SIDE], sc[CORE], sc[CHIP]
    dol[0:half, :] = dot(gal0[...], wo[...]).astype(BF)
    dol[half:, :] = dot(gal1[...], wo[...]).astype(BF)
    band = rows // (NB // 4)
    keys[:, 128:] = marks[...]
    low_lanes = iota((1, 128), 1) < HD
    triangle = iota((band, rows2), 0) >= (iota((band, rows2), 1) & (band - 1))
    for h in range(heads):
        pair = slice((h // 2) * 128, (h // 2) * 128 + 128)
        mine = low_lanes if h % 2 == 0 else ~low_lanes
        if h % 2 == 0:
            keys[:, 0:128] = k[:, pair]
        for t in range(2):
            at = slice(t * half, (t + 1) * half)
            dol_h = jnp.where(mine, dol[at, pair], jnp.zeros((), BF))
            q_h = jnp.where(mine, q[at, pair], jnp.zeros((), BF))
            dw = dot_nt(dol_h, v[:, pair])
            for sb in range(half // band):
                rs = slice(sb * band, (sb + 1) * band)
                here = w[h, t * half + sb * band:t * half + (sb + 1) * band, :].astype(F32)
                part = here * dw[rs, :]
                ds = part - here * jnp.sum(part, axis=-1, keepdims=True)
                place = t * (half // band) + sb
                all_sums[h, place:place + 1, :] = jnp.sum(ds, axis=0, keepdims=True)
                low_sums[h, place:place + 1, :] = jnp.sum(
                    jnp.where(triangle, ds, 0.0), axis=0, keepdims=True
                )
                dsl[rs, :] = (ds * SCORE_SCALE).astype(BF)
            dvt_part = dot_tn(dol_h, w[h, at, :])
            dkt_part = dot_tn(q_h, dsl[...])
            if h % 2 == 0 and t == 0:
                dvt[...] = dvt_part
                dkt[...] = dkt_part
            else:
                dvt[...] += dvt_part
                dkt[...] += dkt_part
            out = dot(dsl[...], keys[...])
            if h % 2 == 0:
                dq[at, pair] = out[:, 0:128].astype(BF)
            else:
                dq[at, pair] = jnp.where(mine, out[:, 0:128].astype(BF), dq[at, pair])
            picked[at, :] = out[:, 128:]
        if h % 2 == 1:
            dv[:, pair] = dvt[...].T.astype(BF)
            dk[:, pair] = dkt[...].T.astype(BF)
        first = picked[...]
        upper = first.astype(BF)
        lower = (first - upper.astype(F32)).astype(BF)
        total1 = jnp.zeros((NX, NX), F32)
        total2 = jnp.zeros((NY, NY), F32)
        for t in range(2):
            at = slice(t * half, (t + 1) * half)
            mq = marks[pl.ds(pl.multiple_of(side * rows + (core ^ t) * half, half), half), :]
            for value in (upper, lower):
                total1 = total1 + dot_tn(mq[:, :NX], value[at, :NX])
                total2 = total2 + dot_tn(mq[:, NX:], value[at, NX:])
        m1[h] = total1
        m2[h] = total2
    quarter = half // 2
    gain_sum = jnp.zeros((1, x.shape[1]), F32)
    for s in range(2):
        for t in range(2):
            for u in range(2):
                start = (side ^ s) * rows + (core ^ t) * half + (chip ^ u) * quarter
                at = pl.ds(pl.multiple_of(start, quarter), quarter)
                da = dot_nt(dk[at, :], w3[:, cols:2 * cols]) + dot_nt(dv[at, :], w3[:, 2 * cols:])
                if s == 0:
                    mine_q = pl.ds(pl.multiple_of(t * half + (chip ^ u) * quarter, quarter), quarter)
                    da = da + dot_nt(dq[mine_q, :], w3[:, :cols])
                low = da.astype(BF)
                if t == 0:
                    keep[u, s] = low
                else:
                    send[u, s] = low
                gain_sum = gain_sum + jnp.sum(da * (x[at, :] * inv[at, :]), axis=0, keepdims=True)
    dg1[...] = gain_sum


def tables_body(heads, rows2, sc, m1, m2, low_sums, all_sums, out):
    rows = rows2 // 2
    half = rows // 2
    band = rows // (NB // 4)
    side, core = sc[SIDE], sc[CORE]
    scale = 1.0 / SCORE_SCALE
    sums0, sums1, sums2 = [], [], []
    for h in range(heads):
        line = jnp.zeros((1, 2 * rows2), F32)
        blank = jnp.zeros((1, rows2), F32)
        for t in range(2):
            for sb in range(half // band):
                place = t * (half // band) + sb
                row = (side * rows + (core ^ t) * half) // band + sb
                low = low_sums[h, place:place + 1, :]
                high = all_sums[h, place:place + 1, :] - low
                back = 2 * rows2 - row * band
                line = line + pltpu.roll(jnp.concatenate([high, blank], axis=1), back, 1)
                line = line + pltpu.roll(jnp.concatenate([low, blank], axis=1), back - band, 1)
        sums0.append(line)
        sums1.append(diagonals(m1[h], NX) * scale)
        sums2.append(diagonals(m2[h], NY) * scale)
    for n, (sums, places) in enumerate((
        (sums0, table_places(2 * rows2, True)),
        (sums1, table_places(2 * NX, False)),
        (sums2, table_places(2 * NY, False)),
    )):
        out[n * heads:(n + 1) * heads, :] = dot_nt(jnp.concatenate(sums, axis=0), places, HIGH)


def diagonals(square, size):
    mirror = (iota((size, size), 0) + iota((size, size), 1) == size - 1).astype(F32)
    flipped = dot(mirror, square, HIGH)
    wide = jnp.concatenate([flipped, jnp.zeros((size, size), F32)], axis=1)
    turned = pltpu.roll(wide, 0, 1, stride=1, stride_axis=0)
    return pltpu.roll(jnp.sum(turned, axis=0, keepdims=True), size + 1, 1)


def weights_body(blocks, sc, a, q_grad, k_grad, v_grad, gal0, gal1, o, small, even, odd,
                 joined, gal, own):
    outs = [(odd if b % 2 else even).at[entry_place(b)] for b in range(blocks)]
    rows2 = a.shape[0]
    rows = rows2 // 2
    half = rows // 2
    width = a.shape[1] // blocks
    cols = o.shape[1]
    joined[:, 0:cols] = k_grad[...]
    joined[:, cols:] = v_grad[...]
    gal[0:half, :] = gal0[...]
    gal[half:, :] = gal1[...]
    for t in range(2):
        start = pl.multiple_of(sc[SIDE] * rows + (sc[CORE] ^ t) * half, half)
        own[t * half:(t + 1) * half, :] = a[pl.ds(start, half), :]
    for b in range(blocks):
        at = slice(b * width, (b + 1) * width)
        kv = dot_tn(a[:, at], joined[...]).astype(BF)
        outs[b][0:width, :] = dot_tn(own[:, at], q_grad[...]).astype(BF)
        outs[b][width:2 * width, :] = kv[:, :cols]
        outs[b][2 * width:3 * width, :] = kv[:, cols:]
        outs[b][3 * width:4 * width, :] = dot_tn(gal[:, at], o[...]).astype(BF)
        outs[b][4 * width:, :] = small[b]


def halves_swapped(value):
    middle = value.shape[1] // 2
    return jnp.concatenate([value[:, middle:], value[:, :middle]], axis=1).astype(F32)


def share_body(sc, keep, came, came_x, dh1, x_q, inv_q, gains, own, out):
    g1 = gains[0:1, :]
    for s in range(2):
        da = keep[0, s].astype(F32) + came[0, s].astype(F32) + came_x[s].astype(F32)
        dx = norm_back(x_q[s], inv_q[s], g1, da)
        if s == 0:
            dx = dx + dh1[...]
            own[...] = dx
        out[s] = dx.astype(BF)


def leave_body(sc, own, parts, came, out):
    quarter = own.shape[0]
    side, core, chip = sc[SIDE], sc[CORE], sc[CHIP]
    slot = core * 2 * quarter + chip * quarter + iota((quarter, 1), 0)
    own_limit = jnp.where(side == 1, sc[LENGTH], sc[COUNT])
    dx = own[...] + halves_swapped(came[1])
    out[0] = (dx * (slot < own_limit).astype(F32)).astype(BF)
    dx = parts[1].astype(F32) + halves_swapped(came[0])
    out[1] = (dx * (slot < sc[LENGTH]).astype(F32)).astype(BF)


def put_columns(src, sc, dst, blocks, width):
    if width % 128 == 0:
        for k in range(blocks):
            at = pl.multiple_of(sc[FIRST + k] * width, 128)
            dst[:, pl.ds(at, width)] = src[:, k * width:(k + 1) * width].astype(dst.dtype)
        return
    full = blocks * width
    columns = iota((full, full), 1)
    rows = iota((full, 1), 0)
    wanted = jnp.zeros((full, 1), jnp.int32)
    for k in range(blocks):
        here = (rows >= k * width) & (rows < (k + 1) * width)
        wanted = jnp.where(here, sc[FIRST + k] * width + rows - k * width, wanted)
    picks = (columns == wanted).astype(F32)
    dst[...] = dot(src[...].astype(F32), picks, HIGH).astype(dst.dtype)


def token_body(blocks, sc, p0, p1, p2, p3, margin, out, own, text, total):
    rows = own.shape[0]
    half, quarter = rows // 2, rows // 4
    width = own.shape[1] // blocks
    side, core, chip = sc[SIDE], sc[CORE], sc[CHIP]
    for ref, t, u in ((p0, 0, 0), (p1, 0, 1), (p2, 1, 0), (p3, 1, 1)):
        at = pl.ds(pl.multiple_of((core ^ t) * half + (chip ^ u) * quarter, quarter), quarter)
        own[at, :] = ref[0]
        text[at, :] = ref[1]

    @pl.when(side == 1)
    def _():
        total[...] = own[...].astype(F32)

    @pl.when(side == 0)
    def _():
        hits = (margin[...] == iota((rows, rows), 1)).astype(BF)
        ok = (iota((rows, 1), 0) < sc[COUNT]).astype(F32)
        total[...] = own[...].astype(F32) + ok * dot_tn(hits, text[...])

    put_columns(total, sc, out, blocks, width)


def output_body(blocks, sc, y_own, y_far, out, whole):
    half = y_own.shape[0]
    core = sc[CORE]
    whole[pl.ds(pl.multiple_of(core * half, half), half), :] = y_own[...]
    whole[pl.ds(pl.multiple_of((1 - core) * half, half), half), :] = y_far[...]
    put_columns(whole, sc, out, blocks, y_own.shape[1] // blocks)


def attention_adam_body(sc, kept, came, last, *refs):
    matrices, gains, tables = refs[0:3], refs[3:6], refs[6:9]
    refs = refs[9:]
    matrix_out, gain_out, table_out = refs[0:4], refs[4:8], refs[8:12]
    total = kept[0].astype(F32) + came[0].astype(F32) + last[...].astype(F32)

    def step(ins, outs, at, value, rate, decay):
        outs[0][at] = value
        new = adam_step(ins[0][at], ins[1][at], ins[2][at], value, rate, decay)
        for out, result in zip(outs[1:], new):
            out[at] = result

    number, width = matrices[0].shape[0], matrices[0].shape[1]
    for n in range(number):
        value = total[n * width:(n + 1) * width, :]
        step(matrices, matrix_out, n, value, MATRIX_RATE, WEIGHT_DECAY)
    small = total[number * width:, :]
    for n in range(2):
        at = (slice(n, n + 1), slice(None))
        step(gains, gain_out, at, small[0:1, n * width:(n + 1) * width], VECTOR_RATE, 0.0)
    share, heads = tables[0].shape[1], tables[0].shape[2]
    wanted = (
        iota((share, NB), 1) == sc[FIRST] * share + iota((share, NB), 0)
    ).astype(F32)
    for n in range(3):
        lines = small[1 + n * heads:1 + (n + 1) * heads, :NB]
        step(tables, table_out, n, dot_nt(wanted, lines, HIGH), VECTOR_RATE, 0.0)


def hidden_adam_body(kept0, came0, last0, kept1, came1, last1, *refs):
    matrices, outs = refs[:3], refs[3:]
    group = jnp.where(pl.program_id(0) < 2, 1.0, 0.0)
    value = group * (kept0[0].astype(F32) + came0[0].astype(F32) + last0[...].astype(F32))
    value = value + (1.0 - group) * (
        kept1[0].astype(F32) + came1[0].astype(F32) + last1[...].astype(F32)
    )
    outs[0][...] = value
    new = adam_step(
        matrices[0][...], matrices[1][...], matrices[2][...], value, MATRIX_RATE, WEIGHT_DECAY
    )
    for out, result in zip(outs[1:], new):
        out[...] = result


def hidden_adam(terms, matrices):
    count, hidden, width = matrices[0].shape
    block = pl.BlockSpec((1, hidden, width), lambda n: (n, 0, 0))
    first = pl.BlockSpec((1, hidden, width), lambda n: (jnp.minimum(n, 1), 0, 0))
    second = pl.BlockSpec((1, hidden, width), lambda n: (0, 0, 0))
    first_pair = pl.BlockSpec((1, 1, hidden, width), lambda n: (0, jnp.minimum(n, 1), 0, 0))
    second_pair = pl.BlockSpec((1, 1, hidden, width), lambda n: (0, 0, 0, 0))
    return pl.pallas_call(
        hidden_adam_body,
        grid=(count,),
        in_specs=[first_pair] * 2 + [first] + [second_pair] * 2 + [second] + [block] * 3,
        out_specs=[block] * 4,
        out_shape=[shape(matrices[0].shape, F32)] * 4,
        cost_estimate=pl.CostEstimate(flops=0, bytes_accessed=0, transcendentals=0),
    )(*terms, *matrices)


def bind(body, *first):
    def bound(*refs):
        return body(*first, *refs)

    return bound


def local(
    tokens,
    cotangent,
    patch_counts,
    patch_ids,
    text_lengths,
    margin,
    box_offsets,
    owners,
    attention_weights,
    attention_first,
    attention_second,
    hidden_weights,
    hidden_first,
    hidden_second,
    norm_gains,
    gain_first,
    gain_second,
    bias_tables,
    table_first,
    table_second,
):
    blocks = lax.axis_size("dp")
    half_way = blocks // 2
    me = lax.axis_index("dp")
    mp = lax.axis_index("mp")
    page = me % half_way
    side = me // half_way
    core, chip = mp % 2, mp // 2
    rows, features = tokens.shape
    half, quarter = rows // 2, rows // 4
    width = features // blocks
    cols = attention_weights.shape[2]
    heads = cols // HD
    hidden = hidden_weights.shape[2]
    share = NB // blocks
    wide = width % 128 == 0

    mine = lax.dynamic_slice_in_dim(tokens, core * half + chip * quarter, quarter, 0)
    packed = call(
        pack_body,
        [attention_weights, norm_gains, bias_tables],
        [shape((4 * width + 16, cols), BF)],
        spaces={0: pltpu.VMEM, 2: pltpu.SMEM},
        behind=[mine],
        cost=2.0,
    )[0]
    turned = jnp.transpose(hidden_weights, (0, 2, 1)).astype(BF)
    eight = blocks == 8
    q0 = swap(mine, "dp", half_way)
    q1 = swap(q0, "mp", 2)
    q2 = swap(q0, "mp", 1)
    q3 = swap(q1, "mp", 1)
    if eight:
        near, far, opposite = [lambda v, m=m: swap(v, "dp", m) for m in (1, 2, 4)]
        ga = {0: packed}
        ga[4], ga[2], ga[1] = opposite(packed), far(packed), near(packed)
        ga[3] = near(after(ga[2], ga[1]))
        held = after(ga[4], q0, ga[2])
        ga[6], ga[5] = far(held), near(held)
        ga[7] = near(after(ga[6], ga[3], q2, q3))
        gathered = [ga[k] for k in range(8)]
    else:
        gathered = gather_xor(packed)

    order = jnp.arange(blocks, dtype=jnp.int32)
    place_of = jnp.sum(
        jnp.where(owners[None, :] == order[:, None], order[None, :], 0), axis=1
    )
    owner_k = me ^ order
    place_k = jnp.sum(
        jnp.where(owner_k[:, None] == order[None, :], place_of[None, :], 0), axis=1
    )
    counts = lax.dynamic_index_in_dim(patch_counts, page, 0, True)
    lengths = lax.dynamic_index_in_dim(text_lengths, page, 0, True)
    scalars = jnp.concatenate([
        jnp.stack([side, core, chip]).astype(jnp.int32), counts, lengths, place_k, owner_k
    ]).astype(jnp.int32)
    ids_column = lax.dynamic_index_in_dim(patch_ids, page, 0, False)[:, None]
    margin_column = lax.dynamic_index_in_dim(margin, page, 0, False)[:, None]
    offsets = lax.dynamic_index_in_dim(box_offsets, page, 0, False)

    x, inv, x_half, x_q, inv_q, gy, marks = call(
        bind(prep_body, blocks),
        [scalars, tokens, q0, q1, q2, q3, cotangent, ids_column, margin_column, offsets],
        [
            shape((2 * rows, features), F32),
            shape((2 * rows, 1), F32),
            shape((half, features), F32),
            shape((2, quarter, features), F32),
            shape((2, quarter, 1), F32),
            shape((rows, features), BF),
            shape((2 * rows, NX + NY), BF),
        ],
        [pltpu.VMEM((2 * rows, features), BF), pltpu.VMEM((2 * rows, features), BF)],
        behind=[ga[3], ga[6]] if eight else [],
        cost=8.0,
    )

    if wide:
        gains_in = jnp.zeros((2, features), F32)
    else:
        gains_in = jnp.stack(gather_xor(norm_gains.astype(BF)), axis=1)
        gains_in = gains_in.reshape(2, features).astype(F32)

    hid = lax.all_gather(after(turned, q0), "dp", axis=0)
    if not wide:
        hid = jnp.transpose(jnp.take(hid, owner_k, axis=0), (1, 2, 0, 3))
        hid = hid.reshape(1, 3, hidden, features)

    a, q, k, v, w, o, kept, sent, w3, wo, gains = call(
        bind(attend_body, blocks),
        [scalars, x, inv, gains_in, marks] + gathered,
        [
            shape((2 * rows, features), BF),
            shape((rows, cols), BF),
            shape((2 * rows, cols), BF),
            shape((2 * rows, cols), BF),
            shape((heads, rows, 2 * rows), BF),
            shape((rows, cols), BF),
            shape((half, features), BF),
            shape((half, features), BF),
            shape((features, 3 * cols), BF),
            shape((features, cols), BF),
            shape((2, features), F32),
        ],
        [
            pltpu.VMEM((2 * rows, 128 + NX + NY), BF),
            pltpu.VMEM((24, 2 * rows), F32),
            pltpu.VMEM((half, 2 * rows), F32),
            pltpu.VMEM((half, 128 + NX + NY), BF),
        ],
        cost=16.0,
    )

    def mp_sum(kept_rows, sent_rows):
        came = swap(sent_rows, "mp", 1)
        chip_sum = (kept_rows.astype(F32) + came.astype(F32)).astype(BF)
        return chip_sum, swap(chip_sum, "mp", 2)

    s_own, s_far = mp_sum(kept, sent)
    h1, inv2, c_own = call(
        enter_body,
        [scalars, x_half, s_own, s_far, gains],
        [shape((half, features), F32), shape((half, 1), F32), shape((half, features), BF)],
    )
    c_far = swap(c_own, "mp", 1)

    f, dgate, dup, kept, sent, wd = call(
        feed_body,
        [scalars, c_own, c_far, gy, hid],
        [shape((rows, hidden), BF)] * 3
        + [shape((half, features), BF)] * 2
        + [shape((hidden, features), BF)],
        [pltpu.VMEM((hidden, features), BF)] * 2 + [pltpu.SemaphoreType.DMA((3, hid.shape[0]))],
        spaces={4: pl.ANY},
        cost=10.0,
    )
    s_own, s_far = mp_sum(kept, sent)
    y_kept, y_sent, *hidden_grads = call(
        bind(down_body, blocks),
        [scalars, c_own, c_far, gy, wd, f, dgate, dup],
        [shape((half, features), BF)] * 2
        + [
            shape((blocks // 2, n, hidden, width) if wide else (n, hidden, features), BF)
            for n in (2, 2, 1, 1)
        ],
        [pltpu.VMEM((rows, features), BF)],
        behind=[s_own],
        cost=8.5,
    )
    if not wide:
        places = [[entry_place(b) for b in range(first, blocks, 2)] for first in (0, 1)]
        for group in (0, 2):
            whole = hidden_grads[group]
            whole = whole.reshape(whole.shape[0], hidden, blocks, width)
            whole = jnp.transpose(whole, (2, 0, 1, 3))
            for first in (0, 1):
                hidden_grads[group + first] = jnp.stack([
                    whole[2 * places[first].index(n) + first] for n in range(blocks // 2)
                ])
    hidden_near = [swap(hidden_grads[group], "dp", 1) for group in (1, 3)]

    dh1_q, gal_own, dg2 = call(
        turn_body,
        [scalars, s_own, s_far, h1, inv2, gains, gy],
        [
            shape((quarter, features), F32),
            shape((half, features), BF),
            shape((1, features), F32),
        ],
        behind=[hidden_grads[1]],
        cost=0.0,
    )
    gal_far = swap(gal_own, "mp", 1)
    y_own, y_far = mp_sum(y_kept, y_sent)

    dq, dk, dv, keep, send, dg1, m1, m2, low_sums, all_sums = call(
        attend_back_body,
        [scalars, gal_own, gal_far, w3, wo, q, k, v, w, marks, x, inv],
        [
            shape((rows, cols), BF),
            shape((2 * rows, cols), BF),
            shape((2 * rows, cols), BF),
            shape((2, 2, quarter, features), BF),
            shape((2, 2, quarter, features), BF),
            shape((1, features), F32),
            shape((heads, NX, NX), F32),
            shape((heads, NY, NY), F32),
            shape((heads, NB // 4, 2 * rows), F32),
            shape((heads, NB // 4, 2 * rows), F32),
        ],
        [
            pltpu.VMEM((rows, cols), BF),
            pltpu.VMEM((128, 2 * rows), F32),
            pltpu.VMEM((128, 2 * rows), F32),
            pltpu.VMEM((2 * rows, 128 + NX + NY), BF),
            pltpu.VMEM((half, 2 * rows), BF),
            pltpu.VMEM((rows, NX + NY), F32),
        ],
        behind=[y_own],
        cost=0.0,
    )
    came = swap(after(send, y_far), "mp", 1)
    to_chip = (keep[1].astype(F32) + came[1].astype(F32)).astype(BF)
    came_x = swap(to_chip, "mp", 2)

    own_limit = jnp.where(side == 1, lengths, counts)
    slots = core * half + jnp.arange(half, dtype=jnp.int32)
    y_low = (
        (slots < own_limit).astype(F32)[:, None]
        * (h1 + (y_own.astype(F32) + y_far.astype(F32)))
    ).astype(BF)
    y_other = swap(y_low, "mp", 1)
    layer_output = call(
        bind(output_body, blocks),
        [scalars, y_low, y_other],
        [shape((rows, features), BF)],
        [pltpu.VMEM((rows, features), BF)],
        cost=0.0,
    )[0]

    first_kept, first_sent = scatter_near(hidden_grads[0], hidden_near[0])
    first_came = swap(first_sent, "dp", 2)
    second_kept, second_sent = scatter_near(hidden_grads[2], after(hidden_near[1], came_x))
    second_came = swap(second_sent, "dp", 2)
    first_last = plus(first_kept[1], first_came[1])
    first_end = swap(first_last, "dp", 4)
    second_last = plus(second_kept[1], second_came[1])
    second_end = swap(second_last, "dp", 4)
    table_part = call(
        bind(tables_body, heads, 2 * rows),
        [scalars, m1, m2, low_sums, all_sums],
        [shape((3 * heads, NB), F32)],
        behind=[to_chip, first_sent],
        cost=0.0,
    )[0]
    gain_part = after(jnp.concatenate([dg1, dg2], axis=0), to_chip)
    gain_part = gain_part + swap(gain_part, "mp", 1)
    gain_part = gain_part + swap(gain_part, "mp", 2)
    gain_rows = jnp.transpose(
        gain_part.reshape(2, blocks, width), (1, 0, 2)
    ).reshape(blocks, 1, 2 * width)
    gain_rows = jnp.pad(gain_rows, ((0, 0), (0, 0), (0, cols - 2 * width)))
    table_rows = jnp.broadcast_to(table_part[None], (blocks,) + table_part.shape)
    table_rows = jnp.pad(
        table_rows, ((0, 0), (0, 15 - table_part.shape[0]), (0, cols - table_part.shape[1]))
    )
    small_grads = jnp.concatenate([gain_rows, table_rows], axis=1).astype(BF)
    even, odd = call(
        bind(weights_body, blocks),
        [scalars, a, dq, dk, dv, gal_own, gal_far, o, small_grads],
        [shape((blocks // 2, 4 * width + 16, cols), BF)] * 2,
        [
            pltpu.VMEM((2 * rows, 2 * cols), BF),
            pltpu.VMEM((rows, features), BF),
            pltpu.VMEM((rows, features), BF),
        ],
        behind=[came],
        cost=0.0,
    )

    own_part, dx_parts = call(
        share_body,
        [scalars, keep, came, came_x, dh1_q, x_q, inv_q, gains],
        [shape((quarter, features), F32), shape((2, quarter, features), BF)],
        behind=[odd, second_sent, first_last],
        cost=0.0,
    )
    dx_came = swap(dx_parts, "dp", half_way)
    near_came = swap(after(odd, dx_parts), "dp", 1)
    pair_kept, pair_sent = scatter_near(even, near_came)
    pair_came = swap(pair_sent, "dp", 2)
    last = plus(pair_kept[1], pair_came[1])
    pieces = call(
        leave_body,
        [scalars, own_part, dx_parts, dx_came],
        [shape((2, quarter, features), BF)],
        behind=[layer_output, second_last, first_end],
        cost=0.0,
    )[0]
    last_came = swap(last, "dp", 4)
    p1 = swap(pieces, "mp", 2)
    p2 = swap(pieces, "mp", 1)
    p3 = swap(after(p1, second_end), "mp", 1)
    hidden_new = hidden_adam(
        [first_kept, first_came, first_end, second_kept, second_came, second_end],
        [jnp.transpose(x, (0, 2, 1)) for x in (hidden_weights, hidden_first, hidden_second)],
    )
    token_gradient = call(
        bind(token_body, blocks),
        [scalars, pieces, p1, p2, p3, margin_column],
        [shape((rows, features), F32)],
        [
            pltpu.VMEM((rows, features), BF),
            pltpu.VMEM((rows, features), BF),
            pltpu.VMEM((rows, features), F32),
        ],
        behind=[hidden_new[0]],
        cost=0.0,
    )[0]

    small_new = call(
        attention_adam_body,
        [scalars, pair_kept, pair_came, last_came]
        + [attention_weights, attention_first, attention_second]
        + [norm_gains, gain_first, gain_second]
        + [bias_tables, table_first, table_second],
        [shape(attention_weights.shape, F32)] * 4
        + [shape(norm_gains.shape, F32)] * 4
        + [shape(bias_tables.shape, F32)] * 4,
        behind=[p2, p3],
        cost=0.0,
    )
    return (
        (layer_output, token_gradient)
        + tuple(small_new[:4])
        + tuple(jnp.transpose(x, (0, 2, 1)) for x in hidden_new)
        + tuple(small_new[4:])
    )


def solution(mesh):
    rows = P("dp", None)
    matrix = P(None, "dp", "mp")
    gain = P(None, "dp")
    return jax.shard_map(
        local,
        mesh=mesh,
        in_specs=(rows,) * 2 + (P(),) * 6 + (matrix,) * 6 + (gain,) * 3 + (matrix,) * 3,
        out_specs=(rows,) * 2 + (matrix,) * 8 + (gain,) * 4 + (matrix,) * 4,
        check_vma=False,
    )
```

```python
import jax
import jax.numpy as jnp
from jax import lax
from jax.experimental import pallas as pl
from jax.experimental.pallas import tpu as pltpu
from jax.sharding import PartitionSpec as P

HD = 64
NB = 32
GX = 32
STEP = 5

NORM_EPSILON = 1e-06
SCORE_SCALE = 0.0625
BETA_ONE = 0.5
BETA_TWO = 0.5
ADAM_EPSILON = 1e-08
MATRIX_RATE = 0.03
VECTOR_RATE = 0.2
WEIGHT_DECAY = 0.01

BF = jnp.bfloat16
F32 = jnp.float32
NX = 128
NY = 256
MASKED = -1e30
FLOPS = 1.15e9
HIGH = lax.Precision.HIGHEST


def dot(a, b, precision=None):
    return lax.dot_general(
        a, b, (((1,), (0,)), ((), ())), preferred_element_type=F32, precision=precision
    )


def dot_nt(a, b, precision=None):
    return lax.dot_general(
        a, b, (((1,), (1,)), ((), ())), preferred_element_type=F32, precision=precision
    )


def dot_tn(a, b):
    return lax.dot_general(a, b, (((0,), (0,)), ((), ())), preferred_element_type=F32)


def iota(shape, axis):
    return lax.broadcasted_iota(jnp.int32, shape, axis)


def call(body, ins, outs, scratch=(), spaces=None, behind=(), cost=3.0, load=(), store=(), place=()):
    spaces = dict(spaces or {})
    spaces.update({n: pltpu.HBM for n in load})
    specs = [
        pl.BlockSpec(memory_space=spaces.get(n, pltpu.VMEM if n else pltpu.SMEM))
        for n in range(len(ins))
    ]
    specs += [pl.BlockSpec(memory_space=pl.ANY)] * len(behind)
    out_specs = [
        pl.BlockSpec(memory_space=pltpu.HBM if n in store or n in place else pltpu.VMEM)
        for n in range(len(outs))
    ]
    moved = [ins[n] for n in load] + [outs[n] for n in store]
    staging = [pltpu.VMEM(x.shape, x.dtype) for x in moved]
    if moved:
        staging.append(pltpu.SemaphoreType.DMA((len(moved),)))
    count, own = len(ins), len(scratch)

    def staged(*refs):
        given, refs = list(refs[:count]), refs[count + len(behind):]
        made, refs = list(refs[:len(outs)]), refs[len(outs):]
        used, buffers = refs[:own], refs[own:]
        copies = []
        for n, at in enumerate(load):
            copies.append(pltpu.make_async_copy(given[at], buffers[n], buffers[-1].at[n]))
            given[at] = buffers[n]
        for item in copies:
            item.start()
        for item in copies:
            item.wait()
        copies = []
        for n, at in enumerate(store, len(load)):
            copies.append(pltpu.make_async_copy(buffers[n], made[at], buffers[-1].at[n]))
            made[at] = buffers[n]
        body(*given, *made, *used)
        for item in copies:
            item.start()
        for item in copies:
            item.wait()

    ins = list(ins)
    for n, space in spaces.items():
        if space is pltpu.HBM:
            ins[n] = pltpu.with_memory_space_constraint(ins[n], pltpu.HBM)
    made_at = [
        pltpu.HBM(x.shape, x.dtype) if n in store or n in place else x for n, x in enumerate(outs)
    ]
    return pl.pallas_call(
        staged,
        in_specs=specs,
        out_specs=out_specs,
        out_shape=made_at,
        scratch_shapes=list(scratch) + staging,
        compiler_params=pltpu.CompilerParams(vmem_limit_bytes=24 * 1024 * 1024),
        cost_estimate=pl.CostEstimate(
            flops=int(cost * FLOPS), bytes_accessed=0, transcendentals=0
        ),
    )(*ins, *behind)


def shape(dims, dtype):
    return jax.ShapeDtypeStruct(tuple(dims), dtype)


def swap(array, axis, mask):
    count = lax.axis_size(axis)
    return lax.ppermute(array, axis, [(i, i ^ mask) for i in range(count)])


def after(array, *others):
    return lax.optimization_barrier((array,) + others)[0]


def gather_xor(block):
    held = [block]
    while len(held) < lax.axis_size("dp"):
        held = held + [swap(x, "dp", len(held)) for x in held]
    return held


def entry_place(entry):
    return entry // 8 * 4 + (0, 2, 1, 3)[entry // 2 % 4]


def plus(left, right):
    return (left.astype(F32) + right.astype(F32)).astype(BF)


def scatter_near(even, came):
    if even.shape[0] == 4:
        return plus(even[:2], came[:2]), plus(even[2:], came[2:])
    sums = plus(even, came)
    while sums.shape[0] > 4:
        middle = sums.shape[0] // 2
        sums = plus(sums[:middle], swap(sums[middle:], "dp", 2 * middle))
    return sums[:2], sums[2:]


def adam_step(weight, moment, square, gradient, step_rate, decay_rate):
    new_moment = BETA_ONE * moment + (1.0 - BETA_ONE) * gradient
    new_square = BETA_TWO * square + (1.0 - BETA_TWO) * gradient * gradient
    moment_hat = new_moment / (1.0 - BETA_ONE**STEP)
    square_hat = new_square / (1.0 - BETA_TWO**STEP)
    new_weight = weight - step_rate * (
        moment_hat / (jnp.sqrt(square_hat) + ADAM_EPSILON) + decay_rate * weight
    )
    return (new_moment, new_square, new_weight)


SIDE, CORE, CHIP, COUNT, LENGTH, FIRST = 0, 1, 2, 3, 4, 5


def take_columns(src, sc, dst_store, blocks, width):
    if width % 128 == 0:
        for k in range(blocks):
            at = pl.multiple_of(sc[FIRST + k] * width, 128)
            dst_store(slice(k * width, (k + 1) * width), src[:, pl.ds(at, width)])
        return
    full = blocks * width
    rows = iota((full, full), 0)
    columns = iota((1, full), 1)
    wanted = jnp.zeros((1, full), jnp.int32)
    for k in range(blocks):
        here = (columns >= k * width) & (columns < (k + 1) * width)
        wanted = jnp.where(here, sc[FIRST + k] * width + columns - k * width, wanted)
    picks = (rows == wanted).astype(BF)
    dst_store(slice(0, full), dot(src[...], picks).astype(BF))


def prep_body(blocks, sc, own, q0, q1, q2, q3, cot, ids, margin, offs,
              x, inv, x_half, x_q, inv_q, gy, marks, raw, rawp):
    rows, width = own.shape[0], own.shape[1] // blocks
    half, quarter = rows // 2, rows // 4
    side, core, chip = sc[SIDE], sc[CORE], sc[CHIP]
    raw[pl.ds(pl.multiple_of(side * rows, rows), rows), :] = own[...]
    for ref, t, u in ((q0, 0, 0), (q1, 0, 1), (q2, 1, 0), (q3, 1, 1)):
        at = (1 - side) * rows + (core ^ t) * half + (chip ^ u) * quarter
        raw[pl.ds(pl.multiple_of(at, quarter), quarter), :] = ref[...]

    def keep(columns, value):
        rawp[:, columns] = value

    take_columns(raw, sc, keep, blocks, width)
    slot = iota((rows, 1), 0)
    patch_ok = (slot < sc[COUNT]).astype(F32)
    text_ok = (slot < sc[LENGTH]).astype(F32)
    patch = rawp[0:rows, :].astype(F32) * patch_ok
    hits = (margin[...] == iota((rows, rows), 1)).astype(BF)
    x[0:rows, :] = patch
    x[rows:, :] = text_ok * (rawp[rows:, :].astype(F32) + dot(hits, patch.astype(BF)))
    for part in range(4):
        at = slice(part * half, (part + 1) * half)
        value = x[at, :]
        inv[at, :] = lax.rsqrt(jnp.mean(value * value, axis=-1, keepdims=True) + NORM_EPSILON)
    start = pl.multiple_of(side * rows + core * half, half)
    x_half[...] = x[pl.ds(start, half), :]
    for s in range(2):
        at = pl.multiple_of((side ^ s) * rows + core * half + chip * quarter, quarter)
        x_q[s] = x[pl.ds(at, quarter), :]
        inv_q[s] = inv[pl.ds(at, quarter), :]

    def keep_low(columns, value):
        rawp[0:rows, columns] = value

    take_columns(cot, sc, keep_low, blocks, width)
    own_limit = jnp.where(side == 1, sc[LENGTH], sc[COUNT])
    for t in range(2):
        at = pl.multiple_of((core ^ t) * half, half)
        ok = (at + iota((half, 1), 0) < own_limit).astype(F32)
        gy[t * half:(t + 1) * half, :] = (rawp[pl.ds(at, half), :].astype(F32) * ok).astype(BF)
    n = ids[...]
    px, py = 4 * (n & (GX - 1)), 4 * (n >> 5)
    lane = iota((rows, 128), 1)
    both = jnp.where(lane == 0, px.astype(F32), jnp.where(lane == 1, py.astype(F32), 0.0))
    under = dot(hits, both.astype(BF))
    off = offs[...]
    cx = under[:, 0:1].astype(jnp.int32) + off[:, 0:1]
    cy = under[:, 1:2].astype(jnp.int32) + off[:, 1:2]
    marks[0:rows, 0:NX] = (iota((rows, NX), 1) == px + 2).astype(BF)
    marks[0:rows, NX:] = (iota((rows, NY), 1) == py + 2).astype(BF)
    marks[rows:, 0:NX] = (iota((rows, NX), 1) == cx).astype(BF)
    marks[rows:, NX:] = (iota((rows, NY), 1) == cy).astype(BF)


def table_places(width, along, named=None):
    lane = iota((NB, width), 1)
    ahead = jnp.where(lane < width // 2, lane, lane - width)
    if along:
        bucket = NB // 2 - 1 - (ahead >> 6)
    else:
        bucket = ((0 - ahead) >> 1) + NB // 2
    bucket = jnp.clip(bucket, 0, NB - 1)
    if named is None:
        named = iota((NB, width), 0)
    return (named == bucket).astype(F32)


def pack_body(weights, gains, tables, out):
    width = weights.shape[1]
    share = tables.shape[1]
    for n in range(4):
        out[n * width:(n + 1) * width, :] = weights[n].astype(BF)
    rest = jnp.zeros((out.shape[0] - 4 * width, out.shape[1]), F32)
    row = iota(rest.shape, 0)
    if width % 128 == 0:
        joined = jnp.concatenate([gains[0:1, :], gains[1:2, :]], axis=1)
        if joined.shape[1] < rest.shape[1]:
            blank = jnp.zeros((1, rest.shape[1] - joined.shape[1]), F32)
            joined = jnp.concatenate([joined, blank], axis=1)
        rest = jnp.where(row == 0, joined, rest)
    lane = iota(rest.shape, 1)
    for n in range(3):
        for t in range(share):
            for h in range(tables.shape[2]):
                here = (row == 1 + n * share + t) & (lane == h)
                rest = jnp.where(here, tables[n, t, h], rest)
    out[4 * width:, :] = rest.astype(BF)


def table_lines(blocks, sc, parts, width):
    share = NB // blocks
    found = []
    for n in range(3):
        lines = [
            parts[b][4 * width:, 0:128].astype(F32)[1 + n * share:1 + (n + 1) * share]
            for b in range(blocks)
        ]
        found.append(jnp.concatenate(lines, axis=0))
    row = iota((NB, 1), 0)
    named = jnp.zeros((NB, 1), jnp.int32)
    for b in range(blocks):
        here = (row >= b * share) & (row < (b + 1) * share)
        named = jnp.where(here, sc[FIRST + b] * share + row - b * share, named)
    return found, named


def attend_body(blocks, sc, *refs):
    x, inv, gains_in, marks = refs[:4]
    parts = refs[4:4 + blocks]
    (a, q, k, v, w_out, o, kept, sent, w3, wo, gains) = refs[4 + blocks:15 + blocks]
    (keys, bias, scores, feats, w, w_sems) = refs[15 + blocks:]
    rows2 = x.shape[0]
    rows = rows2 // 2
    half = rows // 2
    width = x.shape[1] // blocks
    cols = wo.shape[1]
    heads = cols // HD
    side, core = sc[SIDE], sc[CORE]
    for b in range(blocks):
        at = slice(b * width, (b + 1) * width)
        for n in range(3):
            w3[at, n * cols:(n + 1) * cols] = parts[b][n * width:(n + 1) * width, :]
        wo[at, :] = parts[b][3 * width:4 * width, :]
    if width % 128 == 0:
        for b in range(blocks):
            line = parts[b][4 * width:, :].astype(F32)
            at = slice(b * width, (b + 1) * width)
            gains[0:1, at] = line[0:1, :width]
            gains[1:2, at] = line[0:1, width:2 * width]
    else:
        gains[...] = gains_in[...]
    g1 = gains[0:1, :]
    for part in range(4):
        at = slice(part * half, (part + 1) * half)
        a[at, :] = (x[at, :] * inv[at, :] * g1).astype(BF)
        kv = dot(a[at, :], w3[:, cols:]).astype(BF)
        k[at, :] = kv[:, :cols]
        v[at, :] = kv[:, cols:]
    starts = []
    for t in range(2):
        start = pl.multiple_of(side * rows + (core ^ t) * half, half)
        starts.append(start)
        q[t * half:(t + 1) * half, :] = dot(a[pl.ds(start, half), :], w3[:, :cols]).astype(BF)
    tables, named = table_lines(blocks, sc, parts, width)
    base0 = dot_tn(tables[0].astype(BF), table_places(2 * rows2, True, named).astype(BF))
    base1 = dot_tn(tables[1].astype(BF), table_places(2 * NX, False, named).astype(BF))
    base2 = dot_tn(tables[2].astype(BF), table_places(2 * NY, False, named).astype(BF))
    key = iota((1, rows2), 1)
    limit = jnp.where(key < rows, sc[COUNT], rows + sc[LENGTH])
    mask = jnp.where(key < limit, 0.0, MASKED)
    band = rows // (NB // 4)
    keys[:, 128:] = marks[...]
    low_lanes = iota((1, 128), 1) < HD
    triangle = iota((band, rows2), 0) >= (iota((band, rows2), 1) & (band - 1))
    for h in range(heads):
        pair = slice((h // 2) * 128, (h // 2) * 128 + 128)
        mine = low_lanes if h % 2 == 0 else ~low_lanes
        if h % 2 == 0:
            keys[:, 0:128] = k[:, pair]
        for r in range(2 * rows2 // rows * 4 + 1):
            shifted = pltpu.roll(base0[h:h + 1, :], r * band, 1) if r else base0[h:h + 1, :]
            bias[r:r + 1, :] = shifted[:, :rows2] + mask
        t1 = pltpu.roll(
            jnp.broadcast_to(base1[h:h + 1, :], (NX, 2 * NX)), 0, 1, stride=1, stride_axis=0
        )[:, :NX].astype(BF)
        t2 = pltpu.roll(
            jnp.broadcast_to(base2[h:h + 1, :], (NY, 2 * NY)), 0, 1, stride=1, stride_axis=0
        )[:, :NY].astype(BF)
        for t in range(2):
            at = slice(t * half, (t + 1) * half)
            mq = marks[pl.ds(starts[t], half), :]
            feats[:, 0:128] = jnp.where(mine, q[at, pair].astype(F32) * SCORE_SCALE, 0.0).astype(BF)
            feats[:, 128:128 + NX] = dot(mq[:, :NX], t1).astype(BF)
            feats[:, 128 + NX:] = dot(mq[:, NX:], t2).astype(BF)
            scores[...] = dot_nt(feats[...], keys[...])
            first = (side * rows + (core ^ t) * half) // band
            for sb in range(half // band):
                z = scores[sb * band:(sb + 1) * band, :]
                z = z + jnp.where(
                    triangle, bias[pl.ds(first + sb + 1, 1), :], bias[pl.ds(first + sb, 1), :]
                )
                e = jnp.exp(z - jnp.max(z, axis=-1, keepdims=True))
                e = e * (1.0 / jnp.sum(e, axis=-1, keepdims=True))
                w[h, t * half + sb * band:t * half + (sb + 1) * band, :] = e.astype(BF)
            mixed = dot(w[h, at, :], v[:, pair])
            if h % 2 == 0:
                o[at, pair] = mixed.astype(BF)
            else:
                o[at, pair] = jnp.where(mine, mixed.astype(BF), o[at, pair])
        pltpu.make_async_copy(w.at[h], w_out.at[h], w_sems.at[h]).start()
    kept[...] = dot_nt(o[0:half, :], wo[...]).astype(BF)
    sent[...] = dot_nt(o[half:, :], wo[...]).astype(BF)
    for h in range(heads):
        pltpu.make_async_copy(w.at[h], w_out.at[h], w_sems.at[h]).wait()


def enter_body(sc, x_half, s_own, s_far, gains, h1, inv2, c):
    value = x_half[...] + (s_own[...].astype(F32) + s_far[...].astype(F32))
    h1[...] = value
    inverse = lax.rsqrt(jnp.mean(value * value, axis=-1, keepdims=True) + NORM_EPSILON)
    inv2[...] = inverse
    c[...] = (value * inverse * gains[1:2, :]).astype(BF)


GELU_A = 0.7978845608028654
GELU_B = 0.044715


def hidden_copies(sc, hid, targets, sems):
    blocks, width = hid.shape[0], hid.shape[3]
    copies = []
    for b in range(blocks):
        row = sc[FIRST + blocks + b] if blocks > 1 else 0
        for n, dst in enumerate(targets):
            copies.append(pltpu.make_async_copy(
                hid.at[row, n], dst.at[:, pl.ds(b * width, width)], sems.at[n, b]
            ))
    return copies


def feed_body(sc, c_own, c_far, gy, hid, f, dgate, dup, kept, sent, wd, wg, wu, sems):
    half = c_own.shape[0]
    copies = hidden_copies(sc, hid, (wg, wu, wd), sems)
    for item in copies:
        item.start()
    for item in copies:
        item.wait()
    for t, c_ref, out in ((0, c_own, kept), (1, c_far, sent)):
        at = slice(t * half, (t + 1) * half)
        gate = dot_nt(c_ref[...], wg[...])
        up = dot_nt(c_ref[...], wu[...])
        df = dot_nt(gy[at, :], wd[...]).astype(BF).astype(F32)
        inner = jnp.tanh(GELU_A * (gate + GELU_B * gate * gate * gate))
        gelu = 0.5 * gate * (1.0 + inner)
        slope = 0.5 * (1.0 + inner) + 0.5 * gate * (1.0 - inner * inner) * (
            GELU_A * (1.0 + 3.0 * GELU_B * gate * gate)
        )
        f[at, :] = (gelu * up).astype(BF)
        dgate[at, :] = (df * up * slope).astype(BF)
        dup[at, :] = (df * gelu).astype(BF)
        out[...] = (dot(dgate[at, :], wg[...]) + dot(dup[at, :], wu[...])).astype(BF)


def down_body(blocks, sc, c_own, c_far, gy, wd, f, dgate, dup, kept, sent, *refs):
    grads, c = refs[:-1], refs[-1]
    half = c_own.shape[0]
    width = c_own.shape[1] // blocks
    c[0:half, :] = c_own[...]
    c[half:, :] = c_far[...]
    for n, (left, right) in enumerate(((dgate, c), (dup, c), (f, gy))):
        product = dot_tn(left[...], right[...]).astype(BF)
        if len(grads) == 3:
            grads[n][...] = product
            continue
        for b in range(blocks):
            bit, place = (b & 1, entry_place(b)) if n else (b >> 1 & 1, (b & 1) + 2 * (b >> 2))
            grads[2 * n + bit][place] = product[:, b * width:(b + 1) * width]
    kept[...] = dot(f[0:half, :], wd[...]).astype(BF)
    sent[...] = dot(f[half:, :], wd[...]).astype(BF)


def norm_back(value, inverse, gain, grad):
    weighted = grad * gain
    inner = jnp.mean(weighted * value, axis=-1, keepdims=True)
    return inverse * weighted - value * (inverse * inverse * inverse * inner)


def turn_body(sc, s_own, s_far, h1, inv2, gains, gy, dh1_q, gal, dg2):
    half = h1.shape[0]
    quarter = half // 2
    dc = s_own[...].astype(F32) + s_far[...].astype(F32)
    value, inverse = h1[...], inv2[...]
    dh1 = gy[0:half, :].astype(F32) + norm_back(value, inverse, gains[1:2, :], dc)
    gal[...] = dh1.astype(BF)
    pick = sc[CHIP] == 0
    dh1_q[...] = jnp.where(pick, dh1[:quarter], dh1[quarter:])
    terms = dc * (value * inverse)
    mine = jnp.where(pick, terms[:quarter], terms[quarter:])
    dg2[...] = jnp.sum(mine, axis=0, keepdims=True)


def attend_back_body(sc, gal0, gal1, w3, wo, q, k, v, w, marks, x, inv,
                     dq, dk, dv, keep, send, dg1, m1, m2, low_sums, all_sums,
                     dol, dkt, dvt, keys, dsl, picked):
    half = gal0.shape[0]
    rows = 2 * half
    rows2 = x.shape[0]
    cols = wo.shape[1]
    heads = cols // HD
    side, core, chip = sc[SIDE], sc[CORE], sc[CHIP]
    dol[0:half, :] = dot(gal0[...], wo[...]).astype(BF)
    dol[half:, :] = dot(gal1[...], wo[...]).astype(BF)
    band = rows // (NB // 4)
    keys[:, 128:] = marks[...]
    low_lanes = iota((1, 128), 1) < HD
    triangle = iota((band, rows2), 0) >= (iota((band, rows2), 1) & (band - 1))
    for h in range(heads):
        pair = slice((h // 2) * 128, (h // 2) * 128 + 128)
        mine = low_lanes if h % 2 == 0 else ~low_lanes
        if h % 2 == 0:
            keys[:, 0:128] = k[:, pair]
        for t in range(2):
            at = slice(t * half, (t + 1) * half)
            dol_h = jnp.where(mine, dol[at, pair], jnp.zeros((), BF))
            q_h = jnp.where(mine, q[at, pair], jnp.zeros((), BF))
            dw = dot_nt(dol_h, v[:, pair])
            for sb in range(half // band):
                rs = slice(sb * band, (sb + 1) * band)
                here = w[h, t * half + sb * band:t * half + (sb + 1) * band, :].astype(F32)
                part = here * dw[rs, :]
                ds = part - here * jnp.sum(part, axis=-1, keepdims=True)
                place = t * (half // band) + sb
                all_sums[h, place:place + 1, :] = jnp.sum(ds, axis=0, keepdims=True)
                low_sums[h, place:place + 1, :] = jnp.sum(
                    jnp.where(triangle, ds, 0.0), axis=0, keepdims=True
                )
                dsl[rs, :] = (ds * SCORE_SCALE).astype(BF)
            dvt_part = dot_tn(dol_h, w[h, at, :])
            dkt_part = dot_tn(q_h, dsl[...])
            if h % 2 == 0 and t == 0:
                dvt[...] = dvt_part
                dkt[...] = dkt_part
            else:
                dvt[...] += dvt_part
                dkt[...] += dkt_part
            out = dot(dsl[...], keys[...])
            if h % 2 == 0:
                dq[at, pair] = out[:, 0:128].astype(BF)
            else:
                dq[at, pair] = jnp.where(mine, out[:, 0:128].astype(BF), dq[at, pair])
            picked[at, :] = out[:, 128:]
        if h % 2 == 1:
            dv[:, pair] = dvt[...].T.astype(BF)
            dk[:, pair] = dkt[...].T.astype(BF)
        first = picked[...]
        upper = first.astype(BF)
        lower = (first - upper.astype(F32)).astype(BF)
        total1 = jnp.zeros((NX, NX), F32)
        total2 = jnp.zeros((NY, NY), F32)
        for t in range(2):
            at = slice(t * half, (t + 1) * half)
            mq = marks[pl.ds(pl.multiple_of(side * rows + (core ^ t) * half, half), half), :]
            for value in (upper, lower):
                total1 = total1 + dot_tn(mq[:, :NX], value[at, :NX])
                total2 = total2 + dot_tn(mq[:, NX:], value[at, NX:])
        m1[h] = total1
        m2[h] = total2
    quarter = half // 2
    gain_sum = jnp.zeros((1, x.shape[1]), F32)
    for s in range(2):
        for t in range(2):
            for u in range(2):
                start = (side ^ s) * rows + (core ^ t) * half + (chip ^ u) * quarter
                at = pl.ds(pl.multiple_of(start, quarter), quarter)
                da = dot_nt(dk[at, :], w3[:, cols:2 * cols]) + dot_nt(dv[at, :], w3[:, 2 * cols:])
                if s == 0:
                    mine_q = pl.ds(pl.multiple_of(t * half + (chip ^ u) * quarter, quarter), quarter)
                    da = da + dot_nt(dq[mine_q, :], w3[:, :cols])
                low = da.astype(BF)
                if t == 0:
                    keep[u, s] = low
                else:
                    send[u, s] = low
                gain_sum = gain_sum + jnp.sum(da * (x[at, :] * inv[at, :]), axis=0, keepdims=True)
    dg1[...] = gain_sum


def tables_body(heads, rows2, sc, m1, m2, low_sums, all_sums, out):
    rows = rows2 // 2
    half = rows // 2
    band = rows // (NB // 4)
    side, core = sc[SIDE], sc[CORE]
    scale = 1.0 / SCORE_SCALE
    line = jnp.zeros((heads, 2 * rows2), F32)
    blank = jnp.zeros((heads, rows2), F32)
    for t in range(2):
        for sb in range(half // band):
            place = t * (half // band) + sb
            row = (side * rows + (core ^ t) * half) // band + sb
            low = low_sums[:, place, :]
            high = all_sums[:, place, :] - low
            back = 2 * rows2 - row * band
            line = line + pltpu.roll(jnp.concatenate([high, blank], axis=1), back, 1)
            line = line + pltpu.roll(jnp.concatenate([low, blank], axis=1), back - band, 1)
    sums0 = [line]
    sums1 = [diagonals(m1[h], NX) * scale for h in range(heads)]
    sums2 = [diagonals(m2[h], NY) * scale for h in range(heads)]
    for n, (sums, places) in enumerate((
        (sums0, table_places(2 * rows2, True)),
        (sums1, table_places(2 * NX, False)),
        (sums2, table_places(2 * NY, False)),
    )):
        out[n * heads:(n + 1) * heads, :] = dot_nt(jnp.concatenate(sums, axis=0), places, HIGH)


def diagonals(square, size):
    mirror = (iota((size, size), 0) + iota((size, size), 1) == size - 1).astype(F32)
    flipped = dot(mirror, square, HIGH)
    wide = jnp.concatenate([flipped, jnp.zeros((size, size), F32)], axis=1)
    turned = pltpu.roll(wide, 0, 1, stride=1, stride_axis=0)
    return pltpu.roll(jnp.sum(turned, axis=0, keepdims=True), size + 1, 1)


def weights_body(blocks, sc, a, q_grad, k_grad, v_grad, gal0, gal1, o, dg1, dg2, tables, even, odd,
                 joined, gal, own):
    outs = [(odd if b % 2 else even).at[entry_place(b)] for b in range(blocks)]
    rows2 = a.shape[0]
    rows = rows2 // 2
    half = rows // 2
    width = a.shape[1] // blocks
    cols = o.shape[1]
    joined[:, 0:cols] = k_grad[...]
    joined[:, cols:] = v_grad[...]
    gal[0:half, :] = gal0[...]
    gal[half:, :] = gal1[...]
    for t in range(2):
        start = pl.multiple_of(sc[SIDE] * rows + (sc[CORE] ^ t) * half, half)
        own[t * half:(t + 1) * half, :] = a[pl.ds(start, half), :]
    count, buckets = tables.shape
    table_rest = jnp.concatenate([
        jnp.zeros((1, cols), F32),
        jnp.concatenate([tables[...], jnp.zeros((count, cols - buckets), F32)], axis=1),
        jnp.zeros((15 - count, cols), F32),
    ], axis=0)
    first_row = iota((16, 1), 0) == 0
    for b in range(blocks):
        at = slice(b * width, (b + 1) * width)
        kv = dot_tn(a[:, at], joined[...]).astype(BF)
        outs[b][0:width, :] = dot_tn(own[:, at], q_grad[...]).astype(BF)
        outs[b][width:2 * width, :] = kv[:, :cols]
        outs[b][2 * width:3 * width, :] = kv[:, cols:]
        outs[b][3 * width:4 * width, :] = dot_tn(gal[:, at], o[...]).astype(BF)
        line = jnp.concatenate([dg1[:, at], dg2[:, at]], axis=1)
        if 2 * width < cols:
            line = jnp.concatenate([line, jnp.zeros((1, cols - 2 * width), F32)], axis=1)
        outs[b][4 * width:, :] = jnp.where(first_row, line, table_rest).astype(BF)


def halves_swapped(value):
    middle = value.shape[1] // 2
    return jnp.concatenate([value[:, middle:], value[:, :middle]], axis=1).astype(F32)


def share_body(sc, keep, came, came_x, dh1, x_q, inv_q, gains, own, out):
    g1 = gains[0:1, :]
    for s in range(2):
        da = keep[0, s].astype(F32) + came[0, s].astype(F32) + came_x[s].astype(F32)
        dx = norm_back(x_q[s], inv_q[s], g1, da)
        if s == 0:
            dx = dx + dh1[...]
            own[...] = dx
        out[s] = dx.astype(BF)


def leave_body(sc, own, parts, came, out):
    quarter = own.shape[0]
    side, core, chip = sc[SIDE], sc[CORE], sc[CHIP]
    slot = core * 2 * quarter + chip * quarter + iota((quarter, 1), 0)
    own_limit = jnp.where(side == 1, sc[LENGTH], sc[COUNT])
    dx = own[...] + halves_swapped(came[1])
    out[0] = (dx * (slot < own_limit).astype(F32)).astype(BF)
    dx = parts[1].astype(F32) + halves_swapped(came[0])
    out[1] = (dx * (slot < sc[LENGTH]).astype(F32)).astype(BF)


def put_columns(src, sc, dst, blocks, width):
    if width % 128 == 0:
        for k in range(blocks):
            at = pl.multiple_of(sc[FIRST + k] * width, 128)
            dst[:, pl.ds(at, width)] = src[:, k * width:(k + 1) * width].astype(dst.dtype)
        return
    full = blocks * width
    columns = iota((full, full), 1)
    rows = iota((full, 1), 0)
    wanted = jnp.zeros((full, 1), jnp.int32)
    for k in range(blocks):
        here = (rows >= k * width) & (rows < (k + 1) * width)
        wanted = jnp.where(here, sc[FIRST + k] * width + rows - k * width, wanted)
    picks = (columns == wanted).astype(F32)
    dst[...] = dot(src[...].astype(F32), picks, HIGH).astype(dst.dtype)


def token_body(blocks, sc, p0, p1, p2, p3, margin, out, own, text, total):
    rows = own.shape[0]
    half, quarter = rows // 2, rows // 4
    width = own.shape[1] // blocks
    side, core, chip = sc[SIDE], sc[CORE], sc[CHIP]
    for ref, t, u in ((p0, 0, 0), (p1, 0, 1), (p2, 1, 0), (p3, 1, 1)):
        at = pl.ds(pl.multiple_of((core ^ t) * half + (chip ^ u) * quarter, quarter), quarter)
        own[at, :] = ref[0]
        text[at, :] = ref[1]

    @pl.when(side == 1)
    def _():
        total[...] = own[...].astype(F32)

    @pl.when(side == 0)
    def _():
        hits = (margin[...] == iota((rows, rows), 1)).astype(BF)
        ok = (iota((rows, 1), 0) < sc[COUNT]).astype(F32)
        total[...] = own[...].astype(F32) + ok * dot_tn(hits, text[...])

    put_columns(total, sc, out, blocks, width)


def output_body(blocks, sc, y_own, y_far, out, whole):
    half = y_own.shape[0]
    core = sc[CORE]
    whole[pl.ds(pl.multiple_of(core * half, half), half), :] = y_own[...]
    whole[pl.ds(pl.multiple_of((1 - core) * half, half), half), :] = y_far[...]
    put_columns(whole, sc, out, blocks, y_own.shape[1] // blocks)


def attention_adam_body(sc, kept, came, last, *refs):
    matrices, tables = refs[0:3], refs[3:6]
    matrix_out, table_out, gain_sum = refs[6:10], refs[10:14], refs[14]
    total = kept[0].astype(F32) + came[0].astype(F32) + last[...].astype(F32)

    def step(ins, outs, at, value, rate, decay):
        outs[0][at] = value
        new = adam_step(ins[0][at], ins[1][at], ins[2][at], value, rate, decay)
        for out, result in zip(outs[1:], new):
            out[at] = result

    number, width = matrices[0].shape[0], matrices[0].shape[1]
    for n in range(number):
        value = total[n * width:(n + 1) * width, :]
        step(matrices, matrix_out, n, value, MATRIX_RATE, WEIGHT_DECAY)
    small = total[number * width:, :]
    for n in range(2):
        gain_sum[n:n + 1, :] = small[0:1, n * width:(n + 1) * width]
    share, heads = tables[0].shape[1], tables[0].shape[2]
    wanted = (
        iota((share, NB), 1) == sc[FIRST] * share + iota((share, NB), 0)
    ).astype(F32)
    for n in range(3):
        lines = small[1 + n * heads:1 + (n + 1) * heads, 0:NB]
        step(tables, table_out, n, dot_nt(wanted, lines, HIGH), VECTOR_RATE, 0.0)


def hidden_adam_body(counts, sc, *refs):
    terms, refs = refs[:sum(counts)], refs[sum(counts):]
    matrices, outs = refs[:3], refs[3:]
    for n, count in enumerate(counts):
        total = jnp.zeros(matrices[0].shape[1:], F32)
        for term in terms[sum(counts[:n]):sum(counts[:n + 1])]:
            total = total + (term[0] if len(term.shape) == 3 else term[...]).astype(F32)
        outs[0][n] = total
        new = adam_step(
            matrices[0][n], matrices[1][n], matrices[2][n], total, MATRIX_RATE, WEIGHT_DECAY
        )
        for out, result in zip(outs[1:], new):
            out[n] = result


def bind(body, *first):
    def bound(*refs):
        return body(*first, *refs)

    return bound


def local(
    tokens,
    cotangent,
    patch_counts,
    patch_ids,
    text_lengths,
    margin,
    box_offsets,
    owners,
    attention_weights,
    attention_first,
    attention_second,
    hidden_weights,
    hidden_first,
    hidden_second,
    norm_gains,
    gain_first,
    gain_second,
    bias_tables,
    table_first,
    table_second,
):
    blocks = lax.axis_size("dp")
    half_way = blocks // 2
    me = lax.axis_index("dp")
    mp = lax.axis_index("mp")
    page = me % half_way
    side = me // half_way
    core, chip = mp % 2, mp // 2
    rows, features = tokens.shape
    half, quarter = rows // 2, rows // 4
    width = features // blocks
    cols = attention_weights.shape[2]
    heads = cols // HD
    hidden = hidden_weights.shape[2]
    share = NB // blocks
    wide = width % 128 == 0

    mine = lax.dynamic_slice_in_dim(tokens, core * half + chip * quarter, quarter, 0)
    packed = call(
        pack_body,
        [attention_weights, norm_gains, bias_tables],
        [shape((4 * width + 16, cols), BF)],
        spaces={0: pltpu.VMEM, 2: pltpu.SMEM},
        behind=[mine],
        cost=2.0,
    )[0]
    turned = jnp.transpose(hidden_weights, (0, 2, 1)).astype(BF)
    eight = blocks == 8
    direct = eight and wide
    q0 = swap(mine, "dp", half_way)
    q1 = swap(q0, "mp", 2)
    q2 = swap(q0, "mp", 1)
    q3 = swap(q1, "mp", 1)
    if eight:
        near, far, opposite = [lambda v, m=m: swap(v, "dp", m) for m in (1, 2, 4)]
        ga = {0: packed}
        ga[4], ga[2], ga[1] = opposite(packed), far(packed), near(packed)
        ga[3] = near(after(ga[2], ga[1]))
        held = after(ga[4], q0, ga[2])
        ga[6], ga[5] = far(held), near(held)
        ga[7] = near(after(ga[6], ga[3], q2, q3))
        gathered = [ga[k] for k in range(8)]
    else:
        gathered = gather_xor(packed)

    order = jnp.arange(blocks, dtype=jnp.int32)
    place_of = jnp.sum(
        jnp.where(owners[None, :] == order[:, None], order[None, :], 0), axis=1
    )
    owner_k = me ^ order
    place_k = jnp.sum(
        jnp.where(owner_k[:, None] == order[None, :], place_of[None, :], 0), axis=1
    )
    counts = lax.dynamic_index_in_dim(patch_counts, page, 0, True)
    lengths = lax.dynamic_index_in_dim(text_lengths, page, 0, True)
    scalars = jnp.concatenate([
        jnp.stack([side, core, chip]).astype(jnp.int32), counts, lengths, place_k, owner_k
    ]).astype(jnp.int32)
    ids_column = lax.dynamic_index_in_dim(patch_ids, page, 0, False)[:, None]
    margin_column = lax.dynamic_index_in_dim(margin, page, 0, False)[:, None]
    offsets = lax.dynamic_index_in_dim(box_offsets, page, 0, False)

    x, inv, x_half, x_q, inv_q, gy, marks = call(
        bind(prep_body, blocks),
        [scalars, tokens, q0, q1, q2, q3, cotangent, ids_column, margin_column, offsets],
        [
            shape((2 * rows, features), F32),
            shape((2 * rows, 1), F32),
            shape((half, features), F32),
            shape((2, quarter, features), F32),
            shape((2, quarter, 1), F32),
            shape((rows, features), BF),
            shape((2 * rows, NX + NY), BF),
        ],
        [pltpu.VMEM((2 * rows, features), BF), pltpu.VMEM((2 * rows, features), BF)],
        load=(1, 2, 3, 4, 5, 6),
        cost=8.0,
    )

    if wide:
        gains_in = jnp.zeros((2, features), F32)
    else:
        gains_in = jnp.stack(gather_xor(norm_gains.astype(BF)), axis=1)
        gains_in = gains_in.reshape(2, features).astype(F32)

    hid = lax.all_gather(after(turned, q0), "dp", axis=0)
    if not wide:
        hid = jnp.transpose(jnp.take(hid, owner_k, axis=0), (1, 2, 0, 3))
        hid = hid.reshape(1, 3, hidden, features)

    a, q, k, v, w, o, kept, sent, w3, wo, gains = call(
        bind(attend_body, blocks),
        [scalars, x, inv, gains_in, marks] + gathered,
        [
            shape((2 * rows, features), BF),
            shape((rows, cols), BF),
            shape((2 * rows, cols), BF),
            shape((2 * rows, cols), BF),
            shape((heads, rows, 2 * rows), BF),
            shape((rows, cols), BF),
            shape((half, features), BF),
            shape((half, features), BF),
            shape((features, 3 * cols), BF),
            shape((features, cols), BF),
            shape((2, features), F32),
        ],
        [
            pltpu.VMEM((2 * rows, 128 + NX + NY), BF),
            pltpu.VMEM((24, 2 * rows), F32),
            pltpu.VMEM((half, 2 * rows), F32),
            pltpu.VMEM((half, 128 + NX + NY), BF),
            pltpu.VMEM((heads, rows, 2 * rows), BF),
            pltpu.SemaphoreType.DMA((heads,)),
        ],
        place={4},
        load=tuple(range(5, 5 + blocks)),
        cost=16.0,
    )

    def mp_sum(kept_rows, sent_rows):
        came = swap(sent_rows, "mp", 1)
        chip_sum = (kept_rows.astype(F32) + came.astype(F32)).astype(BF)
        return chip_sum, swap(chip_sum, "mp", 2)

    s_own, s_far = mp_sum(kept, sent)
    h1, inv2, c_own = call(
        enter_body,
        [scalars, x_half, s_own, s_far, gains],
        [shape((half, features), F32), shape((half, 1), F32), shape((half, features), BF)],
    )
    c_far = swap(c_own, "mp", 1)

    f, dgate, dup, kept, sent, wd = call(
        feed_body,
        [scalars, c_own, c_far, gy, hid],
        [shape((rows, hidden), BF)] * 3
        + [shape((half, features), BF)] * 2
        + [shape((hidden, features), BF)],
        [pltpu.VMEM((hidden, features), BF)] * 2 + [pltpu.SemaphoreType.DMA((3, hid.shape[0]))],
        spaces={4: pltpu.HBM},
        cost=10.0,
    )
    s_own, s_far = mp_sum(kept, sent)
    y_kept, y_sent, *hidden_grads = call(
        bind(down_body, blocks),
        [scalars, c_own, c_far, gy, wd, f, dgate, dup],
        [shape((half, features), BF)] * 2
        + (
            [shape((blocks // 2, hidden, width), BF)] * 6 if direct
            else [shape((hidden, features), BF)] * 3
        ),
        [pltpu.VMEM((rows, features), BF)],
        behind=[s_own],
        cost=8.5,
    )
    if direct:
        stay0, go0, even1, odd1, even2, odd2 = hidden_grads
        far0 = swap(go0, "dp", 2)
        near1, near2 = swap(odd1, "dp", 1), swap(odd2, "dp", 1)
    else:
        whole = jnp.stack(hidden_grads).reshape(3, hidden, blocks, width)
        whole = jnp.take(jnp.transpose(whole, (2, 0, 1, 3)), owner_k, axis=0)
        hidden_sum = lax.psum_scatter(whole, "dp", scatter_dimension=0)
        hidden_terms = [[hidden_sum[n]] for n in range(3)]

    dh1_q, gal_own, dg2 = call(
        turn_body,
        [scalars, s_own, s_far, h1, inv2, gains, gy],
        [
            shape((quarter, features), F32),
            shape((half, features), BF),
            shape((1, features), F32),
        ],
        behind=[hidden_grads[1]],
        cost=0.0,
    )
    gal_far = swap(gal_own, "mp", 1)
    y_own, y_far = mp_sum(y_kept, y_sent)

    dq, dk, dv, keep, send, dg1, m1, m2, low_sums, all_sums = call(
        attend_back_body,
        [scalars, gal_own, gal_far, w3, wo, q, k, v, w, marks, x, inv],
        [
            shape((rows, cols), BF),
            shape((2 * rows, cols), BF),
            shape((2 * rows, cols), BF),
            shape((2, 2, quarter, features), BF),
            shape((2, 2, quarter, features), BF),
            shape((1, features), F32),
            shape((heads, NX, NX), F32),
            shape((heads, NY, NY), F32),
            shape((heads, NB // 4, 2 * rows), F32),
            shape((heads, NB // 4, 2 * rows), F32),
        ],
        [
            pltpu.VMEM((rows, cols), BF),
            pltpu.VMEM((128, 2 * rows), F32),
            pltpu.VMEM((128, 2 * rows), F32),
            pltpu.VMEM((2 * rows, 128 + NX + NY), BF),
            pltpu.VMEM((half, 2 * rows), BF),
            pltpu.VMEM((rows, NX + NY), F32),
        ],
        store=(0, 1, 2, 5, 6, 7, 8, 9),
        behind=[y_own],
        cost=0.0,
    )
    came = swap(after(send, y_far, *([far0, near1] if direct else [])), "mp", 1)
    to_chip = (keep[1].astype(F32) + came[1].astype(F32)).astype(BF)
    came_x = swap(to_chip, "mp", 2)

    own_limit = jnp.where(side == 1, lengths, counts)
    slots = core * half + jnp.arange(half, dtype=jnp.int32)
    y_low = (
        (slots < own_limit).astype(F32)[:, None]
        * (h1 + (y_own.astype(F32) + y_far.astype(F32)))
    ).astype(BF)
    y_other = swap(y_low, "mp", 1)

    early, middle, late = [], [], []
    if direct:
        keep0, send0 = scatter_near(stay0, after(far0, to_chip))
        far0 = swap(send0, "dp", 4)
        keep1, send1 = scatter_near(even1, after(near1, to_chip))
        far1 = swap(send1, "dp", 2)
        early = [send0, send1]
    table_part = call(
        bind(tables_body, heads, 2 * rows),
        [scalars, m1, m2, low_sums, all_sums],
        [shape((3 * heads, NB), F32)],
        load=(1, 2, 3, 4),
        behind=[to_chip] + early,
        cost=0.0,
    )[0]
    even, odd = call(
        bind(weights_body, blocks),
        [scalars, a, dq, dk, dv, gal_own, gal_far, o, dg1, dg2, table_part],
        [shape((blocks // 2, 4 * width + 16, cols), BF)] * 2,
        [
            pltpu.VMEM((2 * rows, 2 * cols), BF),
            pltpu.VMEM((rows, features), BF),
            pltpu.VMEM((rows, features), BF),
        ],
        behind=[to_chip],
        load=(1, 2, 3, 4, 7, 8),
        cost=0.0,
    )

    if direct:
        last1 = plus(keep1[1], far1[1])
        end1 = swap(last1, "dp", 4)
        last0 = plus(keep0[1], far0[1])
        end0 = swap(last0, "dp", 1)
        middle = [near2, far0, far1]

    own_part, dx_parts = call(
        share_body,
        [scalars, keep, came, came_x, dh1_q, x_q, inv_q, gains],
        [shape((quarter, features), F32), shape((2, quarter, features), BF)],
        cost=0.0,
    )
    dx_came = swap(after(dx_parts, *middle), "dp", half_way)
    if direct:
        keep2, send2 = scatter_near(even2, after(near2, dx_parts))
        far2 = swap(send2, "dp", 2)
        last2 = plus(keep2[1], far2[1])
        end2 = swap(last2, "dp", 4)
        late = [far2, end1, end0]
        hidden_terms = [[keep0, far0, end0], [keep1, far1, end1], [keep2, far2, end2]]
    near_came = swap(after(odd, dx_parts), "dp", 1)
    pair_kept, pair_sent = scatter_near(even, near_came)
    pair_came = swap(pair_sent, "dp", 2)
    last = plus(pair_kept[1], pair_came[1])
    layer_output = call(
        bind(output_body, blocks),
        [scalars, y_low, y_other],
        [shape((rows, features), BF)],
        [pltpu.VMEM((rows, features), BF)],
        cost=0.0,
    )[0]
    pieces = call(
        leave_body,
        [scalars, own_part, dx_parts, dx_came],
        [shape((2, quarter, features), BF)],
        behind=[layer_output],
        cost=0.0,
    )[0]
    last_came = swap(last, "dp", 4)
    p1 = swap(after(pieces, near_came, *late), "mp", 2)
    p2 = swap(after(pieces, pair_came), "mp", 1)
    p3 = swap(after(p1, end2) if direct else p1, "mp", 1)
    hidden_new = call(
        bind(hidden_adam_body, [len(terms) for terms in hidden_terms]),
        [scalars]
        + sum(hidden_terms, [])
        + [jnp.transpose(x, (0, 2, 1)) for x in (hidden_weights, hidden_first, hidden_second)],
        [shape((3, hidden, width), F32)] * 4,
        cost=0.0,
    )
    token_gradient = call(
        bind(token_body, blocks),
        [scalars, pieces, p1, p2, p3, margin_column],
        [shape((rows, features), F32)],
        [
            pltpu.VMEM((rows, features), BF),
            pltpu.VMEM((rows, features), BF),
            pltpu.VMEM((rows, features), F32),
        ],
        cost=0.0,
    )[0]

    small_new = call(
        attention_adam_body,
        [scalars, pair_kept, pair_came, last_came]
        + [attention_weights, attention_first, attention_second]
        + [bias_tables, table_first, table_second],
        [shape(attention_weights.shape, F32)] * 4
        + [shape(bias_tables.shape, F32)] * 4
        + [shape(norm_gains.shape, F32)],
        behind=[token_gradient],
        cost=0.0,
    )
    gain_gradient = small_new[8]
    gain_gradient = gain_gradient + swap(gain_gradient, "mp", 1)
    gain_gradient = gain_gradient + swap(gain_gradient, "mp", 2)
    gain_new = adam_step(norm_gains, gain_first, gain_second, gain_gradient, VECTOR_RATE, 0.0)
    return (
        (layer_output, token_gradient)
        + tuple(small_new[:4])
        + tuple(jnp.transpose(x, (0, 2, 1)) for x in hidden_new)
        + (gain_gradient,)
        + gain_new
        + tuple(small_new[4:8])
    )


def solution(mesh):
    rows = P("dp", None)
    matrix = P(None, "dp", "mp")
    gain = P(None, "dp")
    return jax.shard_map(
        local,
        mesh=mesh,
        in_specs=(rows,) * 2 + (P(),) * 6 + (matrix,) * 6 + (gain,) * 3 + (matrix,) * 3,
        out_specs=(rows,) * 2 + (matrix,) * 8 + (gain,) * 4 + (matrix,) * 4,
        check_vma=False,
    )
```

```python
import jax
import jax.numpy as jnp
from jax import lax
from jax.experimental import pallas as pl
from jax.experimental.pallas import tpu as pltpu
from jax.sharding import PartitionSpec as P

HD = 64
NB = 32
GX = 32
STEP = 5

NORM_EPSILON = 1e-06
SCORE_SCALE = 0.0625
BETA_ONE = 0.5
BETA_TWO = 0.5
ADAM_EPSILON = 1e-08
MATRIX_RATE = 0.03
VECTOR_RATE = 0.2
WEIGHT_DECAY = 0.01

BF = jnp.bfloat16
F32 = jnp.float32
NX = 128
NY = 256
MASKED = -1e30
FLOPS = 1.15e9
HIGH = lax.Precision.HIGHEST


def dot(a, b, precision=None):
    return lax.dot_general(
        a, b, (((1,), (0,)), ((), ())), preferred_element_type=F32, precision=precision
    )


def dot_nt(a, b, precision=None):
    return lax.dot_general(
        a, b, (((1,), (1,)), ((), ())), preferred_element_type=F32, precision=precision
    )


def dot_tn(a, b):
    return lax.dot_general(a, b, (((0,), (0,)), ((), ())), preferred_element_type=F32)


def iota(shape, axis):
    return lax.broadcasted_iota(jnp.int32, shape, axis)


def call(body, ins, outs, scratch=(), spaces=None, behind=(), cost=3.0, load=(), store=(), place=(), early=False):
    spaces = dict(spaces or {})
    spaces.update({n: pltpu.HBM for n in load})
    specs = [
        pl.BlockSpec(memory_space=spaces.get(n, pltpu.VMEM if n else pltpu.SMEM))
        for n in range(len(ins))
    ]
    specs += [pl.BlockSpec(memory_space=pl.ANY)] * len(behind)
    out_specs = [
        pl.BlockSpec(memory_space=pltpu.HBM if n in store or n in place else pltpu.VMEM)
        for n in range(len(outs))
    ]
    moved = [ins[n] for n in load] + [outs[n] for n in store]
    staging = [pltpu.VMEM(x.shape, x.dtype) for x in moved]
    if moved:
        staging.append(pltpu.SemaphoreType.DMA((len(moved),)))
    count, own = len(ins), len(scratch)

    def staged(*refs):
        given, refs = list(refs[:count]), refs[count + len(behind):]
        made, refs = list(refs[:len(outs)]), refs[len(outs):]
        used, buffers = refs[:own], refs[own:]
        copies = []
        for n, at in enumerate(load):
            copies.append(pltpu.make_async_copy(given[at], buffers[n], buffers[-1].at[n]))
            given[at] = buffers[n]
        for item in copies:
            item.start()
        for item in copies:
            item.wait()
        copies = []
        for n, at in enumerate(store, len(load)):
            copies.append(pltpu.make_async_copy(buffers[n], made[at], buffers[-1].at[n]))
            made[at] = buffers[n]

        def flush():
            for item in copies:
                item.start()

        body(*([flush] if early else []), *given, *made, *used)
        if not early:
            flush()
        for item in copies:
            item.wait()

    ins = list(ins)
    for n, space in spaces.items():
        if space is pltpu.HBM:
            ins[n] = pltpu.with_memory_space_constraint(ins[n], pltpu.HBM)
    made_at = [
        pltpu.HBM(x.shape, x.dtype) if n in store or n in place else x for n, x in enumerate(outs)
    ]
    return pl.pallas_call(
        staged,
        in_specs=specs,
        out_specs=out_specs,
        out_shape=made_at,
        scratch_shapes=list(scratch) + staging,
        compiler_params=pltpu.CompilerParams(vmem_limit_bytes=24 * 1024 * 1024),
        cost_estimate=pl.CostEstimate(
            flops=int(cost * FLOPS), bytes_accessed=0, transcendentals=0
        ),
    )(*ins, *behind)


def shape(dims, dtype):
    return jax.ShapeDtypeStruct(tuple(dims), dtype)


def swap(array, axis, mask):
    count = lax.axis_size(axis)
    return lax.ppermute(array, axis, [(i, i ^ mask) for i in range(count)])


def after(array, *others):
    return lax.optimization_barrier((array,) + others)[0]


def gather_xor(block):
    held = [block]
    while len(held) < lax.axis_size("dp"):
        held = held + [swap(x, "dp", len(held)) for x in held]
    return held


def entry_place(entry):
    return entry // 8 * 4 + (0, 2, 1, 3)[entry // 2 % 4]


def plus(left, right):
    return (left.astype(F32) + right.astype(F32)).astype(BF)


def scatter_near(even, came):
    if even.shape[0] == 4:
        return plus(even[:2], came[:2]), plus(even[2:], came[2:])
    sums = plus(even, came)
    while sums.shape[0] > 4:
        middle = sums.shape[0] // 2
        sums = plus(sums[:middle], swap(sums[middle:], "dp", 2 * middle))
    return sums[:2], sums[2:]


def adam_step(weight, moment, square, gradient, step_rate, decay_rate):
    new_moment = BETA_ONE * moment + (1.0 - BETA_ONE) * gradient
    new_square = BETA_TWO * square + (1.0 - BETA_TWO) * gradient * gradient
    moment_hat = new_moment / (1.0 - BETA_ONE**STEP)
    square_hat = new_square / (1.0 - BETA_TWO**STEP)
    new_weight = weight - step_rate * (
        moment_hat / (jnp.sqrt(square_hat) + ADAM_EPSILON) + decay_rate * weight
    )
    return (new_moment, new_square, new_weight)


SIDE, CORE, CHIP, COUNT, LENGTH, FIRST = 0, 1, 2, 3, 4, 5


def take_columns(src, sc, dst_store, blocks, width):
    if width % 128 == 0:
        for k in range(blocks):
            at = pl.multiple_of(sc[FIRST + k] * width, 128)
            dst_store(slice(k * width, (k + 1) * width), src[:, pl.ds(at, width)])
        return
    full = blocks * width
    rows = iota((full, full), 0)
    columns = iota((1, full), 1)
    wanted = jnp.zeros((1, full), jnp.int32)
    for k in range(blocks):
        here = (columns >= k * width) & (columns < (k + 1) * width)
        wanted = jnp.where(here, sc[FIRST + k] * width + columns - k * width, wanted)
    picks = (rows == wanted).astype(BF)
    dst_store(slice(0, full), dot(src[...], picks).astype(BF))


def prep_body(blocks, sc, own, q0, q1, q2, q3, cot, ids, margin, offs,
              x, inv, x_half, x_q, inv_q, gy, marks, raw, rawp):
    rows, width = own.shape[0], own.shape[1] // blocks
    half, quarter = rows // 2, rows // 4
    side, core, chip = sc[SIDE], sc[CORE], sc[CHIP]
    raw[pl.ds(pl.multiple_of(side * rows, rows), rows), :] = own[...]
    for ref, t, u in ((q0, 0, 0), (q1, 0, 1), (q2, 1, 0), (q3, 1, 1)):
        at = (1 - side) * rows + (core ^ t) * half + (chip ^ u) * quarter
        raw[pl.ds(pl.multiple_of(at, quarter), quarter), :] = ref[...]

    def keep(columns, value):
        rawp[:, columns] = value

    take_columns(raw, sc, keep, blocks, width)
    slot = iota((rows, 1), 0)
    patch_ok = (slot < sc[COUNT]).astype(F32)
    text_ok = (slot < sc[LENGTH]).astype(F32)
    patch = rawp[0:rows, :].astype(F32) * patch_ok
    hits = (margin[...] == iota((rows, rows), 1)).astype(BF)
    x[0:rows, :] = patch
    x[rows:, :] = text_ok * (rawp[rows:, :].astype(F32) + dot(hits, patch.astype(BF)))
    for part in range(4):
        at = slice(part * half, (part + 1) * half)
        value = x[at, :]
        inv[at, :] = lax.rsqrt(jnp.mean(value * value, axis=-1, keepdims=True) + NORM_EPSILON)
    start = pl.multiple_of(side * rows + core * half, half)
    x_half[...] = x[pl.ds(start, half), :]
    for s in range(2):
        at = pl.multiple_of((side ^ s) * rows + core * half + chip * quarter, quarter)
        x_q[s] = x[pl.ds(at, quarter), :]
        inv_q[s] = inv[pl.ds(at, quarter), :]

    def keep_low(columns, value):
        rawp[0:rows, columns] = value

    take_columns(cot, sc, keep_low, blocks, width)
    own_limit = jnp.where(side == 1, sc[LENGTH], sc[COUNT])
    for t in range(2):
        at = pl.multiple_of((core ^ t) * half, half)
        ok = (at + iota((half, 1), 0) < own_limit).astype(F32)
        gy[t * half:(t + 1) * half, :] = (rawp[pl.ds(at, half), :].astype(F32) * ok).astype(BF)
    n = ids[...]
    px, py = 4 * (n & (GX - 1)), 4 * (n >> 5)
    lane = iota((rows, 128), 1)
    both = jnp.where(lane == 0, px.astype(F32), jnp.where(lane == 1, py.astype(F32), 0.0))
    under = dot(hits, both.astype(BF))
    off = offs[...]
    cx = under[:, 0:1].astype(jnp.int32) + off[:, 0:1]
    cy = under[:, 1:2].astype(jnp.int32) + off[:, 1:2]
    marks[0:rows, 0:NX] = (iota((rows, NX), 1) == px + 2).astype(BF)
    marks[0:rows, NX:] = (iota((rows, NY), 1) == py + 2).astype(BF)
    marks[rows:, 0:NX] = (iota((rows, NX), 1) == cx).astype(BF)
    marks[rows:, NX:] = (iota((rows, NY), 1) == cy).astype(BF)


def table_places(width, along, named=None):
    lane = iota((NB, width), 1)
    ahead = jnp.where(lane < width // 2, lane, lane - width)
    if along:
        bucket = NB // 2 - 1 - (ahead >> 6)
    else:
        bucket = ((0 - ahead) >> 1) + NB // 2
    bucket = jnp.clip(bucket, 0, NB - 1)
    if named is None:
        named = iota((NB, width), 0)
    return (named == bucket).astype(F32)


def pack_body(weights, gains, tables, out):
    width = weights.shape[1]
    share = tables.shape[1]
    for n in range(4):
        out[n * width:(n + 1) * width, :] = weights[n].astype(BF)
    rest = jnp.zeros((out.shape[0] - 4 * width, out.shape[1]), F32)
    row = iota(rest.shape, 0)
    if width % 128 == 0:
        joined = jnp.concatenate([gains[0:1, :], gains[1:2, :]], axis=1)
        if joined.shape[1] < rest.shape[1]:
            blank = jnp.zeros((1, rest.shape[1] - joined.shape[1]), F32)
            joined = jnp.concatenate([joined, blank], axis=1)
        rest = jnp.where(row == 0, joined, rest)
    lane = iota(rest.shape, 1)
    for n in range(3):
        for t in range(share):
            for h in range(tables.shape[2]):
                here = (row == 1 + n * share + t) & (lane == h)
                rest = jnp.where(here, tables[n, t, h], rest)
    out[4 * width:, :] = rest.astype(BF)


def table_lines(blocks, sc, parts, width):
    share = NB // blocks
    found = []
    for n in range(3):
        lines = [
            parts[b][4 * width:, 0:128].astype(F32)[1 + n * share:1 + (n + 1) * share]
            for b in range(blocks)
        ]
        found.append(jnp.concatenate(lines, axis=0))
    row = iota((NB, 1), 0)
    named = jnp.zeros((NB, 1), jnp.int32)
    for b in range(blocks):
        here = (row >= b * share) & (row < (b + 1) * share)
        named = jnp.where(here, sc[FIRST + b] * share + row - b * share, named)
    return found, named


def attend_body(blocks, sc, *refs):
    x, inv, gains_in, marks = refs[:4]
    parts = refs[4:4 + blocks]
    (a, q, k, v, w_out, o, kept, sent, w3, wo, gains) = refs[4 + blocks:15 + blocks]
    (keys, bias, scores, feats, w, w_sems) = refs[15 + blocks:]
    rows2 = x.shape[0]
    rows = rows2 // 2
    half = rows // 2
    width = x.shape[1] // blocks
    cols = wo.shape[1]
    heads = cols // HD
    side, core = sc[SIDE], sc[CORE]
    for b in range(blocks):
        at = slice(b * width, (b + 1) * width)
        for n in range(3):
            w3[at, n * cols:(n + 1) * cols] = parts[b][n * width:(n + 1) * width, :]
        wo[at, :] = parts[b][3 * width:4 * width, :]
    if width % 128 == 0:
        for b in range(blocks):
            line = parts[b][4 * width:, :].astype(F32)
            at = slice(b * width, (b + 1) * width)
            gains[0:1, at] = line[0:1, :width]
            gains[1:2, at] = line[0:1, width:2 * width]
    else:
        gains[...] = gains_in[...]
    g1 = gains[0:1, :]
    for part in range(4):
        at = slice(part * half, (part + 1) * half)
        a[at, :] = (x[at, :] * inv[at, :] * g1).astype(BF)
        kv = dot(a[at, :], w3[:, cols:]).astype(BF)
        k[at, :] = kv[:, :cols]
        v[at, :] = kv[:, cols:]
    starts = []
    for t in range(2):
        start = pl.multiple_of(side * rows + (core ^ t) * half, half)
        starts.append(start)
        q[t * half:(t + 1) * half, :] = dot(a[pl.ds(start, half), :], w3[:, :cols]).astype(BF)
    tables, named = table_lines(blocks, sc, parts, width)
    base0 = dot_tn(tables[0].astype(BF), table_places(2 * rows2, True, named).astype(BF))
    base1 = dot_tn(tables[1].astype(BF), table_places(2 * NX, False, named).astype(BF))
    base2 = dot_tn(tables[2].astype(BF), table_places(2 * NY, False, named).astype(BF))
    key = iota((1, rows2), 1)
    limit = jnp.where(key < rows, sc[COUNT], rows + sc[LENGTH])
    mask = jnp.where(key < limit, 0.0, MASKED)
    band = rows // (NB // 4)
    keys[:, 128:] = marks[...]
    low_lanes = iota((1, 128), 1) < HD
    triangle = iota((band, rows2), 0) >= (iota((band, rows2), 1) & (band - 1))
    for h in range(heads):
        pair = slice((h // 2) * 128, (h // 2) * 128 + 128)
        mine = low_lanes if h % 2 == 0 else ~low_lanes
        if h % 2 == 0:
            keys[:, 0:128] = k[:, pair]
        for r in range(2 * rows2 // rows * 4 + 1):
            shifted = pltpu.roll(base0[h:h + 1, :], r * band, 1) if r else base0[h:h + 1, :]
            bias[r:r + 1, :] = shifted[:, :rows2] + mask
        t1 = pltpu.roll(
            jnp.broadcast_to(base1[h:h + 1, :], (NX, 2 * NX)), 0, 1, stride=1, stride_axis=0
        )[:, :NX].astype(BF)
        t2 = pltpu.roll(
            jnp.broadcast_to(base2[h:h + 1, :], (NY, 2 * NY)), 0, 1, stride=1, stride_axis=0
        )[:, :NY].astype(BF)
        for t in range(2):
            at = slice(t * half, (t + 1) * half)
            mq = marks[pl.ds(starts[t], half), :]
            feats[:, 0:128] = jnp.where(mine, q[at, pair].astype(F32) * SCORE_SCALE, 0.0).astype(BF)
            feats[:, 128:128 + NX] = dot(mq[:, :NX], t1).astype(BF)
            feats[:, 128 + NX:] = dot(mq[:, NX:], t2).astype(BF)
            scores[...] = dot_nt(feats[...], keys[...])
            first = (side * rows + (core ^ t) * half) // band
            for sb in range(half // band):
                z = scores[sb * band:(sb + 1) * band, :]
                z = z + jnp.where(
                    triangle, bias[pl.ds(first + sb + 1, 1), :], bias[pl.ds(first + sb, 1), :]
                )
                e = jnp.exp(z - jnp.max(z, axis=-1, keepdims=True))
                e = e * (1.0 / jnp.sum(e, axis=-1, keepdims=True))
                w[h, t * half + sb * band:t * half + (sb + 1) * band, :] = e.astype(BF)
            mixed = dot(w[h, at, :], v[:, pair])
            if h % 2 == 0:
                o[at, pair] = mixed.astype(BF)
            else:
                o[at, pair] = jnp.where(mine, mixed.astype(BF), o[at, pair])
        pltpu.make_async_copy(w.at[h], w_out.at[h], w_sems.at[h]).start()
    kept[...] = dot_nt(o[0:half, :], wo[...]).astype(BF)
    sent[...] = dot_nt(o[half:, :], wo[...]).astype(BF)
    for h in range(heads):
        pltpu.make_async_copy(w.at[h], w_out.at[h], w_sems.at[h]).wait()


def enter_body(sc, x_half, s_own, s_far, gains, h1, inv2, c):
    value = x_half[...] + (s_own[...].astype(F32) + s_far[...].astype(F32))
    h1[...] = value
    inverse = lax.rsqrt(jnp.mean(value * value, axis=-1, keepdims=True) + NORM_EPSILON)
    inv2[...] = inverse
    c[...] = (value * inverse * gains[1:2, :]).astype(BF)


GELU_A = 0.7978845608028654
GELU_B = 0.044715


def hidden_copies(sc, hid, targets, sems):
    blocks, width = hid.shape[0], hid.shape[3]
    copies = []
    for n, dst in enumerate(targets):
        copies.append([])
        for b in range(blocks):
            row = sc[FIRST + blocks + b] if blocks > 1 else 0
            copies[n].append(pltpu.make_async_copy(
                hid.at[row, n], dst.at[:, pl.ds(b * width, width)], sems.at[n, b]
            ))
    return copies


def feed_body(sc, c_own, c_far, gy_in, hid, f, dgate, dup, kept, sent, wd,
              wg, wu, sems, c, gy, in_sems):
    half = c_own.shape[0]
    entering = [
        pltpu.make_async_copy(src, dst, in_sems.at[n])
        for n, (src, dst) in enumerate((
            (c_own, c.at[pl.ds(0, half)]), (c_far, c.at[pl.ds(half, half)]), (gy_in, gy)
        ))
    ]
    for item in entering:
        item.start()
    copies = hidden_copies(sc, hid, (wg, wu, wd), sems)
    for group in copies:
        for item in group:
            item.start()
    for item in entering:
        item.wait()
    for t, out in ((0, kept), (1, sent)):
        at = slice(t * half, (t + 1) * half)

        def ready(n):
            for item in copies[n] if t == 0 else ():
                item.wait()

        ready(0)
        gate = dot_nt(c[at, :], wg[...])
        ready(1)
        up = dot_nt(c[at, :], wu[...])
        ready(2)
        df = dot_nt(gy[at, :], wd[...]).astype(BF).astype(F32)
        inner = jnp.tanh(GELU_A * (gate + GELU_B * gate * gate * gate))
        gelu = 0.5 * gate * (1.0 + inner)
        slope = 0.5 * (1.0 + inner) + 0.5 * gate * (1.0 - inner * inner) * (
            GELU_A * (1.0 + 3.0 * GELU_B * gate * gate)
        )
        f[at, :] = (gelu * up).astype(BF)
        dgate[at, :] = (df * up * slope).astype(BF)
        dup[at, :] = (df * gelu).astype(BF)
        out[...] = (dot(dgate[at, :], wg[...]) + dot(dup[at, :], wu[...])).astype(BF)


def down_body(blocks, sc, c_own, c_far, gy, wd, f, dgate, dup, kept, sent, *refs):
    grads, c = refs[:-1], refs[-1]
    half = c_own.shape[0]
    width = c_own.shape[1] // blocks
    c[0:half, :] = c_own[...]
    c[half:, :] = c_far[...]
    for n, (left, right) in enumerate(((dgate, c), (dup, c), (f, gy))):
        product = dot_tn(left[...], right[...]).astype(BF)
        if len(grads) == 3:
            grads[n][...] = product
            continue
        for b in range(blocks):
            bit, place = (b & 1, entry_place(b)) if n else (b >> 1 & 1, (b & 1) + 2 * (b >> 2))
            grads[2 * n + bit][place] = product[:, b * width:(b + 1) * width]
    kept[...] = dot(f[0:half, :], wd[...]).astype(BF)
    sent[...] = dot(f[half:, :], wd[...]).astype(BF)


def norm_back(value, inverse, gain, grad):
    weighted = grad * gain
    inner = jnp.mean(weighted * value, axis=-1, keepdims=True)
    return inverse * weighted - value * (inverse * inverse * inverse * inner)


def turn_body(sc, s_own, s_far, h1, inv2, gains, gy, dh1_q, gal, dg2):
    half = h1.shape[0]
    quarter = half // 2
    dc = s_own[...].astype(F32) + s_far[...].astype(F32)
    value, inverse = h1[...], inv2[...]
    dh1 = gy[0:half, :].astype(F32) + norm_back(value, inverse, gains[1:2, :], dc)
    gal[...] = dh1.astype(BF)
    pick = sc[CHIP] == 0
    dh1_q[...] = jnp.where(pick, dh1[:quarter], dh1[quarter:])
    terms = dc * (value * inverse)
    mine = jnp.where(pick, terms[:quarter], terms[quarter:])
    dg2[...] = jnp.sum(mine, axis=0, keepdims=True)


def attend_back_body(flush, sc, gal0, gal1, w3, wo, q, k, v, w, marks, x, inv,
                     dq, dk, dv, keep, send, dg1, m1, m2, low_sums, all_sums,
                     dol, dkt, dvt, keys, dsl, picked):
    half = gal0.shape[0]
    rows = 2 * half
    rows2 = x.shape[0]
    cols = wo.shape[1]
    heads = cols // HD
    side, core, chip = sc[SIDE], sc[CORE], sc[CHIP]
    dol[0:half, :] = dot(gal0[...], wo[...]).astype(BF)
    dol[half:, :] = dot(gal1[...], wo[...]).astype(BF)
    band = rows // (NB // 4)
    keys[:, 128:] = marks[...]
    low_lanes = iota((1, 128), 1) < HD
    triangle = iota((band, rows2), 0) >= (iota((band, rows2), 1) & (band - 1))
    for h in range(heads):
        pair = slice((h // 2) * 128, (h // 2) * 128 + 128)
        mine = low_lanes if h % 2 == 0 else ~low_lanes
        if h % 2 == 0:
            keys[:, 0:128] = k[:, pair]
        for t in range(2):
            at = slice(t * half, (t + 1) * half)
            dol_h = jnp.where(mine, dol[at, pair], jnp.zeros((), BF))
            q_h = jnp.where(mine, q[at, pair], jnp.zeros((), BF))
            dw = dot_nt(dol_h, v[:, pair])
            for sb in range(half // band):
                rs = slice(sb * band, (sb + 1) * band)
                here = w[h, t * half + sb * band:t * half + (sb + 1) * band, :].astype(F32)
                part = here * dw[rs, :]
                ds = part - here * jnp.sum(part, axis=-1, keepdims=True)
                place = t * (half // band) + sb
                all_sums[h, place:place + 1, :] = jnp.sum(ds, axis=0, keepdims=True)
                low_sums[h, place:place + 1, :] = jnp.sum(
                    jnp.where(triangle, ds, 0.0), axis=0, keepdims=True
                )
                dsl[rs, :] = (ds * SCORE_SCALE).astype(BF)
            dvt_part = dot_tn(dol_h, w[h, at, :])
            dkt_part = dot_tn(q_h, dsl[...])
            if h % 2 == 0 and t == 0:
                dvt[...] = dvt_part
                dkt[...] = dkt_part
            else:
                dvt[...] += dvt_part
                dkt[...] += dkt_part
            out = dot(dsl[...], keys[...])
            if h % 2 == 0:
                dq[at, pair] = out[:, 0:128].astype(BF)
            else:
                dq[at, pair] = jnp.where(mine, out[:, 0:128].astype(BF), dq[at, pair])
            picked[at, :] = out[:, 128:]
        if h % 2 == 1:
            dv[:, pair] = dvt[...].T.astype(BF)
            dk[:, pair] = dkt[...].T.astype(BF)
        first = picked[...]
        upper = first.astype(BF)
        lower = (first - upper.astype(F32)).astype(BF)
        total1 = jnp.zeros((NX, NX), F32)
        total2 = jnp.zeros((NY, NY), F32)
        for t in range(2):
            at = slice(t * half, (t + 1) * half)
            mq = marks[pl.ds(pl.multiple_of(side * rows + (core ^ t) * half, half), half), :]
            for value in (upper, lower):
                total1 = total1 + dot_tn(mq[:, :NX], value[at, :NX])
                total2 = total2 + dot_tn(mq[:, NX:], value[at, NX:])
        m1[h] = total1
        m2[h] = total2
    flush()
    quarter = half // 2
    gain_sum = jnp.zeros((1, x.shape[1]), F32)
    for s in range(2):
        for t in range(2):
            for u in range(2):
                start = (side ^ s) * rows + (core ^ t) * half + (chip ^ u) * quarter
                at = pl.ds(pl.multiple_of(start, quarter), quarter)
                da = dot_nt(dk[at, :], w3[:, cols:2 * cols]) + dot_nt(dv[at, :], w3[:, 2 * cols:])
                if s == 0:
                    mine_q = pl.ds(pl.multiple_of(t * half + (chip ^ u) * quarter, quarter), quarter)
                    da = da + dot_nt(dq[mine_q, :], w3[:, :cols])
                low = da.astype(BF)
                if t == 0:
                    keep[u, s] = low
                else:
                    send[u, s] = low
                gain_sum = gain_sum + jnp.sum(da * (x[at, :] * inv[at, :]), axis=0, keepdims=True)
    dg1[...] = gain_sum


def tables_body(heads, rows2, sc, m1, m2, low_sums, all_sums, out):
    rows = rows2 // 2
    half = rows // 2
    band = rows // (NB // 4)
    side, core = sc[SIDE], sc[CORE]
    scale = 1.0 / SCORE_SCALE
    line = jnp.zeros((heads, 2 * rows2), F32)
    blank = jnp.zeros((heads, rows2), F32)
    for t in range(2):
        for sb in range(half // band):
            place = t * (half // band) + sb
            row = (side * rows + (core ^ t) * half) // band + sb
            low = low_sums[:, place, :]
            high = all_sums[:, place, :] - low
            back = 2 * rows2 - row * band
            line = line + pltpu.roll(jnp.concatenate([high, blank], axis=1), back, 1)
            line = line + pltpu.roll(jnp.concatenate([low, blank], axis=1), back - band, 1)
    sums0 = [line]
    sums1 = [diagonals(m1[h], NX) * scale for h in range(heads)]
    sums2 = [diagonals(m2[h], NY) * scale for h in range(heads)]
    for n, (sums, places) in enumerate((
        (sums0, table_places(2 * rows2, True)),
        (sums1, table_places(2 * NX, False)),
        (sums2, table_places(2 * NY, False)),
    )):
        out[n * heads:(n + 1) * heads, :] = dot_nt(jnp.concatenate(sums, axis=0), places, HIGH)


def diagonals(square, size):
    mirror = (iota((size, size), 0) + iota((size, size), 1) == size - 1).astype(F32)
    flipped = dot(mirror, square, HIGH)
    wide = jnp.concatenate([flipped, jnp.zeros((size, size), F32)], axis=1)
    turned = pltpu.roll(wide, 0, 1, stride=1, stride_axis=0)
    return pltpu.roll(jnp.sum(turned, axis=0, keepdims=True), size + 1, 1)


def weights_body(blocks, sc, a, q_grad, k_grad, v_grad, gal0, gal1, o, dg1, dg2, tables, even, odd,
                 joined, gal, own):
    outs = [(odd if b % 2 else even).at[entry_place(b)] for b in range(blocks)]
    rows2 = a.shape[0]
    rows = rows2 // 2
    half = rows // 2
    width = a.shape[1] // blocks
    cols = o.shape[1]
    joined[:, 0:cols] = k_grad[...]
    joined[:, cols:] = v_grad[...]
    gal[0:half, :] = gal0[...]
    gal[half:, :] = gal1[...]
    for t in range(2):
        start = pl.multiple_of(sc[SIDE] * rows + (sc[CORE] ^ t) * half, half)
        own[t * half:(t + 1) * half, :] = a[pl.ds(start, half), :]
    count, buckets = tables.shape
    table_rest = jnp.concatenate([
        jnp.zeros((1, cols), F32),
        jnp.concatenate([tables[...], jnp.zeros((count, cols - buckets), F32)], axis=1),
        jnp.zeros((15 - count, cols), F32),
    ], axis=0)
    first_row = iota((16, 1), 0) == 0
    for b in range(blocks):
        at = slice(b * width, (b + 1) * width)
        kv = dot_tn(a[:, at], joined[...]).astype(BF)
        outs[b][0:width, :] = dot_tn(own[:, at], q_grad[...]).astype(BF)
        outs[b][width:2 * width, :] = kv[:, :cols]
        outs[b][2 * width:3 * width, :] = kv[:, cols:]
        outs[b][3 * width:4 * width, :] = dot_tn(gal[:, at], o[...]).astype(BF)
        line = jnp.concatenate([dg1[:, at], dg2[:, at]], axis=1)
        if 2 * width < cols:
            line = jnp.concatenate([line, jnp.zeros((1, cols - 2 * width), F32)], axis=1)
        outs[b][4 * width:, :] = jnp.where(first_row, line, table_rest).astype(BF)


def halves_swapped(value):
    middle = value.shape[1] // 2
    return jnp.concatenate([value[:, middle:], value[:, :middle]], axis=1).astype(F32)


def share_body(sc, keep, came, came_x, dh1, x_q, inv_q, gains, own, out):
    g1 = gains[0:1, :]
    for s in range(2):
        da = keep[0, s].astype(F32) + came[0, s].astype(F32) + came_x[s].astype(F32)
        dx = norm_back(x_q[s], inv_q[s], g1, da)
        if s == 0:
            dx = dx + dh1[...]
            own[...] = dx
        out[s] = dx.astype(BF)


def leave_body(sc, own, parts, came, out):
    quarter = own.shape[0]
    side, core, chip = sc[SIDE], sc[CORE], sc[CHIP]
    slot = core * 2 * quarter + chip * quarter + iota((quarter, 1), 0)
    own_limit = jnp.where(side == 1, sc[LENGTH], sc[COUNT])
    dx = own[...] + halves_swapped(came[1])
    out[0] = (dx * (slot < own_limit).astype(F32)).astype(BF)
    dx = parts[1].astype(F32) + halves_swapped(came[0])
    out[1] = (dx * (slot < sc[LENGTH]).astype(F32)).astype(BF)


def put_columns(src, sc, dst, blocks, width):
    if width % 128 == 0:
        for k in range(blocks):
            at = pl.multiple_of(sc[FIRST + k] * width, 128)
            dst[:, pl.ds(at, width)] = src[:, k * width:(k + 1) * width].astype(dst.dtype)
        return
    full = blocks * width
    columns = iota((full, full), 1)
    rows = iota((full, 1), 0)
    wanted = jnp.zeros((full, 1), jnp.int32)
    for k in range(blocks):
        here = (rows >= k * width) & (rows < (k + 1) * width)
        wanted = jnp.where(here, sc[FIRST + k] * width + rows - k * width, wanted)
    picks = (columns == wanted).astype(F32)
    dst[...] = dot(src[...].astype(F32), picks, HIGH).astype(dst.dtype)


def token_body(blocks, sc, p0, p1, p2, p3, margin, out, own, text, total):
    rows = own.shape[0]
    half, quarter = rows // 2, rows // 4
    width = own.shape[1] // blocks
    side, core, chip = sc[SIDE], sc[CORE], sc[CHIP]
    for ref, t, u in ((p0, 0, 0), (p1, 0, 1), (p2, 1, 0), (p3, 1, 1)):
        at = pl.ds(pl.multiple_of((core ^ t) * half + (chip ^ u) * quarter, quarter), quarter)
        own[at, :] = ref[0]
        text[at, :] = ref[1]

    @pl.when(side == 1)
    def _():
        total[...] = own[...].astype(F32)

    @pl.when(side == 0)
    def _():
        hits = (margin[...] == iota((rows, rows), 1)).astype(BF)
        ok = (iota((rows, 1), 0) < sc[COUNT]).astype(F32)
        total[...] = own[...].astype(F32) + ok * dot_tn(hits, text[...])

    put_columns(total, sc, out, blocks, width)


def output_body(blocks, sc, y_own, y_far, out, whole):
    half = y_own.shape[0]
    core = sc[CORE]
    whole[pl.ds(pl.multiple_of(core * half, half), half), :] = y_own[...]
    whole[pl.ds(pl.multiple_of((1 - core) * half, half), half), :] = y_far[...]
    put_columns(whole, sc, out, blocks, y_own.shape[1] // blocks)


def attention_adam_body(sc, kept, came, last, *refs):
    matrices, tables = refs[0:3], refs[3:6]
    matrix_out, table_out = refs[6:10], refs[10:14]
    total = kept[0].astype(F32) + came[0].astype(F32) + last[...].astype(F32)

    def step(ins, outs, at, value, rate, decay):
        outs[0][at] = value
        new = adam_step(ins[0][at], ins[1][at], ins[2][at], value, rate, decay)
        for out, result in zip(outs[1:], new):
            out[at] = result

    number, width = matrices[0].shape[0], matrices[0].shape[1]
    for n in range(number):
        value = total[n * width:(n + 1) * width, :]
        step(matrices, matrix_out, n, value, MATRIX_RATE, WEIGHT_DECAY)
    small = total[number * width:, :]
    share, heads = tables[0].shape[1], tables[0].shape[2]
    wanted = (
        iota((share, NB), 1) == sc[FIRST] * share + iota((share, NB), 0)
    ).astype(F32)
    for n in range(3):
        lines = small[1 + n * heads:1 + (n + 1) * heads, 0:NB]
        step(tables, table_out, n, dot_nt(wanted, lines, HIGH), VECTOR_RATE, 0.0)


def hidden_adam_body(counts, sc, *refs):
    terms, refs = refs[:sum(counts)], refs[sum(counts):]
    matrices, outs = refs[:3], refs[3:]
    for n, count in enumerate(counts):
        total = jnp.zeros(matrices[0].shape[1:], F32)
        for term in terms[sum(counts[:n]):sum(counts[:n + 1])]:
            total = total + (term[0] if len(term.shape) == 3 else term[...]).astype(F32)
        outs[0][n] = total
        new = adam_step(
            matrices[0][n], matrices[1][n], matrices[2][n], total, MATRIX_RATE, WEIGHT_DECAY
        )
        for out, result in zip(outs[1:], new):
            out[n] = result


def bind(body, *first):
    def bound(*refs):
        return body(*first, *refs)

    return bound


def local(
    tokens,
    cotangent,
    patch_counts,
    patch_ids,
    text_lengths,
    margin,
    box_offsets,
    owners,
    attention_weights,
    attention_first,
    attention_second,
    hidden_weights,
    hidden_first,
    hidden_second,
    norm_gains,
    gain_first,
    gain_second,
    bias_tables,
    table_first,
    table_second,
):
    blocks = lax.axis_size("dp")
    half_way = blocks // 2
    me = lax.axis_index("dp")
    mp = lax.axis_index("mp")
    page = me % half_way
    side = me // half_way
    core, chip = mp % 2, mp // 2
    rows, features = tokens.shape
    half, quarter = rows // 2, rows // 4
    width = features // blocks
    cols = attention_weights.shape[2]
    heads = cols // HD
    hidden = hidden_weights.shape[2]
    share = NB // blocks
    wide = width % 128 == 0

    mine = lax.dynamic_slice_in_dim(tokens, core * half + chip * quarter, quarter, 0)
    packed = call(
        pack_body,
        [attention_weights, norm_gains, bias_tables],
        [shape((4 * width + 16, cols), BF)],
        spaces={0: pltpu.VMEM, 2: pltpu.SMEM},
        behind=[mine],
        cost=2.0,
    )[0]
    turned = jnp.transpose(hidden_weights, (0, 2, 1)).astype(BF)
    eight = blocks == 8
    direct = eight and wide
    q0 = swap(mine, "dp", half_way)
    q1 = swap(q0, "mp", 2)
    q2 = swap(q0, "mp", 1)
    q3 = swap(q1, "mp", 1)
    if eight:
        near, far, opposite = [lambda v, m=m: swap(v, "dp", m) for m in (1, 2, 4)]
        ga = {0: packed}
        ga[4], ga[2], ga[1] = opposite(packed), far(packed), near(packed)
        ga[3] = near(after(ga[2], ga[1]))
        held = after(ga[4], q0, ga[2])
        ga[6], ga[5] = far(held), near(held)
        ga[7] = near(after(ga[6], ga[3], q2, q3))
        gathered = [ga[k] for k in range(8)]
    else:
        gathered = gather_xor(packed)

    order = jnp.arange(blocks, dtype=jnp.int32)
    place_of = jnp.sum(
        jnp.where(owners[None, :] == order[:, None], order[None, :], 0), axis=1
    )
    owner_k = me ^ order
    place_k = jnp.sum(
        jnp.where(owner_k[:, None] == order[None, :], place_of[None, :], 0), axis=1
    )
    counts = lax.dynamic_index_in_dim(patch_counts, page, 0, True)
    lengths = lax.dynamic_index_in_dim(text_lengths, page, 0, True)
    scalars = jnp.concatenate([
        jnp.stack([side, core, chip]).astype(jnp.int32), counts, lengths, place_k, owner_k
    ]).astype(jnp.int32)
    ids_column = lax.dynamic_index_in_dim(patch_ids, page, 0, False)[:, None]
    margin_column = lax.dynamic_index_in_dim(margin, page, 0, False)[:, None]
    offsets = lax.dynamic_index_in_dim(box_offsets, page, 0, False)

    x, inv, x_half, x_q, inv_q, gy, marks = call(
        bind(prep_body, blocks),
        [scalars, tokens, q0, q1, q2, q3, cotangent, ids_column, margin_column, offsets],
        [
            shape((2 * rows, features), F32),
            shape((2 * rows, 1), F32),
            shape((half, features), F32),
            shape((2, quarter, features), F32),
            shape((2, quarter, 1), F32),
            shape((rows, features), BF),
            shape((2 * rows, NX + NY), BF),
        ],
        [pltpu.VMEM((2 * rows, features), BF), pltpu.VMEM((2 * rows, features), BF)],
        load=(1, 2, 3, 4, 5, 6),
        cost=8.0,
    )

    if wide:
        gains_in = jnp.zeros((2, features), F32)
    else:
        gains_in = jnp.stack(gather_xor(norm_gains.astype(BF)), axis=1)
        gains_in = gains_in.reshape(2, features).astype(F32)

    hid = lax.all_gather(after(turned, q0), "dp", axis=0)
    if not wide:
        hid = jnp.transpose(jnp.take(hid, owner_k, axis=0), (1, 2, 0, 3))
        hid = hid.reshape(1, 3, hidden, features)

    a, q, k, v, w, o, kept, sent, w3, wo, gains = call(
        bind(attend_body, blocks),
        [scalars, x, inv, gains_in, marks] + gathered,
        [
            shape((2 * rows, features), BF),
            shape((rows, cols), BF),
            shape((2 * rows, cols), BF),
            shape((2 * rows, cols), BF),
            shape((heads, rows, 2 * rows), BF),
            shape((rows, cols), BF),
            shape((half, features), BF),
            shape((half, features), BF),
            shape((features, 3 * cols), BF),
            shape((features, cols), BF),
            shape((2, features), F32),
        ],
        [
            pltpu.VMEM((2 * rows, 128 + NX + NY), BF),
            pltpu.VMEM((24, 2 * rows), F32),
            pltpu.VMEM((half, 2 * rows), F32),
            pltpu.VMEM((half, 128 + NX + NY), BF),
            pltpu.VMEM((heads, rows, 2 * rows), BF),
            pltpu.SemaphoreType.DMA((heads,)),
        ],
        place={4},
        load=tuple(range(5, 5 + blocks)),
        cost=16.0,
    )

    def mp_sum(kept_rows, sent_rows):
        came = swap(sent_rows, "mp", 1)
        chip_sum = (kept_rows.astype(F32) + came.astype(F32)).astype(BF)
        return chip_sum, swap(chip_sum, "mp", 2)

    s_own, s_far = mp_sum(kept, sent)
    h1, inv2, c_own = call(
        enter_body,
        [scalars, x_half, s_own, s_far, gains],
        [shape((half, features), F32), shape((half, 1), F32), shape((half, features), BF)],
        store=(2,),
    )
    c_far = swap(c_own, "mp", 1)

    f, dgate, dup, kept, sent, wd = call(
        feed_body,
        [scalars, c_own, c_far, gy, hid],
        [shape((rows, hidden), BF)] * 3
        + [shape((half, features), BF)] * 2
        + [shape((hidden, features), BF)],
        [pltpu.VMEM((hidden, features), BF)] * 2
        + [pltpu.SemaphoreType.DMA((3, hid.shape[0]))]
        + [pltpu.VMEM((rows, features), BF)] * 2
        + [pltpu.SemaphoreType.DMA((3,))],
        spaces={n: pltpu.HBM for n in (1, 2, 3, 4)},
        cost=10.0,
    )
    s_own, s_far = mp_sum(kept, sent)
    y_kept, y_sent, *hidden_grads = call(
        bind(down_body, blocks),
        [scalars, c_own, c_far, gy, wd, f, dgate, dup],
        [shape((half, features), BF)] * 2
        + (
            [shape((blocks // 2, hidden, width), BF)] * 6 if direct
            else [shape((hidden, features), BF)] * 3
        ),
        [pltpu.VMEM((rows, features), BF)],
        behind=[s_own],
        load=(1, 2, 3),
        cost=8.5,
    )
    if direct:
        stay0, go0, even1, odd1, even2, odd2 = hidden_grads
        far0 = swap(go0, "dp", 2)
        near1, near2 = swap(odd1, "dp", 1), swap(odd2, "dp", 1)
    else:
        whole = jnp.stack(hidden_grads).reshape(3, hidden, blocks, width)
        whole = jnp.take(jnp.transpose(whole, (2, 0, 1, 3)), owner_k, axis=0)
        hidden_sum = lax.psum_scatter(whole, "dp", scatter_dimension=0)
        hidden_terms = [[hidden_sum[n]] for n in range(3)]

    dh1_q, gal_own, dg2 = call(
        turn_body,
        [scalars, s_own, s_far, h1, inv2, gains, gy],
        [
            shape((quarter, features), F32),
            shape((half, features), BF),
            shape((1, features), F32),
        ],
        behind=[hidden_grads[1]],
        cost=0.0,
    )
    gal_far = swap(gal_own, "mp", 1)
    y_own, y_far = mp_sum(y_kept, y_sent)

    dq, dk, dv, keep, send, dg1, m1, m2, low_sums, all_sums = call(
        attend_back_body,
        [scalars, gal_own, gal_far, w3, wo, q, k, v, w, marks, x, inv],
        [
            shape((rows, cols), BF),
            shape((2 * rows, cols), BF),
            shape((2 * rows, cols), BF),
            shape((2, 2, quarter, features), BF),
            shape((2, 2, quarter, features), BF),
            shape((1, features), F32),
            shape((heads, NX, NX), F32),
            shape((heads, NY, NY), F32),
            shape((heads, NB // 4, 2 * rows), F32),
            shape((heads, NB // 4, 2 * rows), F32),
        ],
        [
            pltpu.VMEM((rows, cols), BF),
            pltpu.VMEM((128, 2 * rows), F32),
            pltpu.VMEM((128, 2 * rows), F32),
            pltpu.VMEM((2 * rows, 128 + NX + NY), BF),
            pltpu.VMEM((half, 2 * rows), BF),
            pltpu.VMEM((rows, NX + NY), F32),
        ],
        store=(0, 1, 2, 6, 7, 8, 9),
        early=True,
        behind=[y_own],
        cost=0.0,
    )
    came = swap(after(send, y_far, *([far0, near1] if direct else [])), "mp", 1)
    to_chip = (keep[1].astype(F32) + came[1].astype(F32)).astype(BF)
    came_x = swap(to_chip, "mp", 2)

    own_limit = jnp.where(side == 1, lengths, counts)
    slots = core * half + jnp.arange(half, dtype=jnp.int32)
    y_low = (
        (slots < own_limit).astype(F32)[:, None]
        * (h1 + (y_own.astype(F32) + y_far.astype(F32)))
    ).astype(BF)
    y_other = swap(y_low, "mp", 1)

    early, middle, late = [], [], []
    if direct:
        keep0, send0 = scatter_near(stay0, after(far0, to_chip))
        far0 = swap(send0, "dp", 4)
        keep1, send1 = scatter_near(even1, after(near1, to_chip))
        far1 = swap(send1, "dp", 2)
        early = [send0, send1]
    table_part = call(
        bind(tables_body, heads, 2 * rows),
        [scalars, m1, m2, low_sums, all_sums],
        [shape((3 * heads, NB), F32)],
        load=(1, 2, 3, 4),
        behind=[to_chip] + early,
        cost=0.0,
    )[0]
    even, odd = call(
        bind(weights_body, blocks),
        [scalars, a, dq, dk, dv, gal_own, gal_far, o, dg1, dg2, table_part],
        [shape((blocks // 2, 4 * width + 16, cols), BF)] * 2,
        [
            pltpu.VMEM((2 * rows, 2 * cols), BF),
            pltpu.VMEM((rows, features), BF),
            pltpu.VMEM((rows, features), BF),
        ],
        behind=[to_chip],
        load=(1, 2, 3, 4, 7, 8),
        cost=0.0,
    )

    if direct:
        last1 = plus(keep1[1], far1[1])
        end1 = swap(last1, "dp", 4)
        last0 = plus(keep0[1], far0[1])
        end0 = swap(last0, "dp", 1)
        middle = [near2, far0]

    own_part, dx_parts = call(
        share_body,
        [scalars, keep, came, came_x, dh1_q, x_q, inv_q, gains],
        [shape((quarter, features), F32), shape((2, quarter, features), BF)],
        cost=0.0,
    )
    dx_came = swap(after(dx_parts, *middle), "dp", half_way)
    if direct:
        keep2, send2 = scatter_near(even2, after(near2, dx_parts))
        far2 = swap(send2, "dp", 2)
        last2 = plus(keep2[1], far2[1])
        end2 = swap(last2, "dp", 4)
        late = [far2, end0]
        hidden_terms = [[keep0, far0, end0], [keep1, far1, end1], [keep2, far2, end2]]
    near_came = swap(after(odd, dx_parts, *middle[:2]), "dp", 1)
    pair_kept, pair_sent = scatter_near(even, near_came)
    pair_came = swap(pair_sent, "dp", 2)
    last = plus(pair_kept[1], pair_came[1])
    layer_output = call(
        bind(output_body, blocks),
        [scalars, y_low, y_other],
        [shape((rows, features), BF)],
        [pltpu.VMEM((rows, features), BF)],
        cost=0.0,
    )[0]
    pieces = call(
        leave_body,
        [scalars, own_part, dx_parts, dx_came],
        [shape((2, quarter, features), BF)],
        behind=[layer_output],
        cost=0.0,
    )[0]
    last_came = swap(last, "dp", 4)
    line = slice(4 * width, 4 * width + 1)
    gain_lines = pair_kept[:, line].astype(F32) + pair_came[:, line].astype(F32)
    gain_lines = gain_lines + swap(gain_lines, "mp", 1)
    gain_lines = gain_lines + swap(gain_lines, "mp", 2)
    gain_gradient = gain_lines[0] + swap(gain_lines[1], "dp", 4)
    gain_gradient = gain_gradient[0, :2 * width].reshape(2, width)
    p1 = swap(after(pieces, near_came, *late), "mp", 2)
    p2 = swap(pieces, "mp", 1)
    p3 = swap(after(p1, end1) if direct else p1, "mp", 1)
    hidden_new = call(
        bind(hidden_adam_body, [len(terms) for terms in hidden_terms]),
        [scalars]
        + sum(hidden_terms, [])
        + [jnp.transpose(x, (0, 2, 1)) for x in (hidden_weights, hidden_first, hidden_second)],
        [shape((3, hidden, width), F32)] * 4,
        cost=0.0,
    )
    token_gradient = call(
        bind(token_body, blocks),
        [scalars, pieces, p1, p2, p3, margin_column],
        [shape((rows, features), F32)],
        [
            pltpu.VMEM((rows, features), BF),
            pltpu.VMEM((rows, features), BF),
            pltpu.VMEM((rows, features), F32),
        ],
        cost=0.0,
    )[0]

    small_new = call(
        attention_adam_body,
        [scalars, pair_kept, pair_came, last_came]
        + [attention_weights, attention_first, attention_second]
        + [bias_tables, table_first, table_second],
        [shape(attention_weights.shape, F32)] * 4
        + [shape(bias_tables.shape, F32)] * 4,
        behind=[token_gradient],
        cost=0.0,
    )
    gain_new = adam_step(norm_gains, gain_first, gain_second, gain_gradient, VECTOR_RATE, 0.0)
    return (
        (layer_output, token_gradient)
        + tuple(small_new[:4])
        + tuple(jnp.transpose(x, (0, 2, 1)) for x in hidden_new)
        + (gain_gradient,)
        + gain_new
        + tuple(small_new[4:8])
    )


def solution(mesh):
    rows = P("dp", None)
    matrix = P(None, "dp", "mp")
    gain = P(None, "dp")
    return jax.shard_map(
        local,
        mesh=mesh,
        in_specs=(rows,) * 2 + (P(),) * 6 + (matrix,) * 6 + (gain,) * 3 + (matrix,) * 3,
        out_specs=(rows,) * 2 + (matrix,) * 8 + (gain,) * 4 + (matrix,) * 4,
        check_vma=False,
    )
```

```python
import jax
import jax.numpy as jnp
from jax import lax
from jax.experimental import pallas as pl
from jax.experimental.pallas import tpu as pltpu
from jax.sharding import PartitionSpec as P

HD = 64
NB = 32
GX = 32
STEP = 5

NORM_EPSILON = 1e-06
SCORE_SCALE = 0.0625
BETA_ONE = 0.5
BETA_TWO = 0.5
ADAM_EPSILON = 1e-08
MATRIX_RATE = 0.03
VECTOR_RATE = 0.2
WEIGHT_DECAY = 0.01

BF = jnp.bfloat16
F32 = jnp.float32
NX = 128
NY = 256
MASKED = -1e30
FLOPS = 1.15e9
HIGH = lax.Precision.HIGHEST


def dot(a, b, precision=None):
    return lax.dot_general(
        a, b, (((1,), (0,)), ((), ())), preferred_element_type=F32, precision=precision
    )


def dot_nt(a, b, precision=None):
    return lax.dot_general(
        a, b, (((1,), (1,)), ((), ())), preferred_element_type=F32, precision=precision
    )


def dot_tn(a, b):
    return lax.dot_general(a, b, (((0,), (0,)), ((), ())), preferred_element_type=F32)


def iota(shape, axis):
    return lax.broadcasted_iota(jnp.int32, shape, axis)


def call(body, ins, outs, scratch=(), spaces=None, behind=(), cost=3.0, load=(), store=(), place=(), early=False):
    spaces = dict(spaces or {})
    spaces.update({n: pltpu.HBM for n in load})
    specs = [
        pl.BlockSpec(memory_space=spaces.get(n, pltpu.VMEM if n else pltpu.SMEM))
        for n in range(len(ins))
    ]
    specs += [pl.BlockSpec(memory_space=pl.ANY)] * len(behind)
    out_specs = [
        pl.BlockSpec(memory_space=pltpu.HBM if n in store or n in place else pltpu.VMEM)
        for n in range(len(outs))
    ]
    moved = [ins[n] for n in load] + [outs[n] for n in store]
    staging = [pltpu.VMEM(x.shape, x.dtype) for x in moved]
    if moved:
        staging.append(pltpu.SemaphoreType.DMA((len(moved),)))
    count, own = len(ins), len(scratch)

    def staged(*refs):
        given, refs = list(refs[:count]), refs[count + len(behind):]
        made, refs = list(refs[:len(outs)]), refs[len(outs):]
        used, buffers = refs[:own], refs[own:]
        copies = []
        for n, at in enumerate(load):
            copies.append(pltpu.make_async_copy(given[at], buffers[n], buffers[-1].at[n]))
            given[at] = buffers[n]
        for item in copies:
            item.start()
        for item in copies:
            item.wait()
        copies = []
        for n, at in enumerate(store, len(load)):
            copies.append(pltpu.make_async_copy(buffers[n], made[at], buffers[-1].at[n]))
            made[at] = buffers[n]

        def flush():
            for item in copies:
                item.start()

        body(*([flush] if early else []), *given, *made, *used)
        if not early:
            flush()
        for item in copies:
            item.wait()

    ins = list(ins)
    for n, space in spaces.items():
        if space is pltpu.HBM:
            ins[n] = pltpu.with_memory_space_constraint(ins[n], pltpu.HBM)
    made_at = [
        pltpu.HBM(x.shape, x.dtype) if n in store or n in place else x for n, x in enumerate(outs)
    ]
    return pl.pallas_call(
        staged,
        in_specs=specs,
        out_specs=out_specs,
        out_shape=made_at,
        scratch_shapes=list(scratch) + staging,
        compiler_params=pltpu.CompilerParams(vmem_limit_bytes=24 * 1024 * 1024),
        cost_estimate=pl.CostEstimate(
            flops=int(cost * FLOPS), bytes_accessed=0, transcendentals=0
        ),
    )(*ins, *behind)


def shape(dims, dtype):
    return jax.ShapeDtypeStruct(tuple(dims), dtype)


def swap(array, axis, mask):
    count = lax.axis_size(axis)
    return lax.ppermute(array, axis, [(i, i ^ mask) for i in range(count)])


def after(array, *others):
    return lax.optimization_barrier((array,) + others)[0]


def gather_xor(block):
    held = [block]
    while len(held) < lax.axis_size("dp"):
        held = held + [swap(x, "dp", len(held)) for x in held]
    return held


def entry_place(entry):
    return entry // 8 * 4 + (0, 2, 1, 3)[entry // 2 % 4]


def plus(left, right):
    return (left.astype(F32) + right.astype(F32)).astype(BF)


def scatter_near(even, came):
    if even.shape[0] == 4:
        return plus(even[:2], came[:2]), plus(even[2:], came[2:])
    sums = plus(even, came)
    while sums.shape[0] > 4:
        middle = sums.shape[0] // 2
        sums = plus(sums[:middle], swap(sums[middle:], "dp", 2 * middle))
    return sums[:2], sums[2:]


def adam_step(weight, moment, square, gradient, step_rate, decay_rate):
    new_moment = BETA_ONE * moment + (1.0 - BETA_ONE) * gradient
    new_square = BETA_TWO * square + (1.0 - BETA_TWO) * gradient * gradient
    moment_hat = new_moment / (1.0 - BETA_ONE**STEP)
    square_hat = new_square / (1.0 - BETA_TWO**STEP)
    new_weight = weight - step_rate * (
        moment_hat / (jnp.sqrt(square_hat) + ADAM_EPSILON) + decay_rate * weight
    )
    return (new_moment, new_square, new_weight)


SIDE, CORE, CHIP, COUNT, LENGTH, FIRST = 0, 1, 2, 3, 4, 5


def take_columns(src, sc, dst_store, blocks, width):
    if width % 128 == 0:
        for k in range(blocks):
            at = pl.multiple_of(sc[FIRST + k] * width, 128)
            dst_store(slice(k * width, (k + 1) * width), src[:, pl.ds(at, width)])
        return
    full = blocks * width
    rows = iota((full, full), 0)
    columns = iota((1, full), 1)
    wanted = jnp.zeros((1, full), jnp.int32)
    for k in range(blocks):
        here = (columns >= k * width) & (columns < (k + 1) * width)
        wanted = jnp.where(here, sc[FIRST + k] * width + columns - k * width, wanted)
    picks = (rows == wanted).astype(BF)
    dst_store(slice(0, full), dot(src[...], picks).astype(BF))


def prep_body(blocks, sc, own, q0, q1, q2, q3, cot, ids, margin, offs,
              x, inv, x_half, x_q, inv_q, gy, marks, raw, rawp):
    rows, width = own.shape[0], own.shape[1] // blocks
    half, quarter = rows // 2, rows // 4
    side, core, chip = sc[SIDE], sc[CORE], sc[CHIP]
    raw[pl.ds(pl.multiple_of(side * rows, rows), rows), :] = own[...]
    for ref, t, u in ((q0, 0, 0), (q1, 0, 1), (q2, 1, 0), (q3, 1, 1)):
        at = (1 - side) * rows + (core ^ t) * half + (chip ^ u) * quarter
        raw[pl.ds(pl.multiple_of(at, quarter), quarter), :] = ref[...]

    def keep(columns, value):
        rawp[:, columns] = value

    take_columns(raw, sc, keep, blocks, width)
    slot = iota((rows, 1), 0)
    patch_ok = (slot < sc[COUNT]).astype(F32)
    text_ok = (slot < sc[LENGTH]).astype(F32)
    patch = rawp[0:rows, :].astype(F32) * patch_ok
    hits = (margin[...] == iota((rows, rows), 1)).astype(BF)
    x[0:rows, :] = patch
    x[rows:, :] = text_ok * (rawp[rows:, :].astype(F32) + dot(hits, patch.astype(BF)))
    for part in range(4):
        at = slice(part * half, (part + 1) * half)
        value = x[at, :]
        inv[at, :] = lax.rsqrt(jnp.mean(value * value, axis=-1, keepdims=True) + NORM_EPSILON)
    start = pl.multiple_of(side * rows + core * half, half)
    x_half[...] = x[pl.ds(start, half), :]
    for s in range(2):
        at = pl.multiple_of((side ^ s) * rows + core * half + chip * quarter, quarter)
        x_q[s] = x[pl.ds(at, quarter), :]
        inv_q[s] = inv[pl.ds(at, quarter), :]

    def keep_low(columns, value):
        rawp[0:rows, columns] = value

    take_columns(cot, sc, keep_low, blocks, width)
    own_limit = jnp.where(side == 1, sc[LENGTH], sc[COUNT])
    for t in range(2):
        at = pl.multiple_of((core ^ t) * half, half)
        ok = (at + iota((half, 1), 0) < own_limit).astype(F32)
        gy[t * half:(t + 1) * half, :] = (rawp[pl.ds(at, half), :].astype(F32) * ok).astype(BF)
    n = ids[...]
    px, py = 4 * (n & (GX - 1)), 4 * (n >> 5)
    lane = iota((rows, 128), 1)
    both = jnp.where(lane == 0, px.astype(F32), jnp.where(lane == 1, py.astype(F32), 0.0))
    under = dot(hits, both.astype(BF))
    off = offs[...]
    cx = under[:, 0:1].astype(jnp.int32) + off[:, 0:1]
    cy = under[:, 1:2].astype(jnp.int32) + off[:, 1:2]
    marks[0:rows, 0:NX] = (iota((rows, NX), 1) == px + 2).astype(BF)
    marks[0:rows, NX:] = (iota((rows, NY), 1) == py + 2).astype(BF)
    marks[rows:, 0:NX] = (iota((rows, NX), 1) == cx).astype(BF)
    marks[rows:, NX:] = (iota((rows, NY), 1) == cy).astype(BF)


def table_places(width, along, named=None):
    lane = iota((NB, width), 1)
    ahead = jnp.where(lane < width // 2, lane, lane - width)
    if along:
        bucket = NB // 2 - 1 - (ahead >> 6)
    else:
        bucket = ((0 - ahead) >> 1) + NB // 2
    bucket = jnp.clip(bucket, 0, NB - 1)
    if named is None:
        named = iota((NB, width), 0)
    return (named == bucket).astype(F32)


def pack_body(weights, gains, tables, out):
    width = weights.shape[1]
    share = tables.shape[1]
    for n in range(4):
        out[n * width:(n + 1) * width, :] = weights[n].astype(BF)
    rest = jnp.zeros((out.shape[0] - 4 * width, out.shape[1]), F32)
    row = iota(rest.shape, 0)
    if width % 128 == 0:
        joined = jnp.concatenate([gains[0:1, :], gains[1:2, :]], axis=1)
        if joined.shape[1] < rest.shape[1]:
            blank = jnp.zeros((1, rest.shape[1] - joined.shape[1]), F32)
            joined = jnp.concatenate([joined, blank], axis=1)
        rest = jnp.where(row == 0, joined, rest)
    lane = iota(rest.shape, 1)
    for n in range(3):
        for t in range(share):
            for h in range(tables.shape[2]):
                here = (row == 1 + n * share + t) & (lane == h)
                rest = jnp.where(here, tables[n, t, h], rest)
    out[4 * width:, :] = rest.astype(BF)


def table_lines(blocks, sc, rest):
    share = NB // blocks
    found = []
    for n in range(3):
        lines = [
            rest[b, :, 0:128].astype(F32)[1 + n * share:1 + (n + 1) * share]
            for b in range(blocks)
        ]
        found.append(jnp.concatenate(lines, axis=0))
    row = iota((NB, 1), 0)
    named = jnp.zeros((NB, 1), jnp.int32)
    for b in range(blocks):
        here = (row >= b * share) & (row < (b + 1) * share)
        named = jnp.where(here, sc[FIRST + b] * share + row - b * share, named)
    return found, named


def attend_body(blocks, sc, *refs):
    x, inv, gains_in, marks = refs[:4]
    parts = refs[4:4 + blocks]
    (a, q, k, v, w_out, o, kept, sent, w3, wo, gains) = refs[4 + blocks:15 + blocks]
    (keys, bias, scores, feats, w, w_sems, rest, part_sems) = refs[15 + blocks:]
    rows2 = x.shape[0]
    rows = rows2 // 2
    half = rows // 2
    width = x.shape[1] // blocks
    cols = wo.shape[1]
    heads = cols // HD
    side, core = sc[SIDE], sc[CORE]
    copies = []
    for b in range(blocks):
        at = pl.ds(b * width, width)
        targets = [w3.at[at, pl.ds(n * cols, cols)] for n in range(3)] + [wo.at[at, :]]
        for n, dst in enumerate(targets):
            copies.append(pltpu.make_async_copy(
                parts[b].at[pl.ds(n * width, width), :], dst, part_sems.at[b, n]
            ))
        copies.append(pltpu.make_async_copy(
            parts[b].at[pl.ds(4 * width, 16), :], rest.at[b], part_sems.at[b, 4]
        ))
    for item in copies:
        item.start()
    keys[:, 128:] = marks[...]
    for item in copies:
        item.wait()
    if width % 128 == 0:
        for b in range(blocks):
            line = rest[b].astype(F32)
            at = slice(b * width, (b + 1) * width)
            gains[0:1, at] = line[0:1, :width]
            gains[1:2, at] = line[0:1, width:2 * width]
    else:
        gains[...] = gains_in[...]
    g1 = gains[0:1, :]
    for part in range(4):
        at = slice(part * half, (part + 1) * half)
        a[at, :] = (x[at, :] * inv[at, :] * g1).astype(BF)
        kv = dot(a[at, :], w3[:, cols:]).astype(BF)
        k[at, :] = kv[:, :cols]
        v[at, :] = kv[:, cols:]
    starts = []
    for t in range(2):
        start = pl.multiple_of(side * rows + (core ^ t) * half, half)
        starts.append(start)
        q[t * half:(t + 1) * half, :] = dot(a[pl.ds(start, half), :], w3[:, :cols]).astype(BF)
    tables, named = table_lines(blocks, sc, rest)
    base0 = dot_tn(tables[0].astype(BF), table_places(2 * rows2, True, named).astype(BF))
    base1 = dot_tn(tables[1].astype(BF), table_places(2 * NX, False, named).astype(BF))
    base2 = dot_tn(tables[2].astype(BF), table_places(2 * NY, False, named).astype(BF))
    key = iota((1, rows2), 1)
    limit = jnp.where(key < rows, sc[COUNT], rows + sc[LENGTH])
    mask = jnp.where(key < limit, 0.0, MASKED)
    band = rows // (NB // 4)
    low_lanes = iota((1, 128), 1) < HD
    triangle = iota((band, rows2), 0) >= (iota((band, rows2), 1) & (band - 1))
    for h in range(heads):
        pair = slice((h // 2) * 128, (h // 2) * 128 + 128)
        mine = low_lanes if h % 2 == 0 else ~low_lanes
        if h % 2 == 0:
            keys[:, 0:128] = k[:, pair]
        for r in range(2 * rows2 // rows * 4 + 1):
            shifted = pltpu.roll(base0[h:h + 1, :], r * band, 1) if r else base0[h:h + 1, :]
            bias[r:r + 1, :] = shifted[:, :rows2] + mask
        t1 = pltpu.roll(
            jnp.broadcast_to(base1[h:h + 1, :], (NX, 2 * NX)), 0, 1, stride=1, stride_axis=0
        )[:, :NX].astype(BF)
        t2 = pltpu.roll(
            jnp.broadcast_to(base2[h:h + 1, :], (NY, 2 * NY)), 0, 1, stride=1, stride_axis=0
        )[:, :NY].astype(BF)
        for t in range(2):
            at = slice(t * half, (t + 1) * half)
            mq = marks[pl.ds(starts[t], half), :]
            feats[:, 0:128] = jnp.where(mine, q[at, pair].astype(F32) * SCORE_SCALE, 0.0).astype(BF)
            feats[:, 128:128 + NX] = dot(mq[:, :NX], t1).astype(BF)
            feats[:, 128 + NX:] = dot(mq[:, NX:], t2).astype(BF)
            scores[...] = dot_nt(feats[...], keys[...])
            first = (side * rows + (core ^ t) * half) // band
            for sb in range(half // band):
                z = scores[sb * band:(sb + 1) * band, :]
                z = z + jnp.where(
                    triangle, bias[pl.ds(first + sb + 1, 1), :], bias[pl.ds(first + sb, 1), :]
                )
                e = jnp.exp(z - jnp.max(z, axis=-1, keepdims=True))
                e = e * (1.0 / jnp.sum(e, axis=-1, keepdims=True))
                w[h, t * half + sb * band:t * half + (sb + 1) * band, :] = e.astype(BF)
            mixed = dot(w[h, at, :], v[:, pair])
            if h % 2 == 0:
                o[at, pair] = mixed.astype(BF)
            else:
                o[at, pair] = jnp.where(mine, mixed.astype(BF), o[at, pair])
        pltpu.make_async_copy(w.at[h], w_out.at[h], w_sems.at[h]).start()
    kept[...] = dot_nt(o[0:half, :], wo[...]).astype(BF)
    sent[...] = dot_nt(o[half:, :], wo[...]).astype(BF)
    for h in range(heads):
        pltpu.make_async_copy(w.at[h], w_out.at[h], w_sems.at[h]).wait()


def enter_body(sc, x_half, s_own, s_far, gains, h1, inv2, c):
    value = x_half[...] + (s_own[...].astype(F32) + s_far[...].astype(F32))
    h1[...] = value
    inverse = lax.rsqrt(jnp.mean(value * value, axis=-1, keepdims=True) + NORM_EPSILON)
    inv2[...] = inverse
    c[...] = (value * inverse * gains[1:2, :]).astype(BF)


GELU_A = 0.7978845608028654
GELU_B = 0.044715


def hidden_copies(sc, hid, targets, sems):
    blocks, width = hid.shape[0], hid.shape[3]
    copies = []
    for n, dst in enumerate(targets):
        copies.append([])
        for b in range(blocks):
            row = sc[FIRST + blocks + b] if blocks > 1 else 0
            copies[n].append(pltpu.make_async_copy(
                hid.at[row, n], dst.at[:, pl.ds(b * width, width)], sems.at[n, b]
            ))
    return copies


def feed_body(sc, c_own, c_far, gy_in, hid, f, dgate, dup, kept, sent, wd,
              wg, wu, sems, c, gy, in_sems):
    half = c_own.shape[0]
    entering = [
        pltpu.make_async_copy(src, dst, in_sems.at[n])
        for n, (src, dst) in enumerate((
            (c_own, c.at[pl.ds(0, half)]), (c_far, c.at[pl.ds(half, half)]), (gy_in, gy)
        ))
    ]
    for item in entering:
        item.start()
    copies = hidden_copies(sc, hid, (wg, wu, wd), sems)
    for group in copies:
        for item in group:
            item.start()
    for item in entering:
        item.wait()
    for t, out in ((0, kept), (1, sent)):
        at = slice(t * half, (t + 1) * half)

        def ready(n):
            for item in copies[n] if t == 0 else ():
                item.wait()

        ready(0)
        gate = dot_nt(c[at, :], wg[...])
        ready(1)
        up = dot_nt(c[at, :], wu[...])
        ready(2)
        df = dot_nt(gy[at, :], wd[...]).astype(BF).astype(F32)
        inner = jnp.tanh(GELU_A * (gate + GELU_B * gate * gate * gate))
        gelu = 0.5 * gate * (1.0 + inner)
        slope = 0.5 * (1.0 + inner) + 0.5 * gate * (1.0 - inner * inner) * (
            GELU_A * (1.0 + 3.0 * GELU_B * gate * gate)
        )
        f[at, :] = (gelu * up).astype(BF)
        dgate[at, :] = (df * up * slope).astype(BF)
        dup[at, :] = (df * gelu).astype(BF)
        out[...] = (dot(dgate[at, :], wg[...]) + dot(dup[at, :], wu[...])).astype(BF)


def down_body(blocks, sc, c_own, c_far, gy, wd, f, dgate, dup, kept, sent, *refs):
    grads, c = refs[:-1], refs[-1]
    half = c_own.shape[0]
    width = c_own.shape[1] // blocks
    c[0:half, :] = c_own[...]
    c[half:, :] = c_far[...]
    for n, (left, right) in enumerate(((dgate, c), (dup, c), (f, gy))):
        product = dot_tn(left[...], right[...]).astype(BF)
        if len(grads) == 3:
            grads[n][...] = product
            continue
        for b in range(blocks):
            bit, place = (b & 1, entry_place(b)) if n else (b >> 1 & 1, (b & 1) + 2 * (b >> 2))
            grads[2 * n + bit][place] = product[:, b * width:(b + 1) * width]
    kept[...] = dot(f[0:half, :], wd[...]).astype(BF)
    sent[...] = dot(f[half:, :], wd[...]).astype(BF)


def norm_back(value, inverse, gain, grad):
    weighted = grad * gain
    inner = jnp.mean(weighted * value, axis=-1, keepdims=True)
    return inverse * weighted - value * (inverse * inverse * inverse * inner)


def turn_body(sc, s_own, s_far, h1, inv2, gains, gy, dh1_q, gal, dg2):
    half = h1.shape[0]
    quarter = half // 2
    dc = s_own[...].astype(F32) + s_far[...].astype(F32)
    value, inverse = h1[...], inv2[...]
    dh1 = gy[0:half, :].astype(F32) + norm_back(value, inverse, gains[1:2, :], dc)
    gal[...] = dh1.astype(BF)
    pick = sc[CHIP] == 0
    dh1_q[...] = jnp.where(pick, dh1[:quarter], dh1[quarter:])
    terms = dc * (value * inverse)
    mine = jnp.where(pick, terms[:quarter], terms[quarter:])
    dg2[...] = jnp.sum(mine, axis=0, keepdims=True)


def attend_back_body(flush, sc, gal0, gal1, w3, wo, q, k, v, w, marks, x, inv,
                     dq, dk, dv, keep, send, dg1, m1, m2, low_sums, all_sums,
                     dol, dkt, dvt, keys, dsl, picked):
    half = gal0.shape[0]
    rows = 2 * half
    rows2 = x.shape[0]
    cols = wo.shape[1]
    heads = cols // HD
    side, core, chip = sc[SIDE], sc[CORE], sc[CHIP]
    dol[0:half, :] = dot(gal0[...], wo[...]).astype(BF)
    dol[half:, :] = dot(gal1[...], wo[...]).astype(BF)
    band = rows // (NB // 4)
    keys[:, 128:] = marks[...]
    low_lanes = iota((1, 128), 1) < HD
    triangle = iota((band, rows2), 0) >= (iota((band, rows2), 1) & (band - 1))
    for h in range(heads):
        pair = slice((h // 2) * 128, (h // 2) * 128 + 128)
        mine = low_lanes if h % 2 == 0 else ~low_lanes
        if h % 2 == 0:
            keys[:, 0:128] = k[:, pair]
        for t in range(2):
            at = slice(t * half, (t + 1) * half)
            dol_h = jnp.where(mine, dol[at, pair], jnp.zeros((), BF))
            q_h = jnp.where(mine, q[at, pair], jnp.zeros((), BF))
            dw = dot_nt(dol_h, v[:, pair])
            for sb in range(half // band):
                rs = slice(sb * band, (sb + 1) * band)
                here = w[h, t * half + sb * band:t * half + (sb + 1) * band, :].astype(F32)
                part = here * dw[rs, :]
                ds = part - here * jnp.sum(part, axis=-1, keepdims=True)
                place = t * (half // band) + sb
                all_sums[h, place:place + 1, :] = jnp.sum(ds, axis=0, keepdims=True)
                low_sums[h, place:place + 1, :] = jnp.sum(
                    jnp.where(triangle, ds, 0.0), axis=0, keepdims=True
                )
                dsl[rs, :] = (ds * SCORE_SCALE).astype(BF)
            dvt_part = dot_tn(dol_h, w[h, at, :])
            dkt_part = dot_tn(q_h, dsl[...])
            if h % 2 == 0 and t == 0:
                dvt[...] = dvt_part
                dkt[...] = dkt_part
            else:
                dvt[...] += dvt_part
                dkt[...] += dkt_part
            out = dot(dsl[...], keys[...])
            if h % 2 == 0:
                dq[at, pair] = out[:, 0:128].astype(BF)
            else:
                dq[at, pair] = jnp.where(mine, out[:, 0:128].astype(BF), dq[at, pair])
            picked[at, :] = out[:, 128:]
        if h % 2 == 1:
            dv[:, pair] = dvt[...].T.astype(BF)
            dk[:, pair] = dkt[...].T.astype(BF)
        first = picked[...]
        upper = first.astype(BF)
        lower = (first - upper.astype(F32)).astype(BF)
        total1 = jnp.zeros((NX, NX), F32)
        total2 = jnp.zeros((NY, NY), F32)
        for t in range(2):
            at = slice(t * half, (t + 1) * half)
            mq = marks[pl.ds(pl.multiple_of(side * rows + (core ^ t) * half, half), half), :]
            for value in (upper, lower):
                total1 = total1 + dot_tn(mq[:, :NX], value[at, :NX])
                total2 = total2 + dot_tn(mq[:, NX:], value[at, NX:])
        m1[h] = total1
        m2[h] = total2
    flush()
    quarter = half // 2
    gain_sum = jnp.zeros((1, x.shape[1]), F32)
    for s in range(2):
        for t in range(2):
            for u in range(2):
                start = (side ^ s) * rows + (core ^ t) * half + (chip ^ u) * quarter
                at = pl.ds(pl.multiple_of(start, quarter), quarter)
                da = dot_nt(dk[at, :], w3[:, cols:2 * cols]) + dot_nt(dv[at, :], w3[:, 2 * cols:])
                if s == 0:
                    mine_q = pl.ds(pl.multiple_of(t * half + (chip ^ u) * quarter, quarter), quarter)
                    da = da + dot_nt(dq[mine_q, :], w3[:, :cols])
                low = da.astype(BF)
                if t == 0:
                    keep[u, s] = low
                else:
                    send[u, s] = low
                gain_sum = gain_sum + jnp.sum(da * (x[at, :] * inv[at, :]), axis=0, keepdims=True)
    dg1[...] = gain_sum


def tables_body(heads, rows2, sc, m1, m2, low_sums, all_sums, out):
    rows = rows2 // 2
    half = rows // 2
    band = rows // (NB // 4)
    side, core = sc[SIDE], sc[CORE]
    scale = 1.0 / SCORE_SCALE
    line = jnp.zeros((heads, 2 * rows2), F32)
    blank = jnp.zeros((heads, rows2), F32)
    for t in range(2):
        for sb in range(half // band):
            place = t * (half // band) + sb
            row = (side * rows + (core ^ t) * half) // band + sb
            low = low_sums[:, place, :]
            high = all_sums[:, place, :] - low
            back = 2 * rows2 - row * band
            line = line + pltpu.roll(jnp.concatenate([high, blank], axis=1), back, 1)
            line = line + pltpu.roll(jnp.concatenate([low, blank], axis=1), back - band, 1)
    sums0 = [line]
    sums1 = [diagonals(m1[h], NX) * scale for h in range(heads)]
    sums2 = [diagonals(m2[h], NY) * scale for h in range(heads)]
    for n, (sums, places) in enumerate((
        (sums0, table_places(2 * rows2, True)),
        (sums1, table_places(2 * NX, False)),
        (sums2, table_places(2 * NY, False)),
    )):
        out[n * heads:(n + 1) * heads, :] = dot_nt(jnp.concatenate(sums, axis=0), places, HIGH)


def diagonals(square, size):
    mirror = (iota((size, size), 0) + iota((size, size), 1) == size - 1).astype(F32)
    flipped = dot(mirror, square, HIGH)
    wide = jnp.concatenate([flipped, jnp.zeros((size, size), F32)], axis=1)
    turned = pltpu.roll(wide, 0, 1, stride=1, stride_axis=0)
    return pltpu.roll(jnp.sum(turned, axis=0, keepdims=True), size + 1, 1)


def weights_body(blocks, sc, a, q_grad, k_grad, v_grad, gal0, gal1, o, dg1, dg2, tables, even, odd,
                 joined, gal, own):
    outs = [(odd if b % 2 else even).at[entry_place(b)] for b in range(blocks)]
    rows2 = a.shape[0]
    rows = rows2 // 2
    half = rows // 2
    width = a.shape[1] // blocks
    cols = o.shape[1]
    joined[:, 0:cols] = k_grad[...]
    joined[:, cols:] = v_grad[...]
    gal[0:half, :] = gal0[...]
    gal[half:, :] = gal1[...]
    for t in range(2):
        start = pl.multiple_of(sc[SIDE] * rows + (sc[CORE] ^ t) * half, half)
        own[t * half:(t + 1) * half, :] = a[pl.ds(start, half), :]
    count, buckets = tables.shape
    table_rest = jnp.concatenate([
        jnp.zeros((1, cols), F32),
        jnp.concatenate([tables[...], jnp.zeros((count, cols - buckets), F32)], axis=1),
        jnp.zeros((15 - count, cols), F32),
    ], axis=0)
    first_row = iota((16, 1), 0) == 0
    for b in range(blocks):
        at = slice(b * width, (b + 1) * width)
        kv = dot_tn(a[:, at], joined[...]).astype(BF)
        outs[b][0:width, :] = dot_tn(own[:, at], q_grad[...]).astype(BF)
        outs[b][width:2 * width, :] = kv[:, :cols]
        outs[b][2 * width:3 * width, :] = kv[:, cols:]
        outs[b][3 * width:4 * width, :] = dot_tn(gal[:, at], o[...]).astype(BF)
        line = jnp.concatenate([dg1[:, at], dg2[:, at]], axis=1)
        if 2 * width < cols:
            line = jnp.concatenate([line, jnp.zeros((1, cols - 2 * width), F32)], axis=1)
        outs[b][4 * width:, :] = jnp.where(first_row, line, table_rest).astype(BF)


def halves_swapped(value):
    middle = value.shape[1] // 2
    return jnp.concatenate([value[:, middle:], value[:, :middle]], axis=1).astype(F32)


def share_body(sc, keep, came, came_x, dh1, x_q, inv_q, gains, own, out):
    g1 = gains[0:1, :]
    for s in range(2):
        da = keep[0, s].astype(F32) + came[0, s].astype(F32) + came_x[s].astype(F32)
        dx = norm_back(x_q[s], inv_q[s], g1, da)
        if s == 0:
            dx = dx + dh1[...]
            own[...] = dx
        out[s] = dx.astype(BF)


def leave_body(sc, own, parts, came, out):
    quarter = own.shape[0]
    side, core, chip = sc[SIDE], sc[CORE], sc[CHIP]
    slot = core * 2 * quarter + chip * quarter + iota((quarter, 1), 0)
    own_limit = jnp.where(side == 1, sc[LENGTH], sc[COUNT])
    dx = own[...] + halves_swapped(came[1])
    out[0] = (dx * (slot < own_limit).astype(F32)).astype(BF)
    dx = parts[1].astype(F32) + halves_swapped(came[0])
    out[1] = (dx * (slot < sc[LENGTH]).astype(F32)).astype(BF)


def put_columns(src, sc, dst, blocks, width):
    if width % 128 == 0:
        for k in range(blocks):
            at = pl.multiple_of(sc[FIRST + k] * width, 128)
            dst[:, pl.ds(at, width)] = src[:, k * width:(k + 1) * width].astype(dst.dtype)
        return
    full = blocks * width
    columns = iota((full, full), 1)
    rows = iota((full, 1), 0)
    wanted = jnp.zeros((full, 1), jnp.int32)
    for k in range(blocks):
        here = (rows >= k * width) & (rows < (k + 1) * width)
        wanted = jnp.where(here, sc[FIRST + k] * width + rows - k * width, wanted)
    picks = (columns == wanted).astype(F32)
    dst[...] = dot(src[...].astype(F32), picks, HIGH).astype(dst.dtype)


def token_body(blocks, sc, p0, p1, p2, p3, margin, out, own, text, total):
    rows = own.shape[0]
    half, quarter = rows // 2, rows // 4
    width = own.shape[1] // blocks
    side, core, chip = sc[SIDE], sc[CORE], sc[CHIP]
    for ref, t, u in ((p0, 0, 0), (p1, 0, 1), (p2, 1, 0), (p3, 1, 1)):
        at = pl.ds(pl.multiple_of((core ^ t) * half + (chip ^ u) * quarter, quarter), quarter)
        own[at, :] = ref[0]
        text[at, :] = ref[1]

    @pl.when(side == 1)
    def _():
        total[...] = own[...].astype(F32)

    @pl.when(side == 0)
    def _():
        hits = (margin[...] == iota((rows, rows), 1)).astype(BF)
        ok = (iota((rows, 1), 0) < sc[COUNT]).astype(F32)
        total[...] = own[...].astype(F32) + ok * dot_tn(hits, text[...])

    put_columns(total, sc, out, blocks, width)


def output_body(blocks, sc, y_own, y_far, out, whole):
    half = y_own.shape[0]
    core = sc[CORE]
    whole[pl.ds(pl.multiple_of(core * half, half), half), :] = y_own[...]
    whole[pl.ds(pl.multiple_of((1 - core) * half, half), half), :] = y_far[...]
    put_columns(whole, sc, out, blocks, y_own.shape[1] // blocks)


def attention_adam_body(sc, kept, came, last, *refs):
    matrices, tables = refs[0:3], refs[3:6]
    matrix_out, table_out = refs[6:10], refs[10:14]
    total = kept[0].astype(F32) + came[0].astype(F32) + last[...].astype(F32)

    def step(ins, outs, at, value, rate, decay):
        outs[0][at] = value
        new = adam_step(ins[0][at], ins[1][at], ins[2][at], value, rate, decay)
        for out, result in zip(outs[1:], new):
            out[at] = result

    number, width = matrices[0].shape[0], matrices[0].shape[1]
    for n in range(number):
        value = total[n * width:(n + 1) * width, :]
        step(matrices, matrix_out, n, value, MATRIX_RATE, WEIGHT_DECAY)
    small = total[number * width:, :]
    share, heads = tables[0].shape[1], tables[0].shape[2]
    wanted = (
        iota((share, NB), 1) == sc[FIRST] * share + iota((share, NB), 0)
    ).astype(F32)
    for n in range(3):
        lines = small[1 + n * heads:1 + (n + 1) * heads, 0:NB]
        step(tables, table_out, n, dot_nt(wanted, lines, HIGH), VECTOR_RATE, 0.0)


def hidden_adam_body(counts, sc, *refs):
    terms, refs = refs[:sum(counts)], refs[sum(counts):]
    matrices, outs = refs[:3], refs[3:]
    for n, count in enumerate(counts):
        total = jnp.zeros(matrices[0].shape[1:], F32)
        for term in terms[sum(counts[:n]):sum(counts[:n + 1])]:
            total = total + (term[0] if len(term.shape) == 3 else term[...]).astype(F32)
        outs[0][n] = total
        new = adam_step(
            matrices[0][n], matrices[1][n], matrices[2][n], total, MATRIX_RATE, WEIGHT_DECAY
        )
        for out, result in zip(outs[1:], new):
            out[n] = result


def bind(body, *first):
    def bound(*refs):
        return body(*first, *refs)

    return bound


def local(
    tokens,
    cotangent,
    patch_counts,
    patch_ids,
    text_lengths,
    margin,
    box_offsets,
    owners,
    attention_weights,
    attention_first,
    attention_second,
    hidden_weights,
    hidden_first,
    hidden_second,
    norm_gains,
    gain_first,
    gain_second,
    bias_tables,
    table_first,
    table_second,
):
    blocks = lax.axis_size("dp")
    half_way = blocks // 2
    me = lax.axis_index("dp")
    mp = lax.axis_index("mp")
    page = me % half_way
    side = me // half_way
    core, chip = mp % 2, mp // 2
    rows, features = tokens.shape
    half, quarter = rows // 2, rows // 4
    width = features // blocks
    cols = attention_weights.shape[2]
    heads = cols // HD
    hidden = hidden_weights.shape[2]
    share = NB // blocks
    wide = width % 128 == 0

    mine = lax.dynamic_slice_in_dim(tokens, core * half + chip * quarter, quarter, 0)
    packed = call(
        pack_body,
        [attention_weights, norm_gains, bias_tables],
        [shape((4 * width + 16, cols), BF)],
        spaces={0: pltpu.VMEM, 2: pltpu.SMEM},
        behind=[mine],
        cost=2.0,
    )[0]
    turned = jnp.transpose(hidden_weights, (0, 2, 1)).astype(BF)
    eight = blocks == 8
    direct = eight and wide
    q0 = swap(mine, "dp", half_way)
    q1 = swap(q0, "mp", 2)
    q2 = swap(q0, "mp", 1)
    q3 = swap(q1, "mp", 1)
    if eight:
        near, far, opposite = [lambda v, m=m: swap(v, "dp", m) for m in (1, 2, 4)]
        ga = {0: packed}
        ga[4], ga[2], ga[1] = opposite(packed), far(packed), near(packed)
        ga[3] = near(after(ga[2], ga[1]))
        held = after(ga[4], q0, ga[2])
        ga[6], ga[5] = far(held), near(held)
        ga[7] = near(after(ga[6], ga[3], q2, q3))
        gathered = [ga[k] for k in range(8)]
    else:
        gathered = gather_xor(packed)

    order = jnp.arange(blocks, dtype=jnp.int32)
    place_of = jnp.sum(
        jnp.where(owners[None, :] == order[:, None], order[None, :], 0), axis=1
    )
    owner_k = me ^ order
    place_k = jnp.sum(
        jnp.where(owner_k[:, None] == order[None, :], place_of[None, :], 0), axis=1
    )
    counts = lax.dynamic_index_in_dim(patch_counts, page, 0, True)
    lengths = lax.dynamic_index_in_dim(text_lengths, page, 0, True)
    scalars = jnp.concatenate([
        jnp.stack([side, core, chip]).astype(jnp.int32), counts, lengths, place_k, owner_k
    ]).astype(jnp.int32)
    ids_column = lax.dynamic_index_in_dim(patch_ids, page, 0, False)[:, None]
    margin_column = lax.dynamic_index_in_dim(margin, page, 0, False)[:, None]
    offsets = lax.dynamic_index_in_dim(box_offsets, page, 0, False)

    x, inv, x_half, x_q, inv_q, gy, marks = call(
        bind(prep_body, blocks),
        [scalars, tokens, q0, q1, q2, q3, cotangent, ids_column, margin_column, offsets],
        [
            shape((2 * rows, features), F32),
            shape((2 * rows, 1), F32),
            shape((half, features), F32),
            shape((2, quarter, features), F32),
            shape((2, quarter, 1), F32),
            shape((rows, features), BF),
            shape((2 * rows, NX + NY), BF),
        ],
        [pltpu.VMEM((2 * rows, features), BF), pltpu.VMEM((2 * rows, features), BF)],
        load=(1, 2, 3, 4, 5, 6),
        cost=8.0,
    )

    if wide:
        gains_in = jnp.zeros((2, features), F32)
    else:
        gains_in = jnp.stack(gather_xor(norm_gains.astype(BF)), axis=1)
        gains_in = gains_in.reshape(2, features).astype(F32)

    hid = lax.all_gather(after(turned, q0), "dp", axis=0)
    if not wide:
        hid = jnp.transpose(jnp.take(hid, owner_k, axis=0), (1, 2, 0, 3))
        hid = hid.reshape(1, 3, hidden, features)

    a, q, k, v, w, o, kept, sent, w3, wo, gains = call(
        bind(attend_body, blocks),
        [scalars, x, inv, gains_in, marks] + gathered,
        [
            shape((2 * rows, features), BF),
            shape((rows, cols), BF),
            shape((2 * rows, cols), BF),
            shape((2 * rows, cols), BF),
            shape((heads, rows, 2 * rows), BF),
            shape((rows, cols), BF),
            shape((half, features), BF),
            shape((half, features), BF),
            shape((features, 3 * cols), BF),
            shape((features, cols), BF),
            shape((2, features), F32),
        ],
        [
            pltpu.VMEM((2 * rows, 128 + NX + NY), BF),
            pltpu.VMEM((24, 2 * rows), F32),
            pltpu.VMEM((half, 2 * rows), F32),
            pltpu.VMEM((half, 128 + NX + NY), BF),
            pltpu.VMEM((heads, rows, 2 * rows), BF),
            pltpu.SemaphoreType.DMA((heads,)),
            pltpu.VMEM((blocks, 16, cols), BF),
            pltpu.SemaphoreType.DMA((blocks, 5)),
        ],
        place={4},
        spaces={n: pltpu.HBM for n in range(5, 5 + blocks)},
        cost=16.0,
    )

    def mp_sum(kept_rows, sent_rows):
        came = swap(sent_rows, "mp", 1)
        chip_sum = (kept_rows.astype(F32) + came.astype(F32)).astype(BF)
        return chip_sum, swap(chip_sum, "mp", 2)

    s_own, s_far = mp_sum(kept, sent)
    h1, inv2, c_own = call(
        enter_body,
        [scalars, x_half, s_own, s_far, gains],
        [shape((half, features), F32), shape((half, 1), F32), shape((half, features), BF)],
        store=(2,),
    )
    c_far = swap(c_own, "mp", 1)

    f, dgate, dup, kept, sent, wd = call(
        feed_body,
        [scalars, c_own, c_far, gy, hid],
        [shape((rows, hidden), BF)] * 3
        + [shape((half, features), BF)] * 2
        + [shape((hidden, features), BF)],
        [pltpu.VMEM((hidden, features), BF)] * 2
        + [pltpu.SemaphoreType.DMA((3, hid.shape[0]))]
        + [pltpu.VMEM((rows, features), BF)] * 2
        + [pltpu.SemaphoreType.DMA((3,))],
        spaces={n: pltpu.HBM for n in (1, 2, 3, 4)},
        cost=10.0,
    )
    s_own, s_far = mp_sum(kept, sent)
    y_kept, y_sent, *hidden_grads = call(
        bind(down_body, blocks),
        [scalars, c_own, c_far, gy, wd, f, dgate, dup],
        [shape((half, features), BF)] * 2
        + (
            [shape((blocks // 2, hidden, width), BF)] * 6 if direct
            else [shape((hidden, features), BF)] * 3
        ),
        [pltpu.VMEM((rows, features), BF)],
        behind=[s_own],
        load=(1, 2, 3),
        cost=8.5,
    )
    if direct:
        stay0, go0, even1, odd1, even2, odd2 = hidden_grads
        far0 = swap(go0, "dp", 2)
        near1, near2 = swap(odd1, "dp", 1), swap(odd2, "dp", 1)
    else:
        whole = jnp.stack(hidden_grads).reshape(3, hidden, blocks, width)
        whole = jnp.take(jnp.transpose(whole, (2, 0, 1, 3)), owner_k, axis=0)
        hidden_sum = lax.psum_scatter(whole, "dp", scatter_dimension=0)
        hidden_terms = [[hidden_sum[n]] for n in range(3)]

    dh1_q, gal_own, dg2 = call(
        turn_body,
        [scalars, s_own, s_far, h1, inv2, gains, gy],
        [
            shape((quarter, features), F32),
            shape((half, features), BF),
            shape((1, features), F32),
        ],
        behind=[hidden_grads[1]],
        cost=0.0,
    )
    gal_far = swap(gal_own, "mp", 1)
    y_own, y_far = mp_sum(y_kept, y_sent)

    dq, dk, dv, keep, send, dg1, m1, m2, low_sums, all_sums = call(
        attend_back_body,
        [scalars, gal_own, gal_far, w3, wo, q, k, v, w, marks, x, inv],
        [
            shape((rows, cols), BF),
            shape((2 * rows, cols), BF),
            shape((2 * rows, cols), BF),
            shape((2, 2, quarter, features), BF),
            shape((2, 2, quarter, features), BF),
            shape((1, features), F32),
            shape((heads, NX, NX), F32),
            shape((heads, NY, NY), F32),
            shape((heads, NB // 4, 2 * rows), F32),
            shape((heads, NB // 4, 2 * rows), F32),
        ],
        [
            pltpu.VMEM((rows, cols), BF),
            pltpu.VMEM((128, 2 * rows), F32),
            pltpu.VMEM((128, 2 * rows), F32),
            pltpu.VMEM((2 * rows, 128 + NX + NY), BF),
            pltpu.VMEM((half, 2 * rows), BF),
            pltpu.VMEM((rows, NX + NY), F32),
        ],
        store=(0, 1, 2, 6, 7, 8, 9),
        early=True,
        behind=[y_own],
        cost=0.0,
    )
    came = swap(after(send, y_far, *([far0, near1] if direct else [])), "mp", 1)
    to_chip = (keep[1].astype(F32) + came[1].astype(F32)).astype(BF)
    came_x = swap(to_chip, "mp", 2)

    own_limit = jnp.where(side == 1, lengths, counts)
    slots = core * half + jnp.arange(half, dtype=jnp.int32)
    y_low = (
        (slots < own_limit).astype(F32)[:, None]
        * (h1 + (y_own.astype(F32) + y_far.astype(F32)))
    ).astype(BF)
    y_other = swap(y_low, "mp", 1)

    early, middle, late = [], [], []
    if direct:
        keep0, send0 = scatter_near(stay0, after(far0, to_chip))
        far0 = swap(send0, "dp", 4)
        keep1, send1 = scatter_near(even1, after(near1, to_chip))
        far1 = swap(send1, "dp", 2)
        early = [send0, send1]
    table_part = call(
        bind(tables_body, heads, 2 * rows),
        [scalars, m1, m2, low_sums, all_sums],
        [shape((3 * heads, NB), F32)],
        load=(1, 2, 3, 4),
        behind=[to_chip] + early,
        cost=0.0,
    )[0]
    even, odd = call(
        bind(weights_body, blocks),
        [scalars, a, dq, dk, dv, gal_own, gal_far, o, dg1, dg2, table_part],
        [shape((blocks // 2, 4 * width + 16, cols), BF)] * 2,
        [
            pltpu.VMEM((2 * rows, 2 * cols), BF),
            pltpu.VMEM((rows, features), BF),
            pltpu.VMEM((rows, features), BF),
        ],
        behind=[to_chip],
        load=(1, 2, 3, 4, 7, 8),
        cost=0.0,
    )

    if direct:
        last1 = plus(keep1[1], far1[1])
        end1 = swap(last1, "dp", 4)
        last0 = plus(keep0[1], far0[1])
        end0 = swap(last0, "dp", 1)
        middle = [near2, far0]

    own_part, dx_parts = call(
        share_body,
        [scalars, keep, came, came_x, dh1_q, x_q, inv_q, gains],
        [shape((quarter, features), F32), shape((2, quarter, features), BF)],
        cost=0.0,
    )
    dx_came = swap(after(dx_parts, *middle), "dp", half_way)
    if direct:
        keep2, send2 = scatter_near(even2, after(near2, dx_parts))
        far2 = swap(send2, "dp", 2)
        last2 = plus(keep2[1], far2[1])
        end2 = swap(last2, "dp", 4)
        late = [far2, end0]
        hidden_terms = [[keep0, far0, end0], [keep1, far1, end1], [keep2, far2, end2]]
    near_came = swap(after(odd, dx_parts, *middle[:2]), "dp", 1)
    pair_kept, pair_sent = scatter_near(even, near_came)
    pair_came = swap(pair_sent, "dp", 2)
    last = plus(pair_kept[1], pair_came[1])
    layer_output = call(
        bind(output_body, blocks),
        [scalars, y_low, y_other],
        [shape((rows, features), BF)],
        [pltpu.VMEM((rows, features), BF)],
        cost=0.0,
    )[0]
    pieces = call(
        leave_body,
        [scalars, own_part, dx_parts, dx_came],
        [shape((2, quarter, features), BF)],
        behind=[layer_output],
        cost=0.0,
    )[0]
    last_came = swap(last, "dp", 4)
    line = slice(4 * width, 4 * width + 1)
    gain_lines = pair_kept[:, line].astype(F32) + pair_came[:, line].astype(F32)
    gain_lines = gain_lines + swap(gain_lines, "mp", 1)
    gain_lines = gain_lines + swap(gain_lines, "mp", 2)
    gain_gradient = gain_lines[0] + swap(gain_lines[1], "dp", 4)
    gain_gradient = gain_gradient[0, :2 * width].reshape(2, width)
    p1 = swap(after(pieces, near_came, *late), "mp", 2)
    p2 = swap(pieces, "mp", 1)
    p3 = swap(after(p1, end1) if direct else p1, "mp", 1)
    hidden_new = call(
        bind(hidden_adam_body, [len(terms) for terms in hidden_terms]),
        [scalars]
        + sum(hidden_terms, [])
        + [jnp.transpose(x, (0, 2, 1)) for x in (hidden_weights, hidden_first, hidden_second)],
        [shape((3, hidden, width), F32)] * 4,
        cost=0.0,
    )
    token_gradient = call(
        bind(token_body, blocks),
        [scalars, pieces, p1, p2, p3, margin_column],
        [shape((rows, features), F32)],
        [
            pltpu.VMEM((rows, features), BF),
            pltpu.VMEM((rows, features), BF),
            pltpu.VMEM((rows, features), F32),
        ],
        cost=0.0,
    )[0]

    small_new = call(
        attention_adam_body,
        [scalars, pair_kept, pair_came, last_came]
        + [attention_weights, attention_first, attention_second]
        + [bias_tables, table_first, table_second],
        [shape(attention_weights.shape, F32)] * 4
        + [shape(bias_tables.shape, F32)] * 4,
        behind=[token_gradient],
        cost=0.0,
    )
    gain_new = adam_step(norm_gains, gain_first, gain_second, gain_gradient, VECTOR_RATE, 0.0)
    return (
        (layer_output, token_gradient)
        + tuple(small_new[:4])
        + tuple(jnp.transpose(x, (0, 2, 1)) for x in hidden_new)
        + (gain_gradient,)
        + gain_new
        + tuple(small_new[4:8])
    )


def solution(mesh):
    rows = P("dp", None)
    matrix = P(None, "dp", "mp")
    gain = P(None, "dp")
    return jax.shard_map(
        local,
        mesh=mesh,
        in_specs=(rows,) * 2 + (P(),) * 6 + (matrix,) * 6 + (gain,) * 3 + (matrix,) * 3,
        out_specs=(rows,) * 2 + (matrix,) * 8 + (gain,) * 4 + (matrix,) * 4,
        check_vma=False,
    )
```
